32 devices in a mesh: fsdp: 8 (over z, y), dp: 4 (over x, core).
Axes of the slice: x: 2, y: 2, z: 4, core: 2. Of those that a mesh axis runs over, the one named last changes fastest.
Arguments:
- tokens: bfloat16 [128, 64, 2048], P(('fsdp', 'dp')), may hold values from -6 to 6
- cotangent: bfloat16 [128, 64, 2048], P(('fsdp', 'dp')), may hold values from -6 to 6
- lengths: int32 [128], replicated, may hold values from 16 to 64, as said below
- dealing: int32 [128], replicated, may hold values from 0 to 127, as said below
- attn_gain: float32 [2048], P('fsdp'), may hold values from 0.25 to 1.75
- attn_shift: float32 [2048], P('fsdp'), may hold values from -3 to 3
- query_weight: float32 [2048, 2048], P('fsdp'), may hold values from -0.125 to 0.125
- query_bias: float32 [2048], P('fsdp'), may hold values from -3 to 3
- keyval_weight: float32 [2048, 256], P('fsdp'), may hold values from -0.125 to 0.125
- value_bias: float32 [128], P('fsdp'), may hold values from -3 to 3
- output_weight: float32 [2048, 2048], P('fsdp'), may hold values from -0.5 to 0.5
- output_bias: float32 [2048], P('fsdp'), may hold values from -3 to 3
- mlp_gain: float32 [2048], P('fsdp'), may hold values from 0.25 to 1.75
- mlp_shift: float32 [2048], P('fsdp'), may hold values from -3 to 3
- up_weight: float32 [2048, 8192], P('fsdp'), may hold values from -0.125 to 0.125
- up_bias: float32 [8192], P('fsdp'), may hold values from -3 to 3
- down_weight: float32 [8192, 2048], P('fsdp'), may hold values from -0.0625 to 0.0625
- down_bias: float32 [2048], P('fsdp'), may hold values from -3 to 3
Outputs:
- block_out: bfloat16 [128, 64, 2048], P(('fsdp', 'dp'))
- input_grad: bfloat16 [128, 64, 2048], P(('fsdp', 'dp'))
- attn_gain_grad: float32 [2048], P('fsdp')
- attn_shift_grad: float32 [2048], P('fsdp')
- query_weight_grad: float32 [2048, 2048], P('fsdp')
- query_bias_grad: float32 [2048], P('fsdp')
- keyval_weight_grad: float32 [2048, 256], P('fsdp')
- value_bias_grad: float32 [128], P('fsdp')
- output_weight_grad: float32 [2048, 2048], P('fsdp')
- output_bias_grad: float32 [2048], P('fsdp')
- mlp_gain_grad: float32 [2048], P('fsdp')
- mlp_shift_grad: float32 [2048], P('fsdp')
- up_weight_grad: float32 [2048, 8192], P('fsdp')
- up_bias_grad: float32 [8192], P('fsdp')
- down_weight_grad: float32 [8192, 2048], P('fsdp')
- down_bias_grad: float32 [2048], P('fsdp')
The draws below stay inside these ranges and needn't reach their ends.
Inputs may be any that keep to these rules, and one draw needn't show every extreme that they name: lengths[j] belongs to the sequence at dealt position j; the slots of a sequence past its length are padding. The 2 lengths of one micro-batch of one device (dealt positions g * 16 + r * 4 + m * 2 + k for k below 2) sum to at most 80; some micro-batch sums to exactly 80 and holds a sequence of 64 tokens. dealing is a permutation. Dealt position g * 16 + r * 4 + m * 2 + k is sequence k of micro-batch m of the device with fsdp index g and dp index r; sequence g * 16 + q * 4 + l is the l-th sequence held in the arrays by the device with fsdp index g and dp index q. Every sequence is dealt within its own fsdp index, and no device is dealt more than one sequence held by any one device.
All inputs are finite; a program needn't handle non-finite values.
Results may differ from the reference program's by a relative error of at most 0.018.
Values may be sent and summed in bfloat16 or wider, within the bound.
A program may use at most 448 MiB of HBM per device.

```python
import math
import jax
import jax.numpy as jnp
from jax import lax

D = 2048
HEADS = 16
HEAD = 128
FF = 8192
SEATS = 2
SLOT = 64
PACK = 80
HELD = 4
GROUP = 16
NSEQ = 128


def draw_lengths(key, part):
    key = jax.random.fold_in(key, 11)
    batch_count = NSEQ // SEATS
    shortest = SLOT // 4
    leftover = jnp.full((batch_count,), PACK, jnp.int32)
    columns = []
    for seat_index in range(SEATS):
        key_draw = jax.random.fold_in(key, 2 * seat_index)
        key_coin = jax.random.fold_in(key, 2 * seat_index + 1)
        ceiling = jnp.minimum(SLOT, leftover - (SEATS - 1 - seat_index) * shortest)
        drawn_len = jax.random.randint(key_draw, (batch_count,), shortest, ceiling + 1)
        if seat_index == SEATS - 1:
            coin_flip = jax.random.randint(key_coin, (batch_count,), 0, 2)
            drawn_len = jnp.where(coin_flip == 0, ceiling, drawn_len)
        columns.append(drawn_len)
        leftover = leftover - drawn_len
    length_table = jnp.stack(columns, axis=1)
    chosen = jax.random.randint(jax.random.fold_in(key, 997), (), 0, batch_count)
    forced = jnp.full((SEATS,), shortest, jnp.int32).at[0].set(SLOT)
    length_table = length_table.at[chosen].set(forced)
    return length_table.reshape(NSEQ).astype(jnp.int32)


def deal_group(group_key):
    sender_count = GROUP // HELD
    key_label, key_turn, key_offset, key_local = jax.random.split(group_key, 4)
    relabel = jax.random.permutation(key_label, sender_count)
    turned = jax.random.permutation(key_turn, sender_count)
    offsets = jax.random.permutation(key_offset, sender_count)[:HELD]
    senders = relabel[(turned[:, None] + offsets[None, :]) % sender_count]
    local_order = jax.vmap(lambda sub_key: jax.random.permutation(sub_key, HELD))(jax.random.split(key_local, sender_count))
    held_slot = local_order[senders, jnp.arange(HELD)[None, :]]
    return (senders * HELD + held_slot).reshape(GROUP)


def draw_dealing(key, part):
    key = jax.random.fold_in(key, 23)
    group_count = NSEQ // GROUP
    dealt_seq = jax.vmap(deal_group)(jax.random.split(key, group_count))
    dealt_seq = dealt_seq + (jnp.arange(group_count) * GROUP)[:, None]
    return dealt_seq.reshape(NSEQ).astype(jnp.int32)


def raised(entries, rng, source, target, parts, factor):
    def block_of(dim):
        return (jnp.arange(entries.shape[dim]) // (entries.shape[dim] // parts)).reshape((-1,) + (1,) * (entries.ndim - 1 - dim))

    first = jax.random.permutation(rng, parts)[block_of(target)]
    far = (block_of(target) + parts // 2) % parts
    return jnp.where((block_of(source) == first) | (block_of(source) == far), factor * entries, entries)


def shard_levels(own_key, extent, pieces, least, largest):
    def one(position, shards_of):
        draws = jax.random.uniform(jax.random.fold_in(jax.random.fold_in(own_key, 6), position), (shards_of,), jnp.float32, least / len(pieces), largest / len(pieces))
        return jnp.repeat(jnp.exp(draws), extent[position] // shards_of).reshape((-1,) + (1,) * (len(extent) - position - 1))

    level = one(*pieces[0])
    for cut in pieces[1:]:
        level = level * one(*cut)
    return level


def noise(own_key, shape, deviation, limit, pieces=(), held_as=jnp.bfloat16):
    values = jax.random.normal(own_key, shape, jnp.float32) * deviation
    if len(pieces) > 0:
        values = shard_levels(own_key, shape, pieces, -0.22, 0.18) * values
    return jnp.clip(values, min=-limit, max=limit).astype(held_as)


def heavy_noise(stream_key, shape, scale, limit, cuts, heavy, held_as=jnp.bfloat16):
    array = scale * jax.random.normal(stream_key, shape, jnp.float32)
    if cuts:
        array = array * shard_levels(stream_key, shape, cuts, -0.22, 0.18)
    return jnp.clip(raised(array, jax.random.fold_in(stream_key, 3), *heavy), -limit, limit).astype(held_as)


def setup_inputs(seed: int = 0) -> dict:
    seeds = jax.random.split(jax.random.key(seed), 19)
    tokens = heavy_noise(seeds[0], (NSEQ, SLOT, D), 1.0, 6.0, ((0, 32),), (0, 2, 32, 2.75))
    cotangent = noise(seeds[1], (NSEQ, SLOT, D), 1.0, 6.0, ((0, 32),))
    lengths = draw_lengths(jax.random.fold_in(seeds[18], 71), 0)
    dealing = draw_dealing(jax.random.fold_in(seeds[18], 71), 0)
    attn_gain = jnp.clip(1.0 + 0.15 * jax.random.normal(seeds[4], (D,), jnp.float32), 0.25, 1.75)
    attn_shift = noise(seeds[5], (D,), 0.5, 3.0, ((0, 8),), jnp.float32)
    query_weight = noise(seeds[6], (D, D), D ** -0.5, 0.125, ((0, 8),), jnp.float32)
    query_bias = noise(seeds[7], (D,), 0.5, 3.0, ((0, 8),), jnp.float32)
    keyval_weight = noise(seeds[8], (D, 2 * HEAD), D ** -0.5, 0.125, ((0, 8),), jnp.float32)
    value_bias = noise(seeds[9], (HEAD,), 0.5, 3.0, ((0, 8),), jnp.float32)
    output_weight = noise(seeds[10], (D, D), (4 * D // SLOT) ** -0.5, 0.5, ((0, 8),), jnp.float32)
    output_bias = noise(seeds[11], (D,), 0.5, 3.0, ((0, 8),), jnp.float32)
    mlp_gain = jnp.clip(1.0 + 0.15 * jax.random.normal(seeds[12], (D,), jnp.float32), 0.25, 1.75)
    mlp_shift = noise(seeds[13], (D,), 0.5, 3.0, ((0, 8),), jnp.float32)
    up_weight = noise(seeds[14], (D, FF), D ** -0.5, 0.125, ((0, 8),), jnp.float32)
    up_bias = noise(seeds[15], (FF,), 0.5, 3.0, ((0, 8),), jnp.float32)
    down_weight = noise(seeds[16], (FF, D), FF ** -0.5, 0.0625, ((0, 8),), jnp.float32)
    down_bias = noise(seeds[17], (D,), 0.5, 3.0, ((0, 8),), jnp.float32)
    return dict(tokens=tokens, cotangent=cotangent, lengths=lengths, dealing=dealing, attn_gain=attn_gain, attn_shift=attn_shift, query_weight=query_weight, query_bias=query_bias, keyval_weight=keyval_weight, value_bias=value_bias, output_weight=output_weight, output_bias=output_bias, mlp_gain=mlp_gain, mlp_shift=mlp_shift, up_weight=up_weight, up_bias=up_bias, down_weight=down_weight, down_bias=down_bias)


epsilon = 1e-05
gelu_scale = 0.7978845608028654
gelu_cubic = 0.044715
highest = lax.Precision.HIGHEST

@jax.custom_vjp
def low(v):
    return lax.optimization_barrier(v.astype(jnp.bfloat16)).astype(jnp.float32)

@jax.custom_vjp
def low_back(v):
    return v

def low_keep(v):
    return (low(v), None)

def low_pass(kept, grad):
    return (grad,)

def back_keep(v):
    return (v, None)

def back_low(kept, grad):
    return (low(grad),)
low.defvjp(low_keep, low_pass)
low_back.defvjp(back_keep, back_low)

def layer_norm(row_data, gain_vec, shift_vec):
    center = row_data - lax.optimization_barrier(jnp.mean(row_data, axis=-1, keepdims=True))
    spread = lax.optimization_barrier(jnp.mean(center * center, axis=-1, keepdims=True))
    return center * lax.rsqrt(spread + epsilon) * gain_vec + shift_vec

def gelu_tanh(values):
    return 0.5 * values * (1.0 + jnp.tanh(gelu_scale * (values + gelu_cubic * values * values * values)))

def layer_block(params, row_data, valid_mask):
    groups = row_data.shape[0]
    length = row_data.shape[1]
    normed = low(layer_norm(row_data, params[0], params[1]))
    query_rows = low(low_back(jnp.einsum('gsd,de->gse', normed, params[2], precision=highest) + params[3]))
    value_shift = jnp.concatenate([jnp.zeros_like(params[5]), params[5]])
    keyval = low(low_back(jnp.einsum('gsd,de->gse', normed, params[4], precision=highest) + value_shift))
    query_heads = query_rows.reshape(groups, length, HEADS, HEAD)
    key_rows = keyval[..., :HEAD]
    value_rows = keyval[..., HEAD:]
    score_scale = 1.0 / math.sqrt(HEAD)
    scores = low_back(jnp.einsum('gshd,gtd->ghst', query_heads, key_rows, precision=highest) * score_scale)
    positions = jnp.arange(length)
    causal = positions[None, :] <= positions[:, None]
    allowed = causal[None, None] & valid_mask[:, None, None, :]
    scores = jnp.where(allowed, scores, -1e+30)
    row_max = lax.optimization_barrier(jnp.max(scores, axis=-1, keepdims=True))
    expscores = jnp.exp(scores - row_max)
    probabilities = expscores / lax.optimization_barrier(jnp.sum(expscores, axis=-1, keepdims=True))
    attended = jnp.einsum('ghst,gtd->gshd', low(probabilities), value_rows, precision=highest)
    attended = low(low_back(attended.reshape(groups, length, D)))
    branch = low_back(jnp.einsum('gsd,de->gse', attended, params[6], precision=highest) + params[7])
    middle = row_data + branch
    normed_mlp = low(layer_norm(middle, params[8], params[9]))
    hidden = low_back(jnp.einsum('gsd,df->gsf', normed_mlp, params[10], precision=highest) + params[11])
    activated = low(gelu_tanh(hidden))
    mlp_out = low_back(jnp.einsum('gsf,fd->gsd', activated, params[12], precision=highest) + params[13])
    return jnp.where(valid_mask[..., None], middle + mlp_out, 0.0)

def reference(tokens, cotangent, lengths, dealing, attn_gain, attn_shift, query_weight, query_bias, keyval_weight, value_bias, output_weight, output_bias, mlp_gain, mlp_shift, up_weight, up_bias, down_weight, down_bias):
    true_lengths = jnp.zeros((NSEQ,), jnp.int32).at[dealing].set(lengths)
    valid_mask = jnp.arange(SLOT)[None, :] < true_lengths[:, None]
    masters = (attn_gain, attn_shift, query_weight, query_bias, keyval_weight, value_bias, output_weight, output_bias, mlp_gain, mlp_shift, up_weight, up_bias, down_weight, down_bias)
    group_count = NSEQ // GROUP

    def whole_layer(row_data, params):
        lowered = tuple((low(item) for item in params))

        def one_group(inputs):
            return layer_block(lowered, inputs[0], inputs[1])
        result = lax.map(jax.checkpoint(one_group), (row_data.reshape(group_count, GROUP, SLOT, D), valid_mask.reshape(group_count, GROUP, SLOT)))
        return result.reshape(NSEQ, SLOT, D)
    block_out, pullback = jax.vjp(whole_layer, tokens.astype(jnp.float32), tuple((item.astype(jnp.float32) for item in masters)))
    input_grad, gradients = pullback(cotangent.astype(jnp.float32))
    return (block_out.astype(jnp.bfloat16), input_grad.astype(jnp.bfloat16), gradients[0], gradients[1], gradients[2], gradients[3], gradients[4], gradients[5], gradients[6], gradients[7], gradients[8], gradients[9], gradients[10], gradients[11], gradients[12], gradients[13])
```

```python
import math

import jax
import jax.numpy as jnp
from jax import lax
from jax.experimental import pallas as pl
from jax.experimental.pallas import tpu as pltpu
from jax.sharding import Mesh
from jax.sharding import PartitionSpec as P

HEADS = 16
HEAD = 128
MB = 2
SEATS = 2
PACK = 80

epsilon = 1e-05
gelu_scale = 0.7978845608028654
gelu_cubic = 0.044715

DP = ("x", "c")


def low(values):
    return values.astype(jnp.bfloat16)


def wide(values):
    return values.astype(jnp.float32)


def product(left_mat, right_mat):
    return jnp.dot(left_mat, right_mat, preferred_element_type=jnp.float32)


def product_rows(left_mat, right_mat):
    return lax.dot_general(
        left_mat, right_mat, (((0,), (0,)), ((), ())), preferred_element_type=jnp.float32
    )


def product_cols(left_mat, right_mat):
    return lax.dot_general(
        left_mat, right_mat, (((1,), (1,)), ((), ())), preferred_element_type=jnp.float32
    )


def normalize(rows):
    center = rows - jnp.mean(rows, axis=-1, keepdims=True)
    spread = jnp.mean(center * center, axis=-1, keepdims=True)
    scale = lax.rsqrt(spread + epsilon)
    return center * scale, scale


def norm_back(grad_normed, gain, xhat, scale):
    g = grad_normed * gain
    inner = jnp.mean(g * xhat, axis=-1, keepdims=True)
    return scale * (g - jnp.mean(g, axis=-1, keepdims=True) - xhat * inner)


def gelu_parts(values):
    inner = jnp.tanh(gelu_scale * (values + gelu_cubic * values * values * values))
    activated = 0.5 * values * (1.0 + inner)
    slope = 0.5 * (1.0 + inner) + 0.5 * values * (1.0 - inner * inner) * gelu_scale * (
        1.0 + 3.0 * gelu_cubic * values * values
    )
    return activated, slope


MESH_ID = pl.DeviceIdType.MESH
VMEM_LIMIT = 56 * 1024 * 1024


class Spot:
    def __init__(self, depth):
        self.depth = depth
        self.z = lax.axis_index("z")
        self.y = lax.axis_index("y")
        self.x = lax.axis_index("x")
        self.c = lax.axis_index("c")
        self.to_c = {"c": 1 - self.c}
        self.to_x = {"x": 1 - self.x}
        self.to_y = {"y": 1 - self.y}
        self.to_xc = {"x": 1 - self.x, "c": 1 - self.c}
        self.up = {"z": self.z + 1}
        self.down = {"z": self.z - 1}

    def barrier(self, plane, line):
        bar = pltpu.get_barrier_semaphore()
        for to in plane:
            pl.semaphore_signal(bar, inc=1, device_id=to, device_id_type=MESH_ID)
        if line:

            @pl.when(self.z > 0)
            def _():
                pl.semaphore_signal(bar, inc=1, device_id=self.down, device_id_type=MESH_ID)

            @pl.when(self.z < self.depth - 1)
            def _():
                pl.semaphore_signal(bar, inc=1, device_id=self.up, device_id_type=MESH_ID)

        count = len(plane)
        if line:
            lower = jnp.where(self.z > 0, 1, 0)
            upper = jnp.where(self.z < self.depth - 1, 1, 0)
            count = count + lower + upper
        pl.semaphore_wait(bar, count)


class Net:
    def __init__(self, send_sems, recv_sems, local_sems):
        self.send_sems = send_sems
        self.recv_sems = recv_sems
        self.local_sems = local_sems
        self.count = 0
        self.local_count = 0
        self.open = []

    def remote(self, src, dst, to, arrives=None):
        copy = Copy(self, self.count, src, dst, to, arrives)
        self.count += 1
        return copy

    def local(self, src, dst):
        copy = pltpu.make_async_copy(src, dst, self.local_sems.at[self.local_count])
        self.local_count += 1
        return copy


class Copy:
    def __init__(self, net, index, src, dst, to, arrives):
        def make(target):
            return pltpu.make_async_remote_copy(
                src_ref=src,
                dst_ref=target,
                send_sem=net.send_sems.at[index],
                recv_sem=net.recv_sems.at[index],
                device_id=to,
                device_id_type=MESH_ID,
            )

        self.out = make(dst)
        self.into = make(dst if arrives is None else arrives)

    def start(self):
        self.out.start()

    def got(self):
        self.into.wait_recv()

    def sent(self):
        self.out.wait_send()


class PlaneGather:
    def __init__(self, net, spot, own, slots):
        def at(y, x, c):
            return y * 4 + x * 2 + c

        y, x, c = spot.y, spot.x, spot.c
        half = own.shape[0] // 2
        lo, hi = pl.ds(0, half), pl.ds(half, half)
        me = at(y, x, c)
        on_x, on_y, on_d = at(y, 1 - x, c), at(1 - y, x, c), at(1 - y, 1 - x, c)
        peer = [at(y, x, 1 - c), at(y, 1 - x, 1 - c), at(1 - y, x, 1 - c), at(1 - y, 1 - x, 1 - c)]

        def slot(index):
            return slots.at[index]

        self.keep = net.local(own, slot(me))
        self.x = net.remote(own, slot(me), spot.to_x, slot(on_x))
        self.y = net.remote(own, slot(me), spot.to_y, slot(on_y))
        self.c = net.remote(own, slot(me), spot.to_c, slot(peer[0]))
        self.x_on_y = net.remote(
            slots.at[on_x, lo], slots.at[on_x, lo], spot.to_y, slots.at[on_d, lo]
        )
        self.y_on_x = net.remote(
            slots.at[on_y, hi], slots.at[on_y, hi], spot.to_x, slots.at[on_d, hi]
        )
        self.x_on_c = net.remote(slot(on_x), slot(on_x), spot.to_c, slot(peer[1]))
        self.y_on_c = net.remote(slot(on_y), slot(on_y), spot.to_c, slot(peer[2]))
        self.lo_on_c = net.remote(
            slots.at[on_d, lo], slots.at[on_d, lo], spot.to_c, slots.at[peer[3], lo]
        )
        self.hi_on_c = net.remote(
            slots.at[on_d, hi], slots.at[on_d, hi], spot.to_c, slots.at[peer[3], hi]
        )

    def start(self):
        self.x.start()
        self.y.start()
        self.c.start()
        self.keep.start()

    def middle(self):
        self.x.got()
        self.x_on_y.start()
        self.x_on_c.start()
        self.y.got()
        self.y_on_x.start()
        self.y_on_c.start()

    def last(self):
        self.x_on_y.got()
        self.lo_on_c.start()
        self.y_on_x.got()
        self.hi_on_c.start()

    def finish(self):
        for copy in (self.c, self.x_on_c, self.y_on_c, self.lo_on_c, self.hi_on_c):
            copy.got()
        for copy in (
            self.x,
            self.y,
            self.c,
            self.x_on_y,
            self.y_on_x,
            self.x_on_c,
            self.y_on_c,
            self.lo_on_c,
            self.hi_on_c,
        ):
            copy.sent()
        self.keep.wait()

    remotes = 9
    locals = 1


def add_rows(into, other, step=32):
    rows = into.shape[0]

    @pl.loop(0, rows // step)
    def _(index):
        at = pl.ds(pl.multiple_of(index * step, step), step)
        into[at, :] = low(wide(into[at, :]) + wide(other[at, :]))


class PlaneScatter:
    remotes = 10

    @staticmethod
    def buffers(rows, width):
        return [
            pltpu.VMEM((4, rows, width), jnp.bfloat16),
            pltpu.VMEM((rows, width), jnp.bfloat16),
            pltpu.VMEM((rows, width), jnp.bfloat16),
            pltpu.VMEM((rows, width), jnp.bfloat16),
        ]

    def __init__(self, net, spot, parts, sums, diag, from_x, from_y):
        y, x, c = spot.y, spot.x, spot.c
        half = parts.shape[1] // 2
        lo, hi = pl.ds(0, half), pl.ds(half, half)
        self.own, self.nx, self.ny, self.nd = (
            y * 2 + x,
            y * 2 + 1 - x,
            (1 - y) * 2 + x,
            (1 - y) * 2 + 1 - x,
        )
        self.parts, self.sums, self.diag = parts, sums, diag
        self.from_x, self.from_y, self.c = from_x, from_y, c
        self.lo, self.hi = lo, hi
        self.first = {
            key: net.remote(parts.at[at * 2 + 1 - c], sums.at[at], spot.to_c)
            for key, at in (("d", self.nd), ("x", self.nx), ("y", self.ny), ("o", self.own))
        }
        self.d_lo = net.remote(sums.at[self.nd, lo], diag.at[lo], spot.to_x)
        self.d_hi = net.remote(sums.at[self.nd, hi], diag.at[hi], spot.to_y)
        self.x_lo = net.remote(sums.at[self.nx, lo], from_x.at[lo], spot.to_x)
        self.y_hi = net.remote(sums.at[self.ny, hi], from_y.at[hi], spot.to_y)
        self.x_hi = net.remote(sums.at[self.nx, hi], from_x.at[hi], spot.to_x)
        self.y_lo = net.remote(sums.at[self.ny, lo], from_y.at[lo], spot.to_y)

    def start(self):
        for copy in self.first.values():
            copy.start()

    def pair(self, key, at):
        self.first[key].got()
        add_rows(self.sums.at[at], self.parts.at[at * 2 + self.c])

    def middle(self):
        self.pair("d", self.nd)
        self.d_lo.start()
        self.d_hi.start()
        self.pair("x", self.nx)
        self.x_lo.start()
        self.pair("y", self.ny)
        self.y_hi.start()
        self.pair("o", self.own)

    def last(self):
        self.d_lo.got()
        add_rows(self.sums.at[self.ny, self.lo], self.diag.at[self.lo], 16)
        self.y_lo.start()
        self.d_hi.got()
        add_rows(self.sums.at[self.nx, self.hi], self.diag.at[self.hi], 16)
        self.x_hi.start()

    def finish(self, result):
        for copy in (self.x_lo, self.y_hi, self.x_hi, self.y_lo):
            copy.got()

        @pl.loop(0, result.shape[0] // 16)
        def _(index):
            at = pl.ds(pl.multiple_of(index * 16, 16), 16)
            result[at, :] = (
                wide(self.sums[self.own, at, :]) + wide(self.from_x[at, :]) + wide(self.from_y[at, :])
            )

        for copy in (
            *self.first.values(),
            self.d_lo,
            self.d_hi,
            self.x_lo,
            self.x_hi,
            self.y_lo,
            self.y_hi,
        ):
            copy.sent()


class LineGather:
    def __init__(self, net, spot, slots):
        self.spot, depth, z = spot, spot.depth, spot.z
        self.hops = []
        for step in range(depth - 1):
            lower = jnp.maximum(z - step, 0)
            upper = jnp.minimum(z + step, depth - 1)
            from_low = jnp.maximum(z - 1 - step, 0)
            from_high = jnp.minimum(z + 1 + step, depth - 1)
            self.hops.append(
                (
                    net.remote(slots(lower), slots(lower), spot.up, slots(from_low)),
                    net.remote(slots(upper), slots(upper), spot.down, slots(from_high)),
                )
            )

    @staticmethod
    def remotes(depth):
        return 2 * (depth - 1)

    def sends(self, step):
        z, last = self.spot.z, self.spot.depth - 1
        return (
            ((z >= step) & (z < last), self.hops[step][0]),
            ((z + step <= last) & (z > 0), self.hops[step][1]),
        )

    def takes(self, step):
        z, last = self.spot.z, self.spot.depth - 1
        return ((z >= step + 1, self.hops[step][0]), (z + step + 1 <= last, self.hops[step][1]))

    def start(self, step):
        for cond, copy in self.sends(step):
            pl.when(cond)(copy.start)

    def got(self, step):
        for cond, copy in self.takes(step):
            pl.when(cond)(copy.got)

    def hop(self, step):
        for (came, old), (goes, new) in zip(self.takes(step - 1), self.sends(step)):
            pl.when(came)(old.got)
            pl.when(goes)(new.start)

    def finish(self):
        for step in range(self.spot.depth - 1):
            for cond, copy in self.sends(step):
                pl.when(cond)(copy.sent)


class LineScatter:
    def __init__(self, net, spot, parts, from_low, from_high, add):
        self.spot, depth, z = spot, spot.depth, spot.z
        self.parts, self.from_low, self.from_high, self.add = parts, from_low, from_high, add
        self.ups, self.downs = [], []
        for step in range(depth - 1):
            self.ups.append(net.remote(parts(depth - 1 - step), from_low.at[step], spot.up))
            self.downs.append(net.remote(parts(step), from_high.at[step], spot.down))

    remotes = LineGather.remotes

    def stage(self, step):
        z, last = self.spot.z, self.spot.depth - 1
        up_to, down_to = last - step, step

        @pl.when((z > 0) & (z < up_to))
        def _():
            self.ups[step].got()
            self.add(self.parts(up_to), self.from_low.at[step])

        @pl.when(z < up_to)
        def _():
            self.ups[step].start()

        @pl.when((z < last) & (z > down_to))
        def _():
            self.downs[step].got()
            self.add(self.parts(down_to), self.from_high.at[step])

        @pl.when(z > down_to)
        def _():
            self.downs[step].start()

    def total(self):
        z, last = self.spot.z, self.spot.depth - 1
        for step in range(last):

            @pl.when((z > 0) & (z == last - step))
            def _():
                self.ups[step].got()
                self.add(self.parts(last - step), self.from_low.at[step])

            @pl.when((z < last) & (z == step))
            def _():
                self.downs[step].got()
                self.add(self.parts(step), self.from_high.at[step])

    def finish(self):
        z, last = self.spot.z, self.spot.depth - 1
        for step in range(last):
            pl.when(z < last - step)(self.ups[step].sent)
            pl.when(z > step)(self.downs[step].sent)


class DpGather:
    remotes = 3

    def __init__(self, net, spot, own, slots):
        me = spot.x * 2 + spot.c
        on_x = (1 - spot.x) * 2 + spot.c
        self.keep = net.local(own, slots.at[me])
        self.x = net.remote(own, slots.at[me], spot.to_x, slots.at[on_x])
        self.c = net.remote(own, slots.at[me], spot.to_c, slots.at[spot.x * 2 + 1 - spot.c])
        self.x_on_c = net.remote(
            slots.at[on_x],
            slots.at[on_x],
            spot.to_c,
            slots.at[(1 - spot.x) * 2 + 1 - spot.c],
        )

    def start(self):
        self.x.start()
        self.c.start()
        self.keep.start()

    def last(self):
        self.x.got()
        self.x_on_c.start()

    def finish(self):
        self.c.got()
        self.x_on_c.got()
        for copy in (self.x, self.c, self.x_on_c):
            copy.sent()
        self.keep.wait()


class DpExchange:
    remotes = 3

    def __init__(self, net, spot, parts, slots):
        me = spot.x * 2 + spot.c
        on_x = (1 - spot.x) * 2 + spot.c
        on_c = spot.x * 2 + 1 - spot.c
        on_xc = (1 - spot.x) * 2 + 1 - spot.c
        self.keep = net.local(parts.at[me], slots.at[me])
        self.moves = [
            net.remote(parts.at[at], slots.at[me], to, slots.at[at])
            for at, to in ((on_xc, spot.to_xc), (on_x, spot.to_x), (on_c, spot.to_c))
        ]

    def start(self):
        for copy in self.moves:
            copy.start()
        self.keep.start()

    def got(self):
        for copy in self.moves:
            copy.got()
        self.keep.wait()

    def finish(self):
        for copy in self.moves:
            copy.sent()


def net_scratch(remotes, locals_):
    return [
        pltpu.SemaphoreType.DMA((remotes,)),
        pltpu.SemaphoreType.DMA((remotes,)),
        pltpu.SemaphoreType.DMA((max(locals_, 1),)),
    ]


ANY = pl.BlockSpec(memory_space=pl.ANY)
IN_VMEM = pl.BlockSpec(memory_space=pltpu.VMEM)


def comm_params(collective_id):
    return pltpu.CompilerParams(
        collective_id=collective_id, has_side_effects=True, vmem_limit_bytes=VMEM_LIMIT
    )


def plane_gather(block, depth, collective_id):
    rows, width = block.shape

    def kernel(own, slots, *sems):
        spot = Spot(depth)
        net = Net(*sems)
        gather = PlaneGather(net, spot, own, slots)
        spot.barrier((spot.to_c, spot.to_x, spot.to_y), False)
        gather.start()
        gather.middle()
        gather.last()
        gather.finish()

    out = pl.pallas_call(
        kernel,
        out_shape=jax.ShapeDtypeStruct((8, rows, width), block.dtype),
        in_specs=[ANY],
        out_specs=ANY,
        scratch_shapes=net_scratch(PlaneGather.remotes, 1),
        compiler_params=comm_params(collective_id),
    )(block)
    return out.reshape(8 * rows, width)


def plane_scatter(parts, depth, collective_id):
    count = len(parts)
    rows, width = parts[0].shape[0] // 8, parts[0].shape[1]

    def kernel(*refs):
        sources, results = refs[:count], refs[count : 2 * count]
        scratch = refs[2 * count : -3]
        spot = Spot(depth)
        net = Net(*refs[-3:])
        runs = [
            PlaneScatter(net, spot, source, *scratch[4 * index : 4 * index + 4])
            for index, source in enumerate(sources)
        ]
        spot.barrier((spot.to_c, spot.to_x, spot.to_y), False)
        for run in runs:
            run.start()
        for run in runs:
            run.middle()
        for run in runs:
            run.last()
        for run, result in zip(runs, results):
            run.finish(result)

    return pl.pallas_call(
        kernel,
        out_shape=[jax.ShapeDtypeStruct((rows, width), jnp.float32)] * count,
        in_specs=[IN_VMEM] * count,
        out_specs=[IN_VMEM] * count,
        scratch_shapes=PlaneScatter.buffers(rows, width) * count
        + net_scratch(PlaneScatter.remotes * count, 1),
        compiler_params=comm_params(collective_id),
    )(*[item.reshape(8, rows, width) for item in parts])


def first_gather(
    depth, tokens, cotangent, attn_mine, attn_other, small, out_slice, up_mine, up_other, down_slice
):
    flat, width = tokens.shape
    low_type = jnp.bfloat16

    def shape(*dims):
        return jax.ShapeDtypeStruct(dims, low_type)

    def kernel(
        tok, cot, attn_m, attn_o, small_m, out_m, up_m, up_o, down_m,
        tok_all, cot_all, attn_all, small_all, out_all, out_dealt, up_all, down_all,
        *sems,
    ):
        spot = Spot(depth)
        net = Net(*sems)
        z, y = spot.z, spot.y
        tok_run = PlaneGather(net, spot, tok, tok_all)
        cot_run = PlaneGather(net, spot, cot, cot_all)
        group = depth // 4
        keep_out = net.local(out_m, out_all.at[z // group, z % group])
        keep_attn = net.local(attn_m, attn_all.at[z, y])
        keep_small = net.local(small_m, small_all.at[z, y])
        keep_up = net.local(up_m, up_all.at[z, y])
        keep_down = net.local(down_m, down_all.at[z])
        y_attn = net.remote(attn_o, attn_all.at[z, y], spot.to_y, attn_all.at[z, 1 - y])
        y_small = net.remote(small_m, small_all.at[z, y], spot.to_y, small_all.at[z, 1 - y])
        y_up = net.remote(up_o, up_all.at[z, y], spot.to_y, up_all.at[z, 1 - y])
        run_out = LineGather(net, spot, lambda at: out_all.at[at // group, at % group])
        run_attn = LineGather(net, spot, lambda at: attn_all.at[at])
        run_small = LineGather(net, spot, lambda at: small_all.at[at])
        run_up = LineGather(net, spot, lambda at: up_all.at[at])
        run_down = LineGather(net, spot, lambda at: down_all.at[at])
        deal = DpExchange(net, spot, out_all, out_dealt)
        spot.barrier((spot.to_c, spot.to_x, spot.to_y, spot.to_xc), True)
        keep_out.start()
        y_attn.start()
        y_small.start()
        keep_attn.start()
        keep_small.start()
        y_up.start()
        keep_down.start()
        keep_up.start()
        tok_run.start()
        keep_out.wait()
        run_out.start(0)
        keep_attn.wait()
        y_attn.got()
        run_attn.start(0)
        keep_small.wait()
        y_small.got()
        run_small.start(0)
        keep_down.wait()
        run_down.start(0)
        keep_up.wait()
        y_up.got()
        run_up.start(0)
        tok_run.middle()
        for step in range(1, depth - 1):
            run_out.hop(step)
            run_attn.hop(step)
            run_small.hop(step)
        tok_run.last()
        cot_run.start()
        for run in (run_out, run_attn, run_small):
            run.got(depth - 2)
        deal.start()
        cot_run.middle()
        cot_run.last()
        for step in range(1, depth - 1):
            run_down.hop(step)
            run_up.hop(step)
        deal.got()
        run_down.got(depth - 2)
        run_up.got(depth - 2)
        for run in (run_out, run_attn, run_small, run_up, run_down, tok_run, cot_run, deal):
            run.finish()
        for copy in (y_attn, y_small, y_up):
            copy.sent()

    remotes = 2 * PlaneGather.remotes + 3 + 5 * LineGather.remotes(depth) + DpExchange.remotes
    return pl.pallas_call(
        kernel,
        out_shape=[
            shape(8, flat, width),
            shape(8, flat, width),
            shape(depth, 2, *attn_mine.shape),
            shape(depth, 2, *small.shape),
            shape(4, depth // 4, *out_slice.shape),
            shape(4, depth // 4, *out_slice.shape),
            shape(depth, 2, *up_mine.shape),
            shape(depth, *down_slice.shape),
        ],
        in_specs=[ANY] * 9,
        out_specs=[ANY] * 8,
        scratch_shapes=net_scratch(remotes, 8),
        compiler_params=comm_params(1),
    )(tokens, cotangent, attn_mine, attn_other, small, out_slice, up_mine, up_other, down_slice)


def last_scatter(depth, d_up, d_down, d_attn, d_vec, d_out, grad_parts):
    rows, width = grad_parts.shape[1:]
    low_type = jnp.bfloat16

    def shape(*dims):
        return jax.ShapeDtypeStruct(dims, low_type)

    def add2(into, other):
        add_rows(into, other, 16)

    def add3(into, other):
        for at in range(2):
            add_rows(into.at[at], other.at[at], 16)

    def kernel(
        up, down, attn, vec, out, parts,
        up_all, down_all, attn_all, vec_all, out_all, own_sum,
        up_lo, up_hi, down_lo, down_hi, attn_lo, attn_hi, vec_lo, vec_hi, out_lo, out_hi,
        out_mix, up_got, attn_got, vec_got, sums, diag, from_x, from_y, *sems,
    ):
        spot = Spot(depth)
        net = Net(*sems)
        z, y = spot.z, spot.y
        deal = DpExchange(net, spot, out, out_mix)
        group = depth // 4

        def mixed(at):
            return out_mix.at[at // group, at % group]

        run_up = LineScatter(net, spot, lambda at: up.at[at], up_lo, up_hi, add3)
        run_down = LineScatter(net, spot, lambda at: down.at[at], down_lo, down_hi, add2)
        run_attn = LineScatter(net, spot, lambda at: attn.at[at], attn_lo, attn_hi, add3)
        run_vec = LineScatter(net, spot, lambda at: vec.at[at], vec_lo, vec_hi, add3)
        run_out = LineScatter(net, spot, mixed, out_lo, out_hi, add2)
        plane = PlaneScatter(net, spot, parts, sums, diag, from_x, from_y)
        y_up = net.remote(up.at[z, 1 - y], up_got, spot.to_y)
        y_attn = net.remote(attn.at[z, 1 - y], attn_got, spot.to_y)
        y_vec = net.remote(vec.at[z, 1 - y], vec_got, spot.to_y)
        dp_up = DpGather(net, spot, up.at[z, y], up_all.at[0])
        dp_up2 = DpGather(net, spot, up_got, up_all.at[1])
        dp_down = DpGather(net, spot, down.at[z], down_all)
        dp_attn = DpGather(net, spot, attn.at[z, y], attn_all.at[0])
        dp_attn2 = DpGather(net, spot, attn_got, attn_all.at[1])
        dp_vec = DpGather(net, spot, vec.at[z, y], vec_all)
        dp_out = DpGather(net, spot, mixed(z), out_all)
        spot.barrier((spot.to_c, spot.to_x, spot.to_y, spot.to_xc), True)
        deal.start()
        run_down.stage(0)
        run_up.stage(0)
        plane.start()
        plane.middle()
        for step in range(1, depth - 1):
            run_down.stage(step)
        plane.last()
        for step in range(1, depth - 1):
            run_up.stage(step)
        run_down.total()
        deal.got()
        run_attn.stage(0)
        run_vec.stage(0)
        run_out.stage(0)
        dp_down.start()
        plane.finish(own_sum)
        run_up.total()
        y_up.start()
        dp_up.start()
        for step in range(1, depth - 1):
            run_attn.stage(step)
            run_vec.stage(step)
            run_out.stage(step)
        dp_down.last()
        y_up.got()
        dp_up2.start()
        dp_up.last()
        run_attn.total()
        run_vec.total()
        y_attn.start()
        y_vec.start()
        dp_attn.start()
        run_out.total()
        dp_out.start()
        dp_up2.last()
        y_vec.got()
        y_vec.sent()
        add_rows(vec.at[z, y], vec_got, 16)
        dp_vec.start()
        y_attn.got()
        dp_attn2.start()
        dps = (dp_attn, dp_out, dp_vec, dp_attn2)
        for run in dps:
            run.last()
        for run in (dp_down, dp_up, dp_up2, *dps):
            run.finish()
        for run in (run_up, run_down, run_attn, run_vec, run_out, deal):
            run.finish()
        y_up.sent()
        y_attn.sent()

    remotes = (
        DpExchange.remotes
        + 5 * LineGather.remotes(depth)
        + PlaneScatter.remotes
        + 3
        + 7 * DpGather.remotes
    )
    one = depth - 1

    def twice(*dims):
        return [pltpu.VMEM(dims, low_type)] * 2

    return pl.pallas_call(
        kernel,
        out_shape=[
            shape(2, 4, *d_up.shape[2:]),
            shape(4, *d_down.shape[1:]),
            shape(2, 4, *d_attn.shape[2:]),
            shape(4, *d_vec.shape[2:]),
            shape(4, *d_out.shape[2:]),
            jax.ShapeDtypeStruct((rows, width), jnp.float32),
        ],
        in_specs=[IN_VMEM] * 6,
        out_specs=[ANY] * 5 + [IN_VMEM],
        scratch_shapes=[
            *twice(one, *d_up.shape[1:]),
            *twice(one, *d_down.shape[1:]),
            *twice(one, *d_attn.shape[1:]),
            *twice(one, *d_vec.shape[1:]),
            *twice(one, *d_out.shape[2:]),
            pltpu.VMEM(d_out.shape, low_type),
            pltpu.VMEM(d_up.shape[2:], low_type),
            pltpu.VMEM(d_attn.shape[2:], low_type),
            pltpu.VMEM(d_vec.shape[2:], low_type),
            *PlaneScatter.buffers(rows, width),
            *net_scratch(remotes, 8),
        ],
        compiler_params=comm_params(2),
    )(d_up, d_down, d_attn, d_vec, d_out, grad_parts)


def build(mesh):
    fsdp_size = mesh.shape["fsdp"]
    depth = fsdp_size // 2
    y_slow = depth != 4
    owner_axes = ("y", "z") if y_slow else ("z", "y")

    def owner(z_at, y_at):
        return y_at * depth + z_at if y_slow else z_at * 2 + y_at

    def shards(
        tokens,
        cotangent,
        lengths,
        dealing,
        attn_gain,
        attn_shift,
        query_weight,
        query_bias,
        keyval_weight,
        value_bias,
        output_weight,
        output_bias,
        mlp_gain,
        mlp_shift,
        up_weight,
        up_bias,
        down_weight,
        down_bias,
    ):
        held, slot_len, width = tokens.shape
        my_z = lax.axis_index("z")
        my_y = lax.axis_index("y")
        my_xc = lax.axis_index("x") * 2 + lax.axis_index("c")
        member = my_y * 4 + my_xc
        rows_own = query_weight.shape[0]
        ff = up_weight.shape[1]
        ff_own = down_weight.shape[0]
        ff_seg = ff_own // 4
        out_seg = rows_own // 4
        head_cols = width // 8
        group_seqs = held * 4

        def group_table(table):
            parts = [
                lax.dynamic_slice_in_dim(table, owner(my_z, y_at) * group_seqs, group_seqs)
                for y_at in range(2)
            ]
            return jnp.stack(parts)

        bases = jnp.stack([owner(my_z, y_at) * group_seqs for y_at in range(2)])
        in_group = group_table(dealing) - bases[:, None]
        source = in_group + (jnp.arange(2) * group_seqs)[:, None]
        micro = 2 * 4 * MB
        lens = group_table(lengths).reshape(micro, SEATS)
        source = source.reshape(micro, SEATS)
        ends = jnp.concatenate([lens[:, :1], lens[:, :1] + lens[:, 1:]], axis=1)
        starts = ends - lens
        at = jnp.arange(PACK)
        inside = (at[None, :, None] >= starts[:, None, :]) & (at[None, :, None] < ends[:, None, :])
        row_valid = jnp.any(inside, axis=2)
        seat = jnp.sum(jnp.where(inside, jnp.arange(SEATS)[None, None, :], 0), axis=2)
        segment = jnp.where(row_valid, seat, -1)
        offset = at[None, :] - jnp.sum(jnp.where(inside, starts[:, None, :], 0), axis=2)
        source_row = jnp.sum(jnp.where(inside, source[:, None, :], 0), axis=2) * slot_len + offset
        source_row = jnp.where(row_valid, source_row, 0).reshape(micro * PACK)
        valid = row_valid.reshape(micro * PACK)
        allowed = (
            (at[None, :, None] >= at[None, None, :])
            & (segment[:, :, None] == segment[:, None, :])
            & row_valid[:, None, :]
        )

        def up_columns(y_at):
            cols = [
                lax.dynamic_slice_in_dim(
                    up_weight, owner(z_at, y_at) * ff_own + my_xc * ff_seg, ff_seg, axis=1
                )
                for z_at in range(depth)
            ]
            return low(jnp.concatenate(cols, axis=1))

        def head_base(y_at):
            return owner(my_xc * (depth // 4), y_at) * rows_own

        def query_columns(y_at):
            return low(lax.dynamic_slice_in_dim(query_weight, head_base(y_at), head_cols, axis=1))

        small_parts = [
            attn_gain,
            attn_shift,
            output_bias,
            mlp_gain,
            mlp_shift,
            down_bias,
            query_bias,
            up_bias,
            value_bias,
        ]
        small = low(jnp.concatenate(small_parts))
        small_count = small.shape[0]
        small = jnp.pad(small, (0, 16 * 256 - small_count)).reshape(16, 256)
        attn_mine = jnp.concatenate([query_columns(my_y), low(keyval_weight)], axis=1)
        attn_other = jnp.concatenate([query_columns(1 - my_y), low(keyval_weight)], axis=1)
        out_slice = low(lax.dynamic_slice_in_dim(output_weight, my_xc * out_seg, out_seg, axis=0))
        down_slice = low(lax.dynamic_slice_in_dim(down_weight, my_xc * ff_seg, ff_seg, axis=0))
        flat = held * slot_len
        (
            tokens_all,
            cotangent_all,
            attn_all,
            small_all,
            _,
            out_dealt,
            up_all,
            w_down,
        ) = first_gather(
            depth,
            tokens.reshape(flat, width),
            cotangent.reshape(flat, width),
            attn_mine,
            attn_other,
            small,
            out_slice,
            up_columns(my_y),
            up_columns(1 - my_y),
            down_slice,
        )
        tokens_all = tokens_all.reshape(8 * flat, width)
        cotangent_all = cotangent_all.reshape(8 * flat, width)
        w_down = w_down.reshape(depth * ff_seg, width)
        if y_slow:
            small_all = jnp.transpose(small_all, (1, 0, 2, 3))
        gathered_small = wide(small_all.reshape(fsdp_size, 16 * 256)[:, :small_count])
        sizes = [item.shape[0] for item in small_parts]
        begins = [sum(sizes[:index]) for index in range(len(sizes))]
        (
            gain_a,
            shift_a,
            bias_o,
            gain_m,
            shift_m,
            bias_d,
            bias_q,
            bias_u,
            bias_v,
        ) = [
            gathered_small[:, start : start + size].reshape(-1)
            for start, size in zip(begins, sizes)
        ]
        my_bias_q = lax.dynamic_slice_in_dim(bias_q, head_base(my_y), head_cols)
        my_bias_u = jnp.concatenate(
            [
                lax.dynamic_slice_in_dim(
                    bias_u, owner(z_at, my_y) * ff_own + my_xc * ff_seg, ff_seg
                )
                for z_at in range(depth)
            ]
        )
        bias_kv = jnp.concatenate([jnp.zeros((HEAD,), jnp.float32), bias_v])

        def rows_in_order(gathered):
            if y_slow:
                gathered = jnp.transpose(gathered, (1, 0, 2, 3))
            return gathered.reshape(width, gathered.shape[-1])

        def rows_by_z(values):
            if y_slow:
                return jnp.transpose(
                    values.reshape(2, depth, rows_own, values.shape[-1]), (1, 0, 2, 3)
                )
            return values.reshape(depth, 2, rows_own, values.shape[-1])

        attn_full = rows_in_order(attn_all)
        w_query = attn_full[:, :head_cols]
        w_keyval = attn_full[:, head_cols:]
        w_output = jnp.transpose(out_dealt, (1, 0, 2, 3)).reshape(head_cols, width)
        w_up = rows_in_order(up_all)

        packed = jnp.take(tokens_all, source_row, axis=0)
        grad_mixed = jnp.where(
            valid[:, None], jnp.take(cotangent_all, source_row, axis=0), jnp.zeros((), jnp.bfloat16)
        )
        own_count = MB * PACK
        own_rows = wide(lax.dynamic_slice_in_dim(packed, member * own_count, own_count))
        own_valid = lax.dynamic_slice_in_dim(valid, member * own_count, own_count)[:, None]
        own_grad = wide(lax.dynamic_slice_in_dim(grad_mixed, member * own_count, own_count))

        xhat_all, _ = normalize(wide(packed))
        normed_attn = low(xhat_all * gain_a + shift_a)
        query = low(product(normed_attn, w_query) + my_bias_q)
        keyval = low(product(normed_attn, w_keyval) + bias_kv)
        my_heads = head_cols // HEAD
        query_h = query.reshape(micro, PACK, my_heads, HEAD)
        keys = keyval[:, :HEAD].reshape(micro, PACK, HEAD)
        vals = keyval[:, HEAD:].reshape(micro, PACK, HEAD)
        score_scale = 1.0 / math.sqrt(HEAD)
        scores = (
            jnp.einsum("mshd,mtd->mhst", query_h, keys, preferred_element_type=jnp.float32)
            * score_scale
        )
        scores = jnp.where(allowed[:, None], scores, -1e30)
        expscores = jnp.exp(scores - jnp.max(scores, axis=-1, keepdims=True))
        probs = expscores / jnp.sum(expscores, axis=-1, keepdims=True)
        attended = low(
            jnp.einsum(
                "mhst,mtd->mshd", low(probs), vals, preferred_element_type=jnp.float32
            ).reshape(micro * PACK, head_cols)
        )
        (attn_out,) = plane_scatter([low(product(attended, w_output))], depth, 3)
        middle = own_rows + (attn_out + bias_o)
        xhat_m, scale_m = normalize(middle)
        normed_mlp = plane_gather(low(xhat_m * gain_m + shift_m), depth, 4)
        hidden = product(normed_mlp, w_up) + my_bias_u
        activated, slope = gelu_parts(hidden)
        activated = low(activated)
        grad_hidden = low(slope * product_cols(grad_mixed, w_down))
        mlp_sum, grad_normed = plane_scatter(
            [low(product(activated, w_down)), low(product_cols(grad_hidden, w_up))], depth, 5
        )
        block_own = low(jnp.where(own_valid, middle + (mlp_sum + bias_d), 0.0))
        grad_middle = own_grad + norm_back(grad_normed, gain_m, xhat_m, scale_m)
        d_down = low(product_rows(activated, grad_mixed)).reshape(depth, ff_seg, width)
        d_up = rows_by_z(low(product_rows(normed_mlp, grad_hidden)))

        grad_branch_own = low(grad_middle)
        grad_branch = plane_gather(grad_branch_own, depth, 6)
        d_output = low(product_rows(attended, grad_branch))
        grad_att = low(product_cols(grad_branch, w_output)).reshape(micro, PACK, my_heads, HEAD)
        grad_probs = jnp.einsum("mshd,mtd->mhst", grad_att, vals, preferred_element_type=jnp.float32)
        grad_vals = jnp.einsum(
            "mhst,mshd->mtd", low(probs), grad_att, preferred_element_type=jnp.float32
        )
        inner = jnp.sum(probs * grad_probs, axis=-1, keepdims=True)
        grad_scores = low(probs * (grad_probs - inner))
        grad_query = (
            jnp.einsum("mhst,mtd->mshd", grad_scores, keys, preferred_element_type=jnp.float32)
            * score_scale
        )
        grad_query = low(grad_query.reshape(micro * PACK, head_cols))
        grad_keys = (
            jnp.einsum("mhst,mshd->mtd", grad_scores, query_h, preferred_element_type=jnp.float32)
            * score_scale
        )
        grad_keyval = low(jnp.concatenate([grad_keys, grad_vals], axis=2)).reshape(
            micro * PACK, 2 * HEAD
        )
        d_query = low(product_rows(normed_attn, grad_query))
        d_keyval = low(product_rows(normed_attn, grad_keyval))
        grad_input_part = product_cols(grad_query, w_query) + product_cols(grad_keyval, w_keyval)
        own_xhat, own_scale = normalize(own_rows)

        def colsum(values):
            return jnp.sum(wide(values), axis=0)

        def spread_vec(values, parts, size, full):
            out = jnp.zeros((full,), jnp.float32)
            for index, begin in enumerate(parts):
                out = lax.dynamic_update_slice(
                    out, values[index * size : (index + 1) * size], (begin,)
                )
            return out

        vec_query = spread_vec(colsum(grad_query), [head_base(my_y)], head_cols, width)
        vec_up = spread_vec(
            colsum(grad_hidden),
            [owner(z_at, my_y) * ff_own + my_xc * ff_seg for z_at in range(depth)],
            ff_seg,
            ff,
        )
        vectors = [
            jnp.sum(grad_input_part * xhat_all, axis=0),
            jnp.sum(grad_input_part, axis=0),
            colsum(grad_branch_own),
            jnp.sum(grad_normed * xhat_m, axis=0),
            jnp.sum(grad_normed, axis=0),
            jnp.sum(own_grad, axis=0),
            vec_query,
            vec_up,
            colsum(grad_keyval[:, HEAD:]),
        ]
        vectors = jnp.concatenate([item.reshape(fsdp_size, -1) for item in vectors], axis=1)
        vectors = jnp.pad(low(vectors), ((0, 0), (0, 16 * 256 - small_count)))
        if y_slow:
            d_vec = jnp.transpose(vectors.reshape(2, depth, 16, 256), (1, 0, 2, 3))
        else:
            d_vec = vectors.reshape(depth, 2, 16, 256)

        d_attn = rows_by_z(jnp.concatenate([d_query, d_keyval], axis=1))
        d_out_parts = jnp.transpose(
            d_output.reshape(depth // 4, 4, out_seg, width), (1, 0, 2, 3)
        )
        up_all, down_all, attn_all, vec_all, out_all, grad_first = last_scatter(
            depth,
            d_up,
            d_down,
            d_attn,
            d_vec,
            d_out_parts,
            low(grad_input_part).reshape(8, MB * PACK, width),
        )
        grad_input = low(grad_middle + norm_back(grad_first, gain_a, own_xhat, own_scale))

        def by_y(pair):
            first = my_y == 0
            return (
                jnp.where(first, pair[0], pair[1]),
                jnp.where(first, pair[1], pair[0]),
            )

        up_pair = [item.reshape(4, rows_own, depth, ff_seg) for item in by_y(up_all)]
        if y_slow:
            up_grad = jnp.stack([jnp.transpose(item, (1, 2, 0, 3)) for item in up_pair], axis=1)
        else:
            up_grad = jnp.stack([jnp.transpose(item, (1, 2, 0, 3)) for item in up_pair], axis=2)
        up_grad = wide(up_grad.reshape(rows_own, ff))
        query_pair = by_y(attn_all[..., :head_cols])
        if y_slow:
            query_grad = jnp.stack([jnp.transpose(item, (1, 0, 2)) for item in query_pair], axis=1)
        else:
            query_grad = jnp.stack([jnp.transpose(item, (1, 0, 2)) for item in query_pair], axis=2)
        query_grad = wide(query_grad.reshape(rows_own, width))
        keyval_grad = jnp.sum(wide(attn_all[..., head_cols:]), axis=(0, 1))
        down_grad = wide(down_all.reshape(ff_own, width))
        output_grad = wide(out_all.reshape(rows_own, width))
        vec_own = jnp.sum(wide(vec_all), axis=0).reshape(16 * 256)
        (
            gain_a_grad,
            shift_a_grad,
            bias_o_grad,
            gain_m_grad,
            shift_m_grad,
            bias_d_grad,
            bias_q_grad,
            bias_u_grad,
            bias_v_grad,
        ) = [vec_own[start : start + size] for start, size in zip(begins, sizes)]

        dealt_here = lax.dynamic_index_in_dim(in_group, my_y, 0, keepdims=False)
        holders = (dealt_here // held).reshape(4, held)
        slots = (dealt_here % held).reshape(4, held)
        my_holders = lax.dynamic_index_in_dim(holders, my_xc, 0, keepdims=False)
        my_lens = lax.dynamic_slice_in_dim(lens, member * MB, MB).reshape(held)
        my_starts = (
            lax.dynamic_slice_in_dim(starts, member * MB, MB) + jnp.arange(MB)[:, None] * PACK
        ).reshape(held)
        send_seq = jnp.argmax(my_holders[None, :] == jnp.arange(4)[:, None], axis=1)
        pos = jnp.arange(slot_len)
        live = pos[None, :] < my_lens[send_seq][:, None]
        send_rows = jnp.where(live, my_starts[send_seq][:, None] + pos[None, :], 0)
        slot_of = jnp.sum(jnp.where(holders == my_xc, slots, 0), axis=1)
        from_dev = jnp.argmax(slot_of[None, :] == jnp.arange(held)[:, None], axis=1)

        def send_back(own):
            out = jnp.where(
                live[..., None], jnp.take(own, send_rows, axis=0), jnp.zeros((), jnp.bfloat16)
            )
            got = lax.all_to_all(out, DP, split_axis=0, concat_axis=0, tiled=True)
            return jnp.stack(
                [
                    lax.dynamic_index_in_dim(got, from_dev[index], 0, keepdims=False)
                    for index in range(held)
                ]
            )

        return (
            send_back(block_own),
            send_back(grad_input),
            gain_a_grad,
            shift_a_grad,
            query_grad,
            bias_q_grad,
            keyval_grad,
            bias_v_grad,
            output_grad,
            bias_o_grad,
            gain_m_grad,
            shift_m_grad,
            up_grad,
            bias_u_grad,
            down_grad,
            bias_d_grad,
        )

    return shards, depth, owner_axes


def solution(mesh):
    shards, depth, owner_axes = build(mesh)
    sizes = {"z": depth, "y": 2}
    fine = Mesh(
        mesh.devices.reshape(sizes[owner_axes[0]], sizes[owner_axes[1]], 2, 2),
        owner_axes + ("x", "c"),
    )
    rows = P(owner_axes + ("x", "c"), None, None)
    vec = P(owner_axes)
    mat = P(owner_axes, None)
    in_specs = (
        rows, rows, P(), P(),
        vec, vec, mat, vec, mat, vec, mat, vec, vec, vec, mat, vec, mat, vec,
    )
    out_specs = (
        rows, rows,
        vec, vec, mat, vec, mat, vec, mat, vec, vec, vec, mat, vec, mat, vec,
    )
    return jax.shard_map(shards, mesh=fine, in_specs=in_specs, out_specs=out_specs, check_vma=False)
```

```python
import math

import jax
import jax.numpy as jnp
from jax import lax
from jax.experimental import pallas as pl
from jax.experimental.pallas import tpu as pltpu
from jax.sharding import Mesh
from jax.sharding import PartitionSpec as P

HEADS = 16
HEAD = 128
MB = 2
SEATS = 2
PACK = 80

epsilon = 1e-05
gelu_scale = 0.7978845608028654
gelu_cubic = 0.044715

DP = ("x", "c")


def low(values):
    return values.astype(jnp.bfloat16)


def wide(values):
    return values.astype(jnp.float32)


def product(left_mat, right_mat):
    return jnp.dot(left_mat, right_mat, preferred_element_type=jnp.float32)


def product_rows(left_mat, right_mat):
    return lax.dot_general(
        left_mat, right_mat, (((0,), (0,)), ((), ())), preferred_element_type=jnp.float32
    )


def product_cols(left_mat, right_mat):
    return lax.dot_general(
        left_mat, right_mat, (((1,), (1,)), ((), ())), preferred_element_type=jnp.float32
    )


def normalize(rows):
    center = rows - jnp.mean(rows, axis=-1, keepdims=True)
    spread = jnp.mean(center * center, axis=-1, keepdims=True)
    scale = lax.rsqrt(spread + epsilon)
    return center * scale, scale


def norm_back(grad_normed, gain, xhat, scale):
    g = grad_normed * gain
    inner = jnp.mean(g * xhat, axis=-1, keepdims=True)
    return scale * (g - jnp.mean(g, axis=-1, keepdims=True) - xhat * inner)


def gelu_parts(values):
    inner = jnp.tanh(gelu_scale * (values + gelu_cubic * values * values * values))
    activated = 0.5 * values * (1.0 + inner)
    slope = 0.5 * (1.0 + inner) + 0.5 * values * (1.0 - inner * inner) * gelu_scale * (
        1.0 + 3.0 * gelu_cubic * values * values
    )
    return activated, slope


MESH_ID = pl.DeviceIdType.MESH
VMEM_LIMIT = 56 * 1024 * 1024


class Spot:
    def __init__(self, depth):
        self.depth = depth
        self.z = lax.axis_index("z")
        self.y = lax.axis_index("y")
        self.x = lax.axis_index("x")
        self.c = lax.axis_index("c")
        self.to_c = {"c": 1 - self.c}
        self.to_x = {"x": 1 - self.x}
        self.to_y = {"y": 1 - self.y}
        self.to_xc = {"x": 1 - self.x, "c": 1 - self.c}
        self.up = {"z": self.z + 1}
        self.down = {"z": self.z - 1}

    def ring(self):
        before = {"z": lax.rem(self.z + self.depth - 1, self.depth)}
        return ({"z": lax.rem(self.z + 1, self.depth)}, before)

    def barrier(self, plane, line):
        bar = pltpu.get_barrier_semaphore()
        for to in plane:
            pl.semaphore_signal(bar, inc=1, device_id=to, device_id_type=MESH_ID)
        if line:

            @pl.when(self.z > 0)
            def _():
                pl.semaphore_signal(bar, inc=1, device_id=self.down, device_id_type=MESH_ID)

            @pl.when(self.z < self.depth - 1)
            def _():
                pl.semaphore_signal(bar, inc=1, device_id=self.up, device_id_type=MESH_ID)

        count = len(plane)
        if line:
            lower = jnp.where(self.z > 0, 1, 0)
            upper = jnp.where(self.z < self.depth - 1, 1, 0)
            count = count + lower + upper
        pl.semaphore_wait(bar, count)


class Net:
    def __init__(self, send_sems, recv_sems, local_sems):
        self.send_sems = send_sems
        self.recv_sems = recv_sems
        self.local_sems = local_sems
        self.count = 0
        self.local_count = 0
        self.open = []

    def remote(self, src, dst, to, arrives=None):
        copy = Copy(self, self.count, src, dst, to, arrives)
        self.count += 1
        return copy

    def local(self, src, dst):
        copy = pltpu.make_async_copy(src, dst, self.local_sems.at[self.local_count])
        self.local_count += 1
        return copy


class Copy:
    def __init__(self, net, index, src, dst, to, arrives):
        def make(target):
            return pltpu.make_async_remote_copy(
                src_ref=src,
                dst_ref=target,
                send_sem=net.send_sems.at[index],
                recv_sem=net.recv_sems.at[index],
                device_id=to,
                device_id_type=MESH_ID,
            )

        self.out = make(dst)
        self.into = make(dst if arrives is None else arrives)

    def start(self):
        self.out.start()

    def got(self):
        self.into.wait_recv()

    def sent(self):
        self.out.wait_send()


class PlaneGather:
    def __init__(self, net, spot, own, slots, share=2):
        def at(y, x, c):
            return y * 4 + x * 2 + c

        y, x, c = spot.y, spot.x, spot.c
        self.both = share == 2
        half = own.shape[0] // share
        lo, hi = pl.ds(0, half), pl.ds(half * (share - 1), half)
        me = at(y, x, c)
        on_x, on_y, on_d = at(y, 1 - x, c), at(1 - y, x, c), at(1 - y, 1 - x, c)
        peer = [at(y, x, 1 - c), at(y, 1 - x, 1 - c), at(1 - y, x, 1 - c), at(1 - y, 1 - x, 1 - c)]

        def slot(index):
            return slots.at[index]

        self.keep = net.local(own, slot(me))
        self.x = net.remote(own, slot(me), spot.to_x, slot(on_x))
        self.y = net.remote(own, slot(me), spot.to_y, slot(on_y))
        self.c = net.remote(own, slot(me), spot.to_c, slot(peer[0]))
        self.x_on_y = net.remote(
            slots.at[on_x, lo], slots.at[on_x, lo], spot.to_y, slots.at[on_d, lo]
        )
        self.x_on_c = net.remote(slot(on_x), slot(on_x), spot.to_c, slot(peer[1]))
        self.y_on_c = net.remote(slot(on_y), slot(on_y), spot.to_c, slot(peer[2]))
        self.lo_on_c = net.remote(
            slots.at[on_d, lo], slots.at[on_d, lo], spot.to_c, slots.at[peer[3], lo]
        )
        if self.both:
            self.y_on_x = net.remote(
                slots.at[on_y, hi], slots.at[on_y, hi], spot.to_x, slots.at[on_d, hi]
            )
            self.hi_on_c = net.remote(
                slots.at[on_d, hi], slots.at[on_d, hi], spot.to_c, slots.at[peer[3], hi]
            )

    def start(self):
        self.x.start()
        self.y.start()
        self.c.start()
        self.keep.start()

    def middle(self):
        self.x.got()
        self.x_on_y.start()
        self.x_on_c.start()
        self.y.got()
        if self.both:
            self.y_on_x.start()
        self.y_on_c.start()

    def last(self):
        self.x_on_y.got()
        self.lo_on_c.start()
        if self.both:
            self.y_on_x.got()
            self.hi_on_c.start()

    def finish(self):
        second = (self.y_on_x, self.hi_on_c) if self.both else ()
        for copy in (self.c, self.x_on_c, self.y_on_c, self.lo_on_c, *second[1:]):
            copy.got()
        firsts = (self.x, self.y, self.c, self.x_on_y, self.x_on_c, self.y_on_c, self.lo_on_c)
        for copy in (*firsts, *second):
            copy.sent()
        self.keep.wait()

    remotes = 9
    locals = 1


def add_rows(into, other, step=32):
    rows = into.shape[0]

    @pl.loop(0, rows // step)
    def _(index):
        at = pl.ds(pl.multiple_of(index * step, step), step)
        into[at, :] = low(wide(into[at, :]) + wide(other[at, :]))


class PlaneScatter:
    remotes = 10

    @staticmethod
    def buffers(rows, width):
        return [
            pltpu.VMEM((4, rows, width), jnp.bfloat16),
            pltpu.VMEM((rows, width), jnp.bfloat16),
            pltpu.VMEM((rows, width), jnp.bfloat16),
            pltpu.VMEM((rows, width), jnp.bfloat16),
        ]

    def __init__(self, net, spot, parts, sums, diag, from_x, from_y):
        y, x, c = spot.y, spot.x, spot.c
        half = parts.shape[1] // 2
        lo, hi = pl.ds(0, half), pl.ds(half, half)
        self.own, self.nx, self.ny, self.nd = (
            y * 2 + x,
            y * 2 + 1 - x,
            (1 - y) * 2 + x,
            (1 - y) * 2 + 1 - x,
        )
        self.parts, self.sums, self.diag = parts, sums, diag
        self.stacked = parts.shape[0] == 4
        self.from_x, self.from_y, self.c = from_x, from_y, c
        self.lo, self.hi = lo, hi
        self.first = {
            key: net.remote(
                parts.at[at] if self.stacked else parts.at[at * 2 + 1 - c], sums.at[at], spot.to_c
            )
            for key, at in (("d", self.nd), ("x", self.nx), ("y", self.ny), ("o", self.own))
        }
        self.d_lo = net.remote(sums.at[self.nd, lo], diag.at[lo], spot.to_x)
        self.d_hi = net.remote(sums.at[self.nd, hi], diag.at[hi], spot.to_y)
        self.x_lo = net.remote(sums.at[self.nx, lo], from_x.at[lo], spot.to_x)
        self.y_hi = net.remote(sums.at[self.ny, hi], from_y.at[hi], spot.to_y)
        self.x_hi = net.remote(sums.at[self.nx, hi], from_x.at[hi], spot.to_x)
        self.y_lo = net.remote(sums.at[self.ny, lo], from_y.at[lo], spot.to_y)

    def start(self):
        for copy in self.first.values():
            copy.start()

    def pair(self, key, at):
        self.first[key].got()
        if self.stacked:
            self.compute(at * 2 + self.c, at)
        else:
            add_rows(self.sums.at[at], self.parts.at[at * 2 + self.c])

    def middle(self):
        self.pair("d", self.nd)
        self.d_lo.start()
        self.d_hi.start()
        self.pair("x", self.nx)
        self.x_lo.start()
        self.pair("y", self.ny)
        self.y_hi.start()
        self.pair("o", self.own)

    def last(self):
        self.d_lo.got()
        add_rows(self.sums.at[self.ny, self.lo], self.diag.at[self.lo], 16)
        self.y_lo.start()
        self.d_hi.got()
        add_rows(self.sums.at[self.nx, self.hi], self.diag.at[self.hi], 16)
        self.x_hi.start()

    def finish(self, result):
        for copy in (self.x_lo, self.y_hi, self.x_hi, self.y_lo):
            copy.got()

        @pl.loop(0, result.shape[0] // 16)
        def _(index):
            at = pl.ds(pl.multiple_of(index * 16, 16), 16)
            result[at, :] = (
                wide(self.sums[self.own, at, :]) + wide(self.from_x[at, :]) + wide(self.from_y[at, :])
            )

        for copy in (
            *self.first.values(),
            self.d_lo,
            self.d_hi,
            self.x_lo,
            self.x_hi,
            self.y_lo,
            self.y_hi,
        ):
            copy.sent()


class LineGather:
    def __init__(self, net, spot, slots):
        self.spot, depth, z = spot, spot.depth, spot.z
        self.hops = []
        for step in range(depth - 1):
            lower = jnp.maximum(z - step, 0)
            upper = jnp.minimum(z + step, depth - 1)
            from_low = jnp.maximum(z - 1 - step, 0)
            from_high = jnp.minimum(z + 1 + step, depth - 1)
            self.hops.append(
                (
                    net.remote(slots(lower), slots(lower), spot.up, slots(from_low)),
                    net.remote(slots(upper), slots(upper), spot.down, slots(from_high)),
                )
            )

    @staticmethod
    def remotes(depth):
        return 2 * (depth - 1)

    def sends(self, step):
        z, last = self.spot.z, self.spot.depth - 1
        return (
            ((z >= step) & (z < last), self.hops[step][0]),
            ((z + step <= last) & (z > 0), self.hops[step][1]),
        )

    def takes(self, step):
        z, last = self.spot.z, self.spot.depth - 1
        return ((z >= step + 1, self.hops[step][0]), (z + step + 1 <= last, self.hops[step][1]))

    def start(self, step):
        for cond, copy in self.sends(step):
            pl.when(cond)(copy.start)

    def got(self, step):
        for cond, copy in self.takes(step):
            pl.when(cond)(copy.got)

    def hop(self, step):
        for (came, old), (goes, new) in zip(self.takes(step - 1), self.sends(step)):
            pl.when(came)(old.got)
            pl.when(goes)(new.start)

    def finish(self):
        for step in range(self.spot.depth - 1):
            for cond, copy in self.sends(step):
                pl.when(cond)(copy.sent)


class LineScatter:
    def __init__(self, net, spot, parts, from_low, from_high, add):
        self.spot, depth, z = spot, spot.depth, spot.z
        self.parts, self.from_low, self.from_high, self.add = parts, from_low, from_high, add
        self.ups, self.downs = [], []
        for step in range(depth - 1):
            self.ups.append(net.remote(parts(depth - 1 - step), from_low.at[step], spot.up))
            self.downs.append(net.remote(parts(step), from_high.at[step], spot.down))

    remotes = LineGather.remotes

    def stage(self, step):
        z, last = self.spot.z, self.spot.depth - 1
        up_to, down_to = last - step, step

        @pl.when((z > 0) & (z < up_to))
        def _():
            self.ups[step].got()
            self.add(self.parts(up_to), self.from_low.at[step])

        @pl.when(z < up_to)
        def _():
            self.ups[step].start()

        @pl.when((z < last) & (z > down_to))
        def _():
            self.downs[step].got()
            self.add(self.parts(down_to), self.from_high.at[step])

        @pl.when(z > down_to)
        def _():
            self.downs[step].start()

    def total(self):
        z, last = self.spot.z, self.spot.depth - 1
        for step in range(last):

            @pl.when((z > 0) & (z == last - step))
            def _():
                self.ups[step].got()
                self.add(self.parts(last - step), self.from_low.at[step])

            @pl.when((z < last) & (z == step))
            def _():
                self.downs[step].got()
                self.add(self.parts(step), self.from_high.at[step])

    def finish(self):
        z, last = self.spot.z, self.spot.depth - 1
        for step in range(last):
            pl.when(z < last - step)(self.ups[step].sent)
            pl.when(z > step)(self.downs[step].sent)


class DpGather:
    remotes = 3

    def __init__(self, net, spot, own, slots):
        me = spot.x * 2 + spot.c
        on_x = (1 - spot.x) * 2 + spot.c
        self.keep = net.local(own, slots.at[me])
        self.x = net.remote(own, slots.at[me], spot.to_x, slots.at[on_x])
        self.c = net.remote(own, slots.at[me], spot.to_c, slots.at[spot.x * 2 + 1 - spot.c])
        self.x_on_c = net.remote(
            slots.at[on_x],
            slots.at[on_x],
            spot.to_c,
            slots.at[(1 - spot.x) * 2 + 1 - spot.c],
        )

    def start(self):
        self.x.start()
        self.c.start()
        self.keep.start()

    def last(self):
        self.x.got()
        self.x_on_c.start()

    def finish(self):
        self.c.got()
        self.x_on_c.got()
        for copy in (self.x, self.c, self.x_on_c):
            copy.sent()
        self.keep.wait()


class DpExchange:
    remotes = 3

    def __init__(self, net, spot, parts, slots):
        me = spot.x * 2 + spot.c
        on_x = (1 - spot.x) * 2 + spot.c
        on_c = spot.x * 2 + 1 - spot.c
        on_xc = (1 - spot.x) * 2 + 1 - spot.c
        self.keep = net.local(parts.at[me], slots.at[me])
        self.moves = [
            net.remote(parts.at[at], slots.at[me], to, slots.at[at])
            for at, to in ((on_xc, spot.to_xc), (on_x, spot.to_x), (on_c, spot.to_c))
        ]

    def start(self):
        for copy in self.moves:
            copy.start()
        self.keep.start()

    def got(self):
        for copy in self.moves:
            copy.got()
        self.keep.wait()

    def finish(self):
        for copy in self.moves:
            copy.sent()


def net_scratch(remotes, locals_):
    return [
        pltpu.SemaphoreType.DMA((remotes,)),
        pltpu.SemaphoreType.DMA((remotes,)),
        pltpu.SemaphoreType.DMA((max(locals_, 1),)),
    ]


ANY = pl.BlockSpec(memory_space=pl.ANY)
IN_VMEM = pl.BlockSpec(memory_space=pltpu.VMEM)


def lasts(micros, moved):
    return pl.CostEstimate(
        flops=int(micros * 1e9), bytes_accessed=int(moved), transcendentals=0
    )


def comm_params(collective_id):
    return pltpu.CompilerParams(
        collective_id=collective_id, has_side_effects=True, vmem_limit_bytes=VMEM_LIMIT
    )


def low_shape(*dims):
    return jax.ShapeDtypeStruct(dims, jnp.bfloat16)


def wide_shape(*dims):
    return jax.ShapeDtypeStruct(dims, jnp.float32)


def low_vmem(*dims):
    return pltpu.VMEM(dims, jnp.bfloat16)


def pick_rows(chooser, source, result, step=512):
    width = result.shape[-1]

    @pl.loop(0, width // step)
    def _(index):
        at = pl.ds(pl.multiple_of(index * step, step), step)
        rows = source[..., at].reshape(chooser.shape[1], step)
        result[..., at] = low(product(chooser[...], rows)).reshape(*result.shape[:-1], step)


def opening(depth, owner, tok_send, cot_send, chooser, query_weight, keyval_weight, output_weight, down_weight, small, up_mine, up_other):
    rows = chooser.shape[0]
    width = tok_send.shape[-1]
    group = depth // 4
    rows_own = query_weight.shape[0]
    head_cols = width // 8
    kv_rows = rows_own // 4
    kv_cols = keyval_weight.shape[1]
    seg = down_weight.shape[0] // 4

    def kernel(
        tok, cot, choose, query_w, kv_w, out_w, down_w, small_m, up_m, up_o,
        own_tok, own_cot, up_own, down_2,
        tok_all, cot_all, query_all, kv_all, small_all, out_dealt, up_all, down_all,
        tok_got, cot_got, out_all, kv_line, query_m, query_o, query_y, small_y, down_m, down_1,
        query_f, out_f, kv_f, down_f, *sems,
    ):
        spot = Spot(depth)
        net = Net(*sems)
        z, y = spot.z, spot.y
        xc = spot.x * 2 + spot.c
        after, _ = spot.ring()
        before = lax.rem(z + depth - 1, depth)
        before_2 = lax.rem(z + 2 * depth - 2, depth)

        def head_base(y_at):
            return pl.multiple_of(owner(xc * group, y_at) * rows_own, 128)

        def strip(ref, size):
            return ref.at[pl.ds(pl.multiple_of(xc * size, size), size)]

        def z_slot(at):
            return kv_line.at[pl.ds(pl.multiple_of(at * kv_rows, kv_rows), kv_rows)]

        reads = [
            net.local(query_w.at[:, pl.ds(head_base(1 - y), head_cols)], query_f.at[0]),
            net.local(strip(down_w, seg), down_f),
            net.local(strip(out_w, kv_rows), out_f),
            net.local(strip(kv_w, kv_rows), kv_f),
            net.local(query_w.at[:, pl.ds(head_base(y), head_cols)], query_f.at[1]),
        ]
        tok_deal = DpExchange(net, spot, tok, tok_got)
        cot_deal = DpExchange(net, spot, cot, cot_got)
        tok_run = PlaneGather(net, spot, own_tok, tok_all)
        cot_run = PlaneGather(net, spot, own_cot, cot_all, share=1)
        kv_run = PlaneGather(net, spot, kv_line, kv_all)
        y_query = net.remote(query_o, query_y, spot.to_y)
        y_small = net.remote(small_m, small_y, spot.to_y)
        y_up = net.remote(up_o, up_own.at[y], spot.to_y, up_own.at[1 - y])
        d_hops = [net.remote(down_m, down_1, after), net.remote(down_1, down_2, after)]
        keep_small = net.local(small_m, small_all.at[z, y])
        keep_up_mine = net.local(up_m, up_all.at[z, y])
        keep_query = net.local(query_m, query_all.at[z, y])
        keep_query_y = net.local(query_y, query_all.at[z, 1 - y])
        keep_small_y = net.local(small_y, small_all.at[z, 1 - y])
        keep_up_y = net.local(up_own.at[1 - y], up_all.at[z, 1 - y])
        keep_down = [
            net.local(down_m, down_all.at[z]),
            net.local(down_1, down_all.at[before]),
            net.local(down_2, down_all.at[before_2]),
        ]
        run_out = LineGather(net, spot, lambda at: out_all.at[at // group, at % group])
        run_kv = LineGather(net, spot, z_slot)
        run_query = LineGather(net, spot, lambda at: query_all.at[at])
        run_small = LineGather(net, spot, lambda at: small_all.at[at])
        out_deal = DpExchange(net, spot, out_all, out_dealt)
        for copy in reads:
            copy.start()
        keep_small.start()
        keep_up_mine.start()
        spot.barrier((spot.to_c, spot.to_x, spot.to_y, spot.to_xc, *spot.ring()), False)
        tok_deal.start()
        reads[0].wait()
        query_o[...] = low(query_f[0])
        y_query.start()
        y_small.start()
        reads[2].wait()
        out_all[z // group, z % group] = low(out_f[...])
        run_out.start(0)
        reads[3].wait()
        z_slot(z)[...] = low(kv_f[...])
        run_kv.start(0)
        reads[4].wait()
        query_m[...] = low(query_f[1])
        keep_query.start()
        reads[1].wait()

        @pl.loop(0, seg // 16)
        def _(index):
            at = pl.ds(pl.multiple_of(index * 16, 16), 16)
            down_m[at, :] = low(down_f[at, :])

        keep_query.wait()
        keep_small.wait()
        y_query.got()
        keep_query_y.start()
        y_small.got()
        keep_small_y.start()
        keep_query_y.wait()
        keep_small_y.wait()
        run_query.start(0)
        run_small.start(0)
        y_up.start()
        d_hops[0].start()
        keep_down[0].start()

        @pl.loop(0, rows_own // 16)
        def _(index):
            at = pl.ds(pl.multiple_of(index * 16, 16), 16)
            up_own[y, at, :] = up_m[at, :]

        tok_deal.got()
        pick_rows(choose, tok_got, own_tok)
        tok_run.start()
        cot_deal.start()
        run_out.hop(1)
        run_kv.hop(1)
        run_query.hop(1)
        run_small.hop(1)
        y_up.got()
        keep_up_y.start()
        cot_deal.got()
        pick_rows(choose, cot_got, own_cot)
        tok_run.middle()
        cot_run.start()
        d_hops[0].got()
        d_hops[1].start()
        keep_down[1].start()
        for step in range(2, depth - 1):
            run_out.hop(step)
            run_kv.hop(step)
            run_query.hop(step)
            run_small.hop(step)
        tok_run.last()
        run_out.got(depth - 2)
        run_kv.got(depth - 2)
        kv_run.start()
        out_deal.start()
        run_query.got(depth - 2)
        run_small.got(depth - 2)
        kv_run.middle()
        cot_run.middle()
        kv_run.last()
        cot_run.last()
        d_hops[1].got()
        keep_down[2].start()
        out_deal.got()
        runs = (run_out, run_kv, run_query, run_small, tok_run, kv_run, cot_run)
        for run in (*runs, tok_deal, cot_deal, out_deal):
            run.finish()
        for copy in (y_query, y_small, y_up, *d_hops):
            copy.sent()
        for copy in (keep_up_mine, keep_up_y, *keep_down):
            copy.wait()

    remotes = (
        3 * DpExchange.remotes + 3 * PlaneGather.remotes + 5 + 4 * LineGather.remotes(depth)
    )
    operands = (
        tok_send, cot_send, chooser, query_weight, keyval_weight, output_weight, down_weight, small,
        up_mine, up_other,
    )
    wide_type = jnp.float32
    return pl.pallas_call(
        kernel,
        out_shape=[
            low_shape(rows, width),
            low_shape(rows, width),
            low_shape(2, *up_mine.shape),
            low_shape(seg, width),
            low_shape(8, rows, width),
            low_shape(8, rows, width),
            low_shape(depth, 2, rows_own, head_cols),
            low_shape(8, depth * kv_rows, kv_cols),
            low_shape(depth, 2, *small.shape),
            low_shape(4, group, kv_rows, width),
            low_shape(depth, 2, *up_mine.shape),
            low_shape(depth, seg, width),
        ],
        in_specs=[IN_VMEM] * 3 + [ANY] * 4 + [IN_VMEM] * 3,
        out_specs=[IN_VMEM] * 4 + [ANY] * 8,
        scratch_shapes=[
            low_vmem(*tok_send.shape),
            low_vmem(*tok_send.shape),
            low_vmem(4, group, kv_rows, width),
            low_vmem(depth * kv_rows, kv_cols),
            low_vmem(rows_own, head_cols),
            low_vmem(rows_own, head_cols),
            low_vmem(rows_own, head_cols),
            low_vmem(*small.shape),
            low_vmem(seg, width),
            low_vmem(seg, width),
            pltpu.VMEM((2, rows_own, head_cols), wide_type),
            pltpu.VMEM((kv_rows, width), wide_type),
            pltpu.VMEM((kv_rows, kv_cols), wide_type),
            pltpu.VMEM((seg, width), wide_type),
            *net_scratch(remotes, 24),
        ],
        compiler_params=comm_params(1),
        cost_estimate=lasts(85, 1 << 20),
    )(*operands)


ROWS_STEP = 32


def row_loop(count):
    def decorate(body):
        @pl.loop(0, count // ROWS_STEP)
        def _(index):
            body(pl.ds(pl.multiple_of(index * ROWS_STEP, ROWS_STEP), ROWS_STEP))

    return decorate


def feed_blocks(run, c, parts, block):
    width = parts.shape[-1]

    def columns(body):
        @pl.loop(0, width // 512)
        def _(index):
            body(pl.ds(pl.multiple_of(index * 512, 512), 512))

    def send(at, member):
        @columns
        def _(cols):
            parts[at, :, cols] = low(block(member, cols))

    def merge(member, at):
        @columns
        def _(cols):
            run.sums[at, :, cols] = low(wide(run.sums[at, :, cols]) + block(member, cols))

    run.compute = merge
    for key, at in (("d", run.nd), ("x", run.nx), ("y", run.ny), ("o", run.own)):
        send(at, at * 2 + 1 - c)
        run.first[key].start()


def attention_out(depth, attended, w_output, own_tok, bias, gain, shift, up_piece):
    rows, width = own_tok.shape

    def kernel(att, w_out, tok, bias_row, gain_row, shift_row, piece, middle, normed_all, hop_1, hop_2,
               parts, normed, sums, diag, from_x, from_y, *sems):
        spot = Spot(depth)
        net = Net(*sems)
        run = PlaneScatter(net, spot, parts, sums, diag, from_x, from_y)
        gather = PlaneGather(net, spot, normed, normed_all)
        after, _ = spot.ring()
        ups = [net.remote(piece, hop_1, after), net.remote(hop_1, hop_2, after)]

        def block(member, cols):
            rows_at = pl.ds(pl.multiple_of(member * rows, rows), rows)
            return product(att[rows_at, :], w_out[:, cols])

        spot.barrier((spot.to_c, spot.to_x, spot.to_y, *spot.ring()), False)
        ups[0].start()
        feed_blocks(run, spot.c, parts, block)
        run.middle()
        run.last()
        run.finish(middle)

        @row_loop(rows)
        def _(at):
            total = wide(tok[at, :]) + (middle[at, :] + bias_row[...])
            middle[at, :] = total
            xhat, _ = normalize(total)
            normed[at, :] = low(xhat * gain_row[...] + shift_row[...])

        gather.start()
        ups[0].got()
        ups[1].start()
        gather.middle()
        gather.last()
        gather.finish()
        ups[1].got()
        for copy in ups:
            copy.sent()

    return pl.pallas_call(
        kernel,
        out_shape=[
            wide_shape(rows, width),
            low_shape(8, rows, width),
            low_shape(*up_piece.shape),
            low_shape(*up_piece.shape),
        ],
        in_specs=[IN_VMEM] * 6 + [ANY],
        out_specs=[IN_VMEM, ANY, ANY, ANY],
        scratch_shapes=[
            low_vmem(4, rows, width),
            low_vmem(rows, width),
            *PlaneScatter.buffers(rows, width),
            *net_scratch(PlaneScatter.remotes + PlaneGather.remotes + 2, 1),
        ],
        compiler_params=comm_params(3),
        cost_estimate=lasts(60, 1 << 20),
    )(attended, w_output, own_tok, bias, gain, shift, up_piece)


def mlp_back(depth, grad_hidden, w_up, activated, w_down, middle, own_cot, gain, bias, d_down, d_up):
    rows, width = own_cot.shape

    def kernel(gh, up, act, down, mid, cot, gain_row, bias_row, dd, du,
               grad_normed, grad_middle, branch_all, block_out, dd_sum, du_sum,
               parts, branch, sums, diag, from_x, from_y,
               parts2, sums2, diag2, from_x2, from_y2, mlp_sum, dd_got, *sems):
        spot = Spot(depth)
        net = Net(*sems)
        z = spot.z
        run = PlaneScatter(net, spot, parts, sums, diag, from_x, from_y)
        run2 = PlaneScatter(net, spot, parts2, sums2, diag2, from_x2, from_y2)
        gather = PlaneGather(net, spot, branch, branch_all)
        after, _ = spot.ring()

        def slot(step):
            return lax.rem(z + 2 * depth - 1 - step, depth)

        def landing(step):
            return dd_sum if step == depth - 1 else dd_got.at[step - 1]

        du_hop = net.remote(du.at[slot(0)], du_sum, after)
        dd_hops = [net.remote(dd.at[slot(0)], landing(1), after)]
        for step in range(1, depth - 1):
            dd_hops.append(net.remote(landing(step), landing(step + 1), after))

        def ring_step(step):
            dd_hops[step - 1].got()
            add_rows(landing(step), dd.at[slot(step)], 32)
            if step < depth - 1:
                dd_hops[step].start()

        def block(member, cols):
            rows_at = pl.ds(pl.multiple_of(member * rows, rows), rows)
            return product_cols(gh[rows_at, :], up[cols, :])

        def block2(member, cols):
            rows_at = pl.ds(pl.multiple_of(member * rows, rows), rows)
            return product(act[rows_at, :], down[:, cols])

        spot.barrier((spot.to_c, spot.to_x, spot.to_y, *spot.ring()), False)
        dd_hops[0].start()
        feed_blocks(run, spot.c, parts, block)
        run.middle()
        feed_blocks(run2, spot.c, parts2, block2)
        run.last()
        ring_step(1)
        run.finish(grad_normed)

        @row_loop(rows)
        def _(at):
            xhat, scale = normalize(mid[at, :])
            grad = wide(cot[at, :]) + norm_back(grad_normed[at, :], gain_row[...], xhat, scale)
            grad_middle[at, :] = grad
            branch[at, :] = low(grad)

        gather.start()
        for step in range(2, depth - 1):
            ring_step(step)
        gather.middle()
        run2.middle()
        gather.last()
        ring_step(depth - 1)
        du_hop.start()
        run2.last()
        gather.finish()
        run2.finish(mlp_sum)

        @row_loop(rows)
        def _(at):
            block_out[at, :] = low(mid[at, :] + (mlp_sum[at, :] + bias_row[...]))

        du_hop.got()
        for at in range(2):
            add_rows(du_sum.at[at], du.at[slot(1), at], 32)
        for copy in (*dd_hops, du_hop):
            copy.sent()

    return pl.pallas_call(
        kernel,
        out_shape=[
            wide_shape(rows, width),
            wide_shape(rows, width),
            low_shape(8, rows, width),
            low_shape(rows, width),
            low_shape(*d_down.shape[1:]),
            low_shape(*d_up.shape[1:]),
        ],
        in_specs=[IN_VMEM] * 10,
        out_specs=[IN_VMEM, IN_VMEM, ANY, IN_VMEM, IN_VMEM, IN_VMEM],
        scratch_shapes=[
            low_vmem(4, rows, width),
            low_vmem(rows, width),
            *PlaneScatter.buffers(rows, width),
            low_vmem(4, rows, width),
            *PlaneScatter.buffers(rows, width),
            pltpu.VMEM((rows, width), jnp.float32),
            low_vmem(depth - 2, *d_down.shape[1:]),
            *net_scratch(2 * PlaneScatter.remotes + PlaneGather.remotes + depth, 1),
        ],
        compiler_params=comm_params(5),
        cost_estimate=lasts(95, 1 << 20),
    )(grad_hidden, w_up, activated, w_down, middle, own_cot, gain, bias, d_down, d_up)


def closing(depth, up_own, down_own, down_x, d_query, d_keyval, d_vec, d_out, grad_parts, own_tok, grad_middle, gain, block, chooser):
    rows, width = grad_parts.shape[1:]
    kv_rows, kv_cols = d_keyval.shape[1] // depth, d_keyval.shape[2]
    group = depth // 4
    slots = chooser.shape[0] // 4

    def add2(into, other):
        add_rows(into, other, 16)

    def add3(into, other):
        for at in range(2):
            add_rows(into.at[at], other.at[at], 16)

    def kernel(
        up, down, down_x_in, query, kv, vec, out, parts, tok, grad_mid, gain_row, block_own, choose,
        up_all, down_all, query_all, kv_all, vec_all, out_all, block_got, grad_got,
        query_lo, query_hi, kv_lo, kv_hi, vec_lo, vec_hi, out_lo, out_hi,
        out_mix, up_got, query_got, vec_got, first, grad_low, block_send, grad_send, kv_line, kv_wide,
        sums, diag, from_x, from_y, kv_sums, kv_diag, kv_from_x, kv_from_y, *sems,
    ):
        spot = Spot(depth)
        net = Net(*sems)
        z, y = spot.z, spot.y
        deal = DpExchange(net, spot, out, out_mix)

        def mixed(at):
            return out_mix.at[at // group, at % group]

        def kv_part(at):
            return kv_line.at[pl.ds(pl.multiple_of(at * kv_rows, kv_rows), kv_rows)]

        run_query = LineScatter(net, spot, lambda at: query.at[at], query_lo, query_hi, add3)
        run_kv = LineScatter(net, spot, kv_part, kv_lo, kv_hi, add2)
        run_vec = LineScatter(net, spot, lambda at: vec.at[at], vec_lo, vec_hi, add3)
        run_out = LineScatter(net, spot, mixed, out_lo, out_hi, add2)
        plane = PlaneScatter(net, spot, parts, sums, diag, from_x, from_y)
        kv_plane = PlaneScatter(net, spot, kv, kv_sums, kv_diag, kv_from_x, kv_from_y)
        y_up = net.remote(up.at[1 - y], up_got, spot.to_y)
        y_query = net.remote(query.at[z, 1 - y], query_got, spot.to_y)
        y_vec = net.remote(vec.at[z, 1 - y], vec_got, spot.to_y)
        dp_up = DpGather(net, spot, up.at[y], up_all.at[y])
        dp_up2 = DpGather(net, spot, up_got, up_all.at[1 - y])
        xc, on_x = spot.x * 2 + spot.c, (1 - spot.x) * 2 + spot.c
        keep_down = [
            net.local(down, down_all.at[xc]),
            net.local(down_x_in, down_all.at[on_x]),
        ]
        down_moves = [
            net.remote(down, down_all.at[xc], spot.to_c, down_all.at[spot.x * 2 + 1 - spot.c]),
            net.remote(
                down_x_in,
                down_all.at[on_x],
                spot.to_c,
                down_all.at[(1 - spot.x) * 2 + 1 - spot.c],
            ),
        ]
        dp_query = DpGather(net, spot, query.at[z, y], query_all.at[y])
        dp_query2 = DpGather(net, spot, query_got, query_all.at[1 - y])
        dp_kv = DpGather(net, spot, kv_part(z), kv_all)
        dp_vec = DpGather(net, spot, vec.at[z, y], vec_all)
        dp_out = DpGather(net, spot, mixed(z), out_all)
        back_block = DpExchange(net, spot, block_send, block_got)
        back_grad = DpExchange(net, spot, grad_send, grad_got)
        spot.barrier((spot.to_c, spot.to_x, spot.to_y, spot.to_xc), True)
        plane.start()
        kv_plane.start()
        run_query.stage(0)
        deal.start()
        y_up.start()
        kv_plane.middle()
        plane.middle()
        kv_plane.last()
        deal.got()
        run_out.stage(0)
        run_query.stage(1)
        kv_plane.finish(kv_wide)
        kv_line[...] = low(kv_wide[...])
        run_kv.stage(0)
        run_vec.stage(0)
        pick_rows(choose, block_own, block_send)
        plane.last()
        run_out.stage(1)
        run_kv.stage(1)
        run_vec.stage(1)
        for copy in (*down_moves, *keep_down):
            copy.start()
        plane.finish(first)

        @row_loop(rows)
        def _(at):
            xhat, scale = normalize(wide(tok[at, :]))
            grad = grad_mid[at, :] + norm_back(first[at, :], gain_row[...], xhat, scale)
            grad_low[at, :] = low(grad)

        pick_rows(choose, grad_low, grad_send)
        back_grad.start()
        for step in range(2, depth - 1):
            run_query.stage(step)
            run_out.stage(step)
            run_kv.stage(step)
            run_vec.stage(step)
        y_up.got()
        dp_up.start()
        dp_up2.start()
        run_query.total()
        y_query.start()
        dp_query.start()
        run_out.total()
        dp_out.start()
        run_kv.total()
        dp_kv.start()
        run_vec.total()
        y_vec.start()
        back_block.start()
        dp_up.last()
        dp_up2.last()
        y_query.got()
        dp_query2.start()
        y_vec.got()
        y_vec.sent()
        add_rows(vec.at[z, y], vec_got, 16)
        dp_vec.start()
        dps = (dp_query, dp_out, dp_kv, dp_query2, dp_vec)
        for run in dps:
            run.last()
        back_grad.got()
        back_block.got()
        for run in (dp_up, dp_up2, *dps, back_grad, back_block):
            run.finish()
        for copy in down_moves:
            copy.got()
            copy.sent()
        for copy in keep_down:
            copy.wait()
        for run in (run_query, run_kv, run_vec, run_out, deal):
            run.finish()
        for copy in (y_up, y_query):
            copy.sent()

    remotes = (
        3 * DpExchange.remotes
        + 4 * LineGather.remotes(depth)
        + 2 * PlaneScatter.remotes
        + 3
        + 8 * DpGather.remotes
    )
    one = depth - 1

    def twice(*dims):
        return [low_vmem(*dims)] * 2

    return pl.pallas_call(
        kernel,
        out_shape=[
            low_shape(2, 4, *up_own.shape[1:]),
            low_shape(4, *down_own.shape),
            low_shape(2, 4, *d_query.shape[2:]),
            low_shape(4, kv_rows, kv_cols),
            low_shape(4, *d_vec.shape[2:]),
            low_shape(4, *d_out.shape[2:]),
            low_shape(4, slots, width),
            low_shape(4, slots, width),
        ],
        in_specs=[IN_VMEM] * 13,
        out_specs=[ANY] * 8,
        scratch_shapes=[
            *twice(one, *d_query.shape[1:]),
            *twice(one, kv_rows, kv_cols),
            *twice(one, *d_vec.shape[1:]),
            *twice(one, *d_out.shape[2:]),
            low_vmem(*d_out.shape),
            low_vmem(*up_own.shape[1:]),
            low_vmem(*d_query.shape[2:]),
            low_vmem(*d_vec.shape[2:]),
            pltpu.VMEM((rows, width), jnp.float32),
            low_vmem(rows, width),
            low_vmem(4, slots, width),
            low_vmem(4, slots, width),
            low_vmem(depth * kv_rows, kv_cols),
            pltpu.VMEM((depth * kv_rows, kv_cols), jnp.float32),
            *PlaneScatter.buffers(rows, width),
            *PlaneScatter.buffers(depth * kv_rows, kv_cols),
            *net_scratch(remotes, 12),
        ],
        compiler_params=comm_params(2),
        cost_estimate=lasts(90, 1 << 20),
    )(
        up_own, down_own, down_x, d_query, d_keyval, d_vec, d_out, grad_parts, own_tok, grad_middle,
        gain, block, chooser,
    )


def spread_columns(blocks, depth, seg, y_slow):
    rows = blocks.shape[2]
    wide_seg = seg % 128 == 0
    if not wide_seg:
        parts = blocks.reshape(2, 4, rows, depth, seg)
        order = (2, 0, 3, 1, 4) if y_slow else (2, 3, 0, 1, 4)
        return wide(jnp.transpose(parts, order).reshape(rows, 8 * depth * seg))

    step = 32

    def kernel(block, out):
        for y in range(2):
            for z in range(depth):
                for xc in range(4):
                    owner = y * depth + z if y_slow else z * 2 + y
                    at = (owner * 4 + xc) * seg
                    out[:, at : at + seg] = wide(block[y, xc, :, z * seg : (z + 1) * seg])

    return pl.pallas_call(
        kernel,
        grid=(rows // step,),
        in_specs=[pl.BlockSpec((2, 4, step, depth * seg), lambda index: (0, 0, index, 0))],
        out_specs=pl.BlockSpec((step, 8 * depth * seg), lambda index: (index, 0)),
        out_shape=jax.ShapeDtypeStruct((rows, 8 * depth * seg), jnp.float32),
    )(blocks)


def build(mesh):
    fsdp_size = mesh.shape["fsdp"]
    depth = fsdp_size // 2
    y_slow = depth != 4
    owner_axes = ("y", "z") if y_slow else ("z", "y")

    def owner(z_at, y_at):
        return y_at * depth + z_at if y_slow else z_at * 2 + y_at

    def shards(
        tokens,
        cotangent,
        lengths,
        dealing,
        attn_gain,
        attn_shift,
        query_weight,
        query_bias,
        keyval_weight,
        value_bias,
        output_weight,
        output_bias,
        mlp_gain,
        mlp_shift,
        up_weight,
        up_bias,
        down_weight,
        down_bias,
    ):
        held, slot_len, width = tokens.shape
        my_z = lax.axis_index("z")
        my_y = lax.axis_index("y")
        my_xc = lax.axis_index("x") * 2 + lax.axis_index("c")
        member = my_y * 4 + my_xc
        rows_own = query_weight.shape[0]
        ff = up_weight.shape[1]
        ff_own = down_weight.shape[0]
        ff_seg = ff_own // 4
        out_seg = rows_own // 4
        head_cols = width // 8
        group_seqs = held * 4

        def plane_table(table):
            parts = [
                lax.dynamic_slice_in_dim(table, owner(my_z, y_at) * group_seqs, group_seqs)
                for y_at in range(2)
            ]
            return jnp.stack(parts)

        micro = 2 * 4 * MB
        dealt_here = (
            lax.dynamic_slice_in_dim(dealing, owner(my_z, my_y) * group_seqs, group_seqs)
            - owner(my_z, my_y) * group_seqs
        )
        holders = (dealt_here // held).reshape(4, held)
        slots = (dealt_here % held).reshape(4, held)
        slot_for = jnp.sum(jnp.where(holders == my_xc, slots, 0), axis=1)
        my_holders = lax.dynamic_index_in_dim(holders, my_xc, 0, keepdims=False)
        lens = plane_table(lengths).reshape(micro, SEATS)
        ends = jnp.concatenate([lens[:, :1], lens[:, :1] + lens[:, 1:]], axis=1)
        starts = ends - lens
        at = jnp.arange(PACK)
        inside = (at[None, :, None] >= starts[:, None, :]) & (at[None, :, None] < ends[:, None, :])
        row_valid = jnp.any(inside, axis=2)
        seat = jnp.sum(jnp.where(inside, jnp.arange(SEATS)[None, None, :], 0), axis=2)
        segment = jnp.where(row_valid, seat, -1)
        allowed = (
            (at[None, :, None] >= at[None, None, :])
            & (segment[:, :, None] == segment[:, None, :])
            & row_valid[:, None, :]
        )
        my_inside = lax.dynamic_slice_in_dim(inside, member * MB, MB)
        my_starts = lax.dynamic_slice_in_dim(starts, member * MB, MB)
        my_lens = lax.dynamic_slice_in_dim(lens, member * MB, MB).reshape(held)
        offset = at[None, :] - jnp.sum(jnp.where(my_inside, my_starts[:, None, :], 0), axis=2)
        from_dev = jnp.sum(
            jnp.where(my_inside, my_holders.reshape(MB, 1, SEATS), 0), axis=2
        )
        own_count = MB * PACK
        own_valid = jnp.any(my_inside, axis=2).reshape(own_count)[:, None]
        source_row = jnp.where(
            own_valid[:, 0], (from_dev * slot_len + offset).reshape(own_count), 0
        )

        def up_columns(y_at):
            cols = [
                lax.dynamic_slice_in_dim(
                    up_weight, owner(z_at, y_at) * ff_own + my_xc * ff_seg, ff_seg, axis=1
                )
                for z_at in range(depth)
            ]
            return low(jnp.concatenate(cols, axis=1))

        def head_base(y_at):
            return owner(my_xc * (depth // 4), y_at) * rows_own

        def query_columns(y_at):
            return low(lax.dynamic_slice_in_dim(query_weight, head_base(y_at), head_cols, axis=1))

        small_parts = [
            attn_gain,
            attn_shift,
            output_bias,
            mlp_gain,
            mlp_shift,
            down_bias,
            query_bias,
            up_bias,
            value_bias,
        ]
        small = low(lax.optimization_barrier(jnp.concatenate(small_parts)))
        small_count = small.shape[0]
        small = jnp.pad(small, (0, 16 * 256 - small_count)).reshape(16, 256)
        def dealt(array):
            return jnp.stack(
                [
                    lax.dynamic_index_in_dim(array, slot_for[index], 0, keepdims=False)
                    for index in range(4)
                ]
            )

        flat = held * slot_len
        chooser = low((source_row[:, None] == jnp.arange(flat)[None, :]) & own_valid)
        (
            own_low,
            own_cot,
            up_piece,
            down_piece,
            tokens_all,
            cotangent_all,
            query_all,
            keyval_all,
            small_all,
            out_dealt,
            up_all,
            down_all,
        ) = opening(
            depth,
            owner,
            dealt(tokens),
            dealt(cotangent),
            chooser,
            query_weight,
            keyval_weight,
            output_weight,
            down_weight,
            small,
            up_columns(my_y),
            up_columns(1 - my_y),
        )

        ring = [(index, (index + 1) % depth) for index in range(depth)]

        def ring_slot(buffer, piece, step):
            at = (my_z - step + depth) % depth
            return lax.dynamic_update_slice(
                buffer, piece[None], (at,) + (0,) * piece.ndim
            )

        for step in range(3, depth):
            down_piece = lax.ppermute(down_piece, "z", ring)
            down_all = ring_slot(down_all, down_piece, step)
        for step in range(1, depth - 2):
            up_piece = lax.ppermute(up_piece, "z", ring)
            up_all = ring_slot(up_all, up_piece, step)
        if y_slow:
            small_all = jnp.transpose(small_all, (1, 0, 2, 3))
        gathered_small = wide(small_all.reshape(fsdp_size, 16 * 256)[:, :small_count])
        sizes = [item.shape[0] for item in small_parts]
        begins = [sum(sizes[:index]) for index in range(len(sizes))]
        (
            gain_a,
            shift_a,
            bias_o,
            gain_m,
            shift_m,
            bias_d,
            bias_q,
            bias_u,
            bias_v,
        ) = [
            gathered_small[:, start : start + size].reshape(-1)
            for start, size in zip(begins, sizes)
        ]
        my_bias_q = lax.dynamic_slice_in_dim(bias_q, head_base(my_y), head_cols)
        my_bias_u = jnp.concatenate(
            [
                lax.dynamic_slice_in_dim(
                    bias_u, owner(z_at, my_y) * ff_own + my_xc * ff_seg, ff_seg
                )
                for z_at in range(depth)
            ]
        )
        bias_kv = jnp.concatenate([jnp.zeros((HEAD,), jnp.float32), bias_v])

        def rows_in_order(gathered):
            if y_slow:
                gathered = jnp.transpose(gathered, (1, 0, 2, 3))
            return gathered.reshape(width, gathered.shape[-1])

        def rows_by_z(values):
            if y_slow:
                return jnp.transpose(
                    values.reshape(2, depth, rows_own, values.shape[-1]), (1, 0, 2, 3)
                )
            return values.reshape(depth, 2, rows_own, values.shape[-1])

        w_query = rows_in_order(query_all)
        keyval_all = keyval_all.reshape(2, 4, depth, out_seg, 2 * HEAD)
        order = (0, 2, 1, 3, 4) if y_slow else (2, 0, 1, 3, 4)
        w_keyval = jnp.transpose(keyval_all, order).reshape(width, 2 * HEAD)
        w_output = jnp.transpose(out_dealt, (1, 0, 2, 3)).reshape(head_cols, width)

        packed = tokens_all.reshape(micro * PACK, width)
        grad_mixed = cotangent_all.reshape(micro * PACK, width)
        own_grad = wide(own_cot)

        xhat_all, _ = normalize(wide(packed))
        normed_attn = low(xhat_all * gain_a + shift_a)
        query = low(product(normed_attn, w_query) + my_bias_q)
        keyval = low(product(normed_attn, w_keyval) + bias_kv)
        my_heads = head_cols // HEAD
        query_h = query.reshape(micro, PACK, my_heads, HEAD)
        keys = keyval[:, :HEAD].reshape(micro, PACK, HEAD)
        vals = keyval[:, HEAD:].reshape(micro, PACK, HEAD)
        score_scale = 1.0 / math.sqrt(HEAD)
        scores = (
            jnp.einsum("mshd,mtd->mhst", query_h, keys, preferred_element_type=jnp.float32)
            * score_scale
        )
        scores = jnp.where(allowed[:, None], scores, -1e30)
        expscores = jnp.exp(scores - jnp.max(scores, axis=-1, keepdims=True))
        probs = expscores / jnp.sum(expscores, axis=-1, keepdims=True)
        attended = low(
            jnp.einsum(
                "mhst,mtd->mshd", low(probs), vals, preferred_element_type=jnp.float32
            ).reshape(micro * PACK, head_cols)
        )
        attended, down_piece = lax.optimization_barrier((attended, down_piece))
        middle, normed_mlp, up_hop_1, up_hop_2 = attention_out(
            depth,
            attended,
            w_output,
            own_low,
            bias_o[None],
            gain_m[None],
            shift_m[None],
            up_piece,
        )
        up_all = ring_slot(up_all, up_hop_1, depth - 2)
        up_all = ring_slot(up_all, up_hop_2, depth - 1)
        normed_mlp = normed_mlp.reshape(micro * PACK, width)
        w_down = down_all.reshape(depth * ff_seg, width)
        grad_act = product_cols(grad_mixed, w_down)
        w_up = rows_in_order(up_all)
        hidden = product(normed_mlp, w_up) + my_bias_u
        activated, slope = gelu_parts(hidden)
        activated = low(activated)
        grad_hidden = low(slope * grad_act)

        down_parts = low(product_rows(activated, grad_mixed)).reshape(depth, ff_seg, width)
        up_parts = rows_by_z(low(product_rows(normed_mlp, grad_hidden)))
        grad_normed, grad_middle, grad_branch, block_own, d_down, d_up = mlp_back(
            depth,
            grad_hidden,
            w_up,
            activated,
            w_down,
            middle,
            own_cot,
            gain_m[None],
            bias_d[None],
            down_parts,
            up_parts,
        )
        grad_branch = grad_branch.reshape(micro * PACK, width)
        down_x = lax.ppermute(d_down, "x", [(0, 1), (1, 0)])
        for step in range(2, depth):
            d_up = lax.ppermute(d_up, "z", ring)
            at = (my_z - 1 - step + 2 * depth) % depth
            term = lax.dynamic_index_in_dim(up_parts, at, 0, keepdims=False)
            d_up = low(wide(d_up) + wide(term))
        xhat_m, _ = normalize(middle)
        grad_branch_own = low(grad_middle)
        d_output = low(product_rows(attended, grad_branch))
        grad_att = low(product_cols(grad_branch, w_output)).reshape(micro, PACK, my_heads, HEAD)
        grad_probs = jnp.einsum("mshd,mtd->mhst", grad_att, vals, preferred_element_type=jnp.float32)
        grad_vals = jnp.einsum(
            "mhst,mshd->mtd", low(probs), grad_att, preferred_element_type=jnp.float32
        )
        inner = jnp.sum(probs * grad_probs, axis=-1, keepdims=True)
        grad_scores = low(probs * (grad_probs - inner))
        grad_query = (
            jnp.einsum("mhst,mtd->mshd", grad_scores, keys, preferred_element_type=jnp.float32)
            * score_scale
        )
        grad_query = low(grad_query.reshape(micro * PACK, head_cols))
        grad_keys = (
            jnp.einsum("mhst,mshd->mtd", grad_scores, query_h, preferred_element_type=jnp.float32)
            * score_scale
        )
        grad_keyval = low(jnp.concatenate([grad_keys, grad_vals], axis=2)).reshape(
            micro * PACK, 2 * HEAD
        )
        d_query = low(product_rows(normed_attn, grad_query))
        d_keyval = low(product_rows(normed_attn, grad_keyval))
        grad_input_part = product_cols(grad_query, w_query) + product_cols(grad_keyval, w_keyval)
        def colsum(values):
            return jnp.sum(wide(values), axis=0)

        def spread_vec(values, parts, size, full):
            out = jnp.zeros((full,), jnp.float32)
            for index, begin in enumerate(parts):
                out = lax.dynamic_update_slice(
                    out, values[index * size : (index + 1) * size], (begin,)
                )
            return out

        vec_query = spread_vec(colsum(grad_query), [head_base(my_y)], head_cols, width)
        vec_up = spread_vec(
            colsum(grad_hidden),
            [owner(z_at, my_y) * ff_own + my_xc * ff_seg for z_at in range(depth)],
            ff_seg,
            ff,
        )
        vectors = [
            jnp.sum(grad_input_part * xhat_all, axis=0),
            jnp.sum(grad_input_part, axis=0),
            colsum(grad_branch_own),
            jnp.sum(grad_normed * xhat_m, axis=0),
            jnp.sum(grad_normed, axis=0),
            jnp.sum(own_grad, axis=0),
            vec_query,
            vec_up,
            colsum(grad_keyval[:, HEAD:]),
        ]
        vectors = jnp.concatenate([item.reshape(fsdp_size, -1) for item in vectors], axis=1)
        vectors = jnp.pad(low(vectors), ((0, 0), (0, 16 * 256 - small_count)))
        if y_slow:
            d_vec = jnp.transpose(vectors.reshape(2, depth, 16, 256), (1, 0, 2, 3))
        else:
            d_vec = vectors.reshape(depth, 2, 16, 256)

        d_out_parts = jnp.transpose(
            d_output.reshape(depth // 4, 4, out_seg, width), (1, 0, 2, 3)
        )
        if y_slow:
            d_keyval = d_keyval.reshape(2, depth, 4, out_seg, 2 * HEAD)
            d_keyval = jnp.transpose(d_keyval, (0, 2, 1, 3, 4))
        else:
            d_keyval = d_keyval.reshape(depth, 2, 4, out_seg, 2 * HEAD)
            d_keyval = jnp.transpose(d_keyval, (1, 2, 0, 3, 4))
        d_keyval = d_keyval.reshape(8, depth * out_seg, 2 * HEAD)

        send_seq = jnp.argmax(my_holders[None, :] == jnp.arange(4)[:, None], axis=1)
        pos = jnp.arange(slot_len)
        live = pos[None, :] < my_lens[send_seq][:, None]
        seq_starts = (my_starts + jnp.arange(MB)[:, None] * PACK).reshape(held)
        send_rows = jnp.where(live, seq_starts[send_seq][:, None] + pos[None, :], -1)
        back_chooser = low(send_rows.reshape(flat)[:, None] == jnp.arange(own_count)[None, :])
        up_all, down_all, query_sum, kv_sum, vec_all, out_all, block_got, grad_got = closing(
            depth,
            d_up,
            d_down,
            down_x,
            rows_by_z(d_query),
            d_keyval,
            d_vec,
            d_out_parts,
            low(grad_input_part).reshape(8, own_count, width),
            own_low,
            grad_middle,
            gain_a[None],
            block_own,
            back_chooser,
        )
        from_dealt = jnp.argmax(slot_for[None, :] == jnp.arange(held)[:, None], axis=1)

        def held_order(got):
            return jnp.stack(
                [
                    lax.dynamic_index_in_dim(got, from_dealt[index], 0, keepdims=False)
                    for index in range(held)
                ]
            )

        up_grad = spread_columns(up_all, depth, ff_seg, y_slow)
        if y_slow:
            query_grad = jnp.transpose(query_sum, (2, 0, 1, 3))
        else:
            query_grad = jnp.transpose(query_sum, (2, 1, 0, 3))
        query_grad = wide(query_grad.reshape(rows_own, width))
        keyval_grad = wide(kv_sum.reshape(rows_own, 2 * HEAD))
        down_grad = wide(down_all.reshape(ff_own, width))
        output_grad = wide(out_all.reshape(rows_own, width))
        vec_own = jnp.sum(wide(vec_all), axis=0).reshape(16 * 256)
        (
            gain_a_grad,
            shift_a_grad,
            bias_o_grad,
            gain_m_grad,
            shift_m_grad,
            bias_d_grad,
            bias_q_grad,
            bias_u_grad,
            bias_v_grad,
        ) = [vec_own[start : start + size] for start, size in zip(begins, sizes)]

        return (
            held_order(block_got),
            held_order(grad_got),
            gain_a_grad,
            shift_a_grad,
            query_grad,
            bias_q_grad,
            keyval_grad,
            bias_v_grad,
            output_grad,
            bias_o_grad,
            gain_m_grad,
            shift_m_grad,
            up_grad,
            bias_u_grad,
            down_grad,
            bias_d_grad,
        )

    return shards, depth, owner_axes


def solution(mesh):
    shards, depth, owner_axes = build(mesh)
    sizes = {"z": depth, "y": 2}
    fine = Mesh(
        mesh.devices.reshape(sizes[owner_axes[0]], sizes[owner_axes[1]], 2, 2),
        owner_axes + ("x", "c"),
    )
    rows = P(owner_axes + ("x", "c"), None, None)
    vec = P(owner_axes)
    mat = P(owner_axes, None)
    in_specs = (
        rows, rows, P(), P(),
        vec, vec, mat, vec, mat, vec, mat, vec, vec, vec, mat, vec, mat, vec,
    )
    out_specs = (
        rows, rows,
        vec, vec, mat, vec, mat, vec, mat, vec, vec, vec, mat, vec, mat, vec,
    )
    return jax.shard_map(shards, mesh=fine, in_specs=in_specs, out_specs=out_specs, check_vma=False)
```

```python
import math

import jax
import jax.numpy as jnp
from jax import lax
from jax.experimental import pallas as pl
from jax.experimental.pallas import tpu as pltpu
from jax.sharding import Mesh
from jax.sharding import PartitionSpec as P

HEADS = 16
HEAD = 128
MB = 2
SEATS = 2
PACK = 80

epsilon = 1e-05
gelu_scale = 0.7978845608028654
gelu_cubic = 0.044715

DP = ("x", "c")


def low(values):
    return values.astype(jnp.bfloat16)


def wide(values):
    return values.astype(jnp.float32)


def product(left_mat, right_mat):
    return jnp.dot(left_mat, right_mat, preferred_element_type=jnp.float32)


def product_rows(left_mat, right_mat):
    return lax.dot_general(
        left_mat, right_mat, (((0,), (0,)), ((), ())), preferred_element_type=jnp.float32
    )


def product_cols(left_mat, right_mat):
    return lax.dot_general(
        left_mat, right_mat, (((1,), (1,)), ((), ())), preferred_element_type=jnp.float32
    )


def normalize(rows):
    center = rows - jnp.mean(rows, axis=-1, keepdims=True)
    spread = jnp.mean(center * center, axis=-1, keepdims=True)
    scale = lax.rsqrt(spread + epsilon)
    return center * scale, scale


def norm_back(grad_normed, gain, xhat, scale):
    g = grad_normed * gain
    inner = jnp.mean(g * xhat, axis=-1, keepdims=True)
    return scale * (g - jnp.mean(g, axis=-1, keepdims=True) - xhat * inner)


def gelu_parts(values):
    inner = jnp.tanh(gelu_scale * (values + gelu_cubic * values * values * values))
    activated = 0.5 * values * (1.0 + inner)
    slope = 0.5 * (1.0 + inner) + 0.5 * values * (1.0 - inner * inner) * gelu_scale * (
        1.0 + 3.0 * gelu_cubic * values * values
    )
    return activated, slope


MESH_ID = pl.DeviceIdType.MESH
VMEM_LIMIT = 56 * 1024 * 1024


class Spot:
    def __init__(self, depth):
        self.depth = depth
        self.z = lax.axis_index("z")
        self.y = lax.axis_index("y")
        self.x = lax.axis_index("x")
        self.c = lax.axis_index("c")
        self.to_c = {"c": 1 - self.c}
        self.to_x = {"x": 1 - self.x}
        self.to_y = {"y": 1 - self.y}
        self.to_xc = {"x": 1 - self.x, "c": 1 - self.c}
        self.up = {"z": self.z + 1}
        self.down = {"z": self.z - 1}

    def ring(self):
        before = {"z": lax.rem(self.z + self.depth - 1, self.depth)}
        return ({"z": lax.rem(self.z + 1, self.depth)}, before)

    def barrier(self, plane, line):
        bar = pltpu.get_barrier_semaphore()
        for to in plane:
            pl.semaphore_signal(bar, inc=1, device_id=to, device_id_type=MESH_ID)
        if line:

            @pl.when(self.z > 0)
            def _():
                pl.semaphore_signal(bar, inc=1, device_id=self.down, device_id_type=MESH_ID)

            @pl.when(self.z < self.depth - 1)
            def _():
                pl.semaphore_signal(bar, inc=1, device_id=self.up, device_id_type=MESH_ID)

        count = len(plane)
        if line:
            lower = jnp.where(self.z > 0, 1, 0)
            upper = jnp.where(self.z < self.depth - 1, 1, 0)
            count = count + lower + upper
        pl.semaphore_wait(bar, count)


class Net:
    def __init__(self, send_sems, recv_sems, local_sems):
        self.send_sems = send_sems
        self.recv_sems = recv_sems
        self.local_sems = local_sems
        self.count = 0
        self.local_count = 0
        self.open = []

    def remote(self, src, dst, to, arrives=None):
        copy = Copy(self, self.count, src, dst, to, arrives)
        self.count += 1
        return copy

    def local(self, src, dst):
        copy = pltpu.make_async_copy(src, dst, self.local_sems.at[self.local_count])
        self.local_count += 1
        return copy


class Copy:
    def __init__(self, net, index, src, dst, to, arrives):
        def make(target):
            return pltpu.make_async_remote_copy(
                src_ref=src,
                dst_ref=target,
                send_sem=net.send_sems.at[index],
                recv_sem=net.recv_sems.at[index],
                device_id=to,
                device_id_type=MESH_ID,
            )

        self.out = make(dst)
        self.into = make(dst if arrives is None else arrives)

    def start(self):
        self.out.start()

    def got(self):
        self.into.wait_recv()

    def sent(self):
        self.out.wait_send()


class PlaneGather:
    def __init__(self, net, spot, own, slots, share=2):
        def at(y, x, c):
            return y * 4 + x * 2 + c

        y, x, c = spot.y, spot.x, spot.c
        self.both = share == 2
        half = own.shape[0] // share
        lo, hi = pl.ds(0, half), pl.ds(half * (share - 1), half)
        me = at(y, x, c)
        on_x, on_y, on_d = at(y, 1 - x, c), at(1 - y, x, c), at(1 - y, 1 - x, c)
        peer = [at(y, x, 1 - c), at(y, 1 - x, 1 - c), at(1 - y, x, 1 - c), at(1 - y, 1 - x, 1 - c)]

        def slot(index):
            return slots.at[index]

        self.keep = net.local(own, slot(me))
        self.x = net.remote(own, slot(me), spot.to_x, slot(on_x))
        self.y = net.remote(own, slot(me), spot.to_y, slot(on_y))
        self.c = net.remote(own, slot(me), spot.to_c, slot(peer[0]))
        self.x_on_y = net.remote(
            slots.at[on_x, lo], slots.at[on_x, lo], spot.to_y, slots.at[on_d, lo]
        )
        self.x_on_c = net.remote(slot(on_x), slot(on_x), spot.to_c, slot(peer[1]))
        self.y_on_c = net.remote(slot(on_y), slot(on_y), spot.to_c, slot(peer[2]))
        self.lo_on_c = net.remote(
            slots.at[on_d, lo], slots.at[on_d, lo], spot.to_c, slots.at[peer[3], lo]
        )
        if self.both:
            self.y_on_x = net.remote(
                slots.at[on_y, hi], slots.at[on_y, hi], spot.to_x, slots.at[on_d, hi]
            )
            self.hi_on_c = net.remote(
                slots.at[on_d, hi], slots.at[on_d, hi], spot.to_c, slots.at[peer[3], hi]
            )

    def start(self):
        self.x.start()
        self.y.start()
        self.c.start()
        self.keep.start()

    def middle(self):
        self.x.got()
        self.x_on_y.start()
        self.x_on_c.start()
        self.y.got()
        if self.both:
            self.y_on_x.start()
        self.y_on_c.start()

    def last(self):
        self.x_on_y.got()
        self.lo_on_c.start()
        if self.both:
            self.y_on_x.got()
            self.hi_on_c.start()

    def finish(self):
        second = (self.y_on_x, self.hi_on_c) if self.both else ()
        for copy in (self.c, self.x_on_c, self.y_on_c, self.lo_on_c, *second[1:]):
            copy.got()
        firsts = (self.x, self.y, self.c, self.x_on_y, self.x_on_c, self.y_on_c, self.lo_on_c)
        for copy in (*firsts, *second):
            copy.sent()
        self.keep.wait()

    remotes = 9
    locals = 1


def add_rows(into, other, step=32):
    rows = into.shape[0]

    @pl.loop(0, rows // step)
    def _(index):
        at = pl.ds(pl.multiple_of(index * step, step), step)
        into[at, :] = low(wide(into[at, :]) + wide(other[at, :]))


class PlaneScatter:
    remotes = 10

    @staticmethod
    def buffers(rows, width):
        return [
            pltpu.VMEM((4, rows, width), jnp.bfloat16),
            pltpu.VMEM((rows, width), jnp.bfloat16),
            pltpu.VMEM((rows, width), jnp.bfloat16),
            pltpu.VMEM((rows, width), jnp.bfloat16),
        ]

    def __init__(self, net, spot, parts, sums, diag, from_x, from_y):
        y, x, c = spot.y, spot.x, spot.c
        half = parts.shape[1] // 2
        lo, hi = pl.ds(0, half), pl.ds(half, half)
        self.own, self.nx, self.ny, self.nd = (
            y * 2 + x,
            y * 2 + 1 - x,
            (1 - y) * 2 + x,
            (1 - y) * 2 + 1 - x,
        )
        self.parts, self.sums, self.diag = parts, sums, diag
        self.stacked = parts.shape[0] == 4
        self.from_x, self.from_y, self.c = from_x, from_y, c
        self.lo, self.hi = lo, hi
        self.first = {
            key: net.remote(
                parts.at[at] if self.stacked else parts.at[at * 2 + 1 - c], sums.at[at], spot.to_c
            )
            for key, at in (("d", self.nd), ("x", self.nx), ("y", self.ny), ("o", self.own))
        }
        self.d_lo = net.remote(sums.at[self.nd, lo], diag.at[lo], spot.to_x)
        self.d_hi = net.remote(sums.at[self.nd, hi], diag.at[hi], spot.to_y)
        self.x_lo = net.remote(sums.at[self.nx, lo], from_x.at[lo], spot.to_x)
        self.y_hi = net.remote(sums.at[self.ny, hi], from_y.at[hi], spot.to_y)
        self.x_hi = net.remote(sums.at[self.nx, hi], from_x.at[hi], spot.to_x)
        self.y_lo = net.remote(sums.at[self.ny, lo], from_y.at[lo], spot.to_y)

    def start(self):
        for copy in self.first.values():
            copy.start()

    def pair(self, key, at):
        self.first[key].got()
        if self.stacked:
            self.compute(at * 2 + self.c, at)
        else:
            add_rows(self.sums.at[at], self.parts.at[at * 2 + self.c])

    def middle(self):
        self.pair("d", self.nd)
        self.d_lo.start()
        self.d_hi.start()
        self.pair("x", self.nx)
        self.x_lo.start()
        self.pair("y", self.ny)
        self.y_hi.start()
        self.pair("o", self.own)

    def last(self):
        self.d_lo.got()
        add_rows(self.sums.at[self.ny, self.lo], self.diag.at[self.lo], 16)
        self.y_lo.start()
        self.d_hi.got()
        add_rows(self.sums.at[self.nx, self.hi], self.diag.at[self.hi], 16)
        self.x_hi.start()

    def finish(self, result):
        for copy in (self.x_lo, self.y_hi, self.x_hi, self.y_lo):
            copy.got()

        @pl.loop(0, result.shape[0] // 16)
        def _(index):
            at = pl.ds(pl.multiple_of(index * 16, 16), 16)
            result[at, :] = (
                wide(self.sums[self.own, at, :]) + wide(self.from_x[at, :]) + wide(self.from_y[at, :])
            )

        for copy in (
            *self.first.values(),
            self.d_lo,
            self.d_hi,
            self.x_lo,
            self.x_hi,
            self.y_lo,
            self.y_hi,
        ):
            copy.sent()


class LineGather:
    def __init__(self, net, spot, slots, moves=None):
        self.spot, depth, z = spot, spot.depth, spot.z
        self.moves = moves
        self.hops = []
        for step in range(depth - 1):
            lower = jnp.maximum(z - step, 0)
            upper = jnp.minimum(z + step, depth - 1)
            from_low = jnp.maximum(z - 1 - step, 0)
            from_high = jnp.minimum(z + 1 + step, depth - 1)
            self.hops.append(
                (
                    net.remote(slots(lower), slots(lower), spot.up, slots(from_low)),
                    net.remote(slots(upper), slots(upper), spot.down, slots(from_high)),
                )
            )

    @staticmethod
    def remotes(depth):
        return 2 * (depth - 1)

    def pick(self, cond, slot):
        return cond if self.moves is None else cond & self.moves(slot)

    def sends(self, step):
        z, last = self.spot.z, self.spot.depth - 1
        return (
            (self.pick((z >= step) & (z < last), z - step), self.hops[step][0]),
            (self.pick((z + step <= last) & (z > 0), z + step), self.hops[step][1]),
        )

    def takes(self, step):
        z, last = self.spot.z, self.spot.depth - 1
        return (
            (self.pick(z >= step + 1, z - 1 - step), self.hops[step][0]),
            (self.pick(z + step + 1 <= last, z + 1 + step), self.hops[step][1]),
        )

    def start(self, step):
        for cond, copy in self.sends(step):
            pl.when(cond)(copy.start)

    def got(self, step):
        for cond, copy in self.takes(step):
            pl.when(cond)(copy.got)

    def hop(self, step):
        for (came, old), (goes, new) in zip(self.takes(step - 1), self.sends(step)):
            pl.when(came)(old.got)
            pl.when(goes)(new.start)

    def finish(self):
        for step in range(self.spot.depth - 1):
            for cond, copy in self.sends(step):
                pl.when(cond)(copy.sent)


class LineScatter:
    def __init__(self, net, spot, parts, from_low, from_high, add):
        self.spot, depth, z = spot, spot.depth, spot.z
        self.parts, self.from_low, self.from_high, self.add = parts, from_low, from_high, add
        self.ups, self.downs = [], []
        for step in range(depth - 1):
            self.ups.append(net.remote(parts(depth - 1 - step), from_low.at[step], spot.up))
            self.downs.append(net.remote(parts(step), from_high.at[step], spot.down))

    remotes = LineGather.remotes

    def stage(self, step):
        z, last = self.spot.z, self.spot.depth - 1
        up_to, down_to = last - step, step

        @pl.when((z > 0) & (z < up_to))
        def _():
            self.ups[step].got()
            self.add(self.parts(up_to), self.from_low.at[step])

        @pl.when(z < up_to)
        def _():
            self.ups[step].start()

        @pl.when((z < last) & (z > down_to))
        def _():
            self.downs[step].got()
            self.add(self.parts(down_to), self.from_high.at[step])

        @pl.when(z > down_to)
        def _():
            self.downs[step].start()

    def total(self):
        z, last = self.spot.z, self.spot.depth - 1
        for step in range(last):

            @pl.when((z > 0) & (z == last - step))
            def _():
                self.ups[step].got()
                self.add(self.parts(last - step), self.from_low.at[step])

            @pl.when((z < last) & (z == step))
            def _():
                self.downs[step].got()
                self.add(self.parts(step), self.from_high.at[step])

    def finish(self):
        z, last = self.spot.z, self.spot.depth - 1
        for step in range(last):
            pl.when(z < last - step)(self.ups[step].sent)
            pl.when(z > step)(self.downs[step].sent)


class DpGather:
    remotes = 3

    def __init__(self, net, spot, own, slots):
        me = spot.x * 2 + spot.c
        on_x = (1 - spot.x) * 2 + spot.c
        self.keep = net.local(own, slots.at[me])
        self.x = net.remote(own, slots.at[me], spot.to_x, slots.at[on_x])
        self.c = net.remote(own, slots.at[me], spot.to_c, slots.at[spot.x * 2 + 1 - spot.c])
        self.x_on_c = net.remote(
            slots.at[on_x],
            slots.at[on_x],
            spot.to_c,
            slots.at[(1 - spot.x) * 2 + 1 - spot.c],
        )

    def start(self):
        self.x.start()
        self.c.start()
        self.keep.start()

    def last(self):
        self.x.got()
        self.x_on_c.start()

    def finish(self):
        self.c.got()
        self.x_on_c.got()
        for copy in (self.x, self.c, self.x_on_c):
            copy.sent()
        self.keep.wait()


class DpExchange:
    remotes = 3

    def __init__(self, net, spot, parts, slots):
        me = spot.x * 2 + spot.c
        on_x = (1 - spot.x) * 2 + spot.c
        on_c = spot.x * 2 + 1 - spot.c
        on_xc = (1 - spot.x) * 2 + 1 - spot.c
        self.keep = net.local(parts.at[me], slots.at[me])
        self.moves = [
            net.remote(parts.at[at], slots.at[me], to, slots.at[at])
            for at, to in ((on_xc, spot.to_xc), (on_x, spot.to_x), (on_c, spot.to_c))
        ]

    def start(self):
        for copy in self.moves:
            copy.start()
        self.keep.start()

    def got(self):
        for copy in self.moves:
            copy.got()
        self.keep.wait()

    def finish(self):
        for copy in self.moves:
            copy.sent()


def net_scratch(remotes, locals_):
    return [
        pltpu.SemaphoreType.DMA((remotes,)),
        pltpu.SemaphoreType.DMA((remotes,)),
        pltpu.SemaphoreType.DMA((max(locals_, 1),)),
    ]


ANY = pl.BlockSpec(memory_space=pl.ANY)
IN_VMEM = pl.BlockSpec(memory_space=pltpu.VMEM)


def lasts(micros, moved):
    return pl.CostEstimate(
        flops=int(micros * 1e9), bytes_accessed=int(moved), transcendentals=0
    )


def comm_params(collective_id):
    return pltpu.CompilerParams(
        collective_id=collective_id, has_side_effects=True, vmem_limit_bytes=VMEM_LIMIT
    )


def low_shape(*dims):
    return jax.ShapeDtypeStruct(dims, jnp.bfloat16)


def wide_shape(*dims):
    return jax.ShapeDtypeStruct(dims, jnp.float32)


def low_vmem(*dims):
    return pltpu.VMEM(dims, jnp.bfloat16)


def pick_rows(chooser, source, result, step=512):
    width = result.shape[-1]

    @pl.loop(0, width // step)
    def _(index):
        at = pl.ds(pl.multiple_of(index * step, step), step)
        rows = source[..., at].reshape(chooser.shape[1], step)
        result[..., at] = low(product(chooser[...], rows)).reshape(*result.shape[:-1], step)


def opening(depth, owner, tokens, cotangent, sender, chooser, query_weight, keyval_weight, output_weight, small, up_mine, up_other):
    rows = chooser.shape[0]
    width = tokens.shape[-1]
    group = depth // 4
    rows_own = query_weight.shape[0]
    head_cols = width // 8
    kv_rows = rows_own // 4
    kv_cols = keyval_weight.shape[1]

    def kernel(
        tok_held, cot_held, send, choose, query_w, kv_w, out_w, small_m, up_m, up_o,
        own_tok, own_cot, up_own,
        tok_all, query_all, kv_all, small_all, out_all,
        tok, cot, tok_got, cot_got, out_v, kv_line, query_m, query_o, query_y, small_y,
        query_f, out_f, kv_f, *sems,
    ):
        spot = Spot(depth)
        net = Net(*sems)
        z, y = spot.z, spot.y
        xc = spot.x * 2 + spot.c
        source = z // group == xc

        def head_base(y_at):
            return pl.multiple_of(owner(xc * group, y_at) * rows_own, 128)

        def strip(ref, size):
            return ref.at[pl.ds(pl.multiple_of(xc * size, size), size)]

        def z_slot(at):
            return kv_line.at[pl.ds(pl.multiple_of(at * kv_rows, kv_rows), kv_rows)]

        read_query_o = net.local(query_w.at[:, pl.ds(head_base(1 - y), head_cols)], query_f.at[0])
        read_out = net.local(out_w, out_f)
        read_kv = net.local(strip(kv_w, kv_rows), kv_f)
        read_query = net.local(query_w.at[:, pl.ds(head_base(y), head_cols)], query_f.at[1])
        tok_deal = DpExchange(net, spot, tok, tok_got)
        cot_deal = DpExchange(net, spot, cot, cot_got)
        tok_run = PlaneGather(net, spot, own_tok, tok_all)
        kv_run = PlaneGather(net, spot, kv_line, kv_all)
        y_query = net.remote(query_o, query_y, spot.to_y)
        y_small = net.remote(small_m, small_y, spot.to_y)
        y_up = net.remote(up_o, up_own.at[y], spot.to_y, up_own.at[1 - y])
        keep_small = net.local(small_m, small_all.at[z, y])
        keep_query = net.local(query_m, query_all.at[z, y])
        keep_query_y = net.local(query_y, query_all.at[z, 1 - y])
        keep_small_y = net.local(small_y, small_all.at[z, 1 - y])
        keep_out = net.local(out_v, out_all)
        run_kv = LineGather(net, spot, z_slot)
        run_query = LineGather(net, spot, lambda at: query_all.at[at])
        run_small = LineGather(net, spot, lambda at: small_all.at[at])

        def piece_of_out(piece):
            rows_at = pl.ds(piece * kv_rows, kv_rows)
            return LineGather(
                net,
                spot,
                lambda at: out_v.at[at % group, rows_at],
                lambda at: at // group == xc,
            )

        run_outs = [piece_of_out(piece) for piece in range(4)]
        read_query_o.start()
        pl.when(source)(read_out.start)
        read_kv.start()
        read_query.start()
        keep_small.start()
        spot.barrier((spot.to_c, spot.to_x, spot.to_y, spot.to_xc), True)
        pick_rows(send, tok_held, tok)
        tok_deal.start()
        read_query_o.wait()
        query_o[...] = low(query_f[0])
        y_query.start()
        y_small.start()
        y_up.start()

        @pl.when(source)
        def _():
            read_out.wait()

            @pl.loop(0, rows_own // 16)
            def _(index):
                at = pl.ds(pl.multiple_of(index * 16, 16), 16)
                out_v[z % group, at, :] = low(out_f[at, :])

        for run in run_outs:
            run.start(0)
        read_kv.wait()
        z_slot(z)[...] = low(kv_f[...])
        run_kv.start(0)
        read_query.wait()
        query_m[...] = low(query_f[1])
        keep_query.start()
        keep_query.wait()
        keep_small.wait()
        y_query.got()
        keep_query_y.start()
        y_small.got()
        keep_small_y.start()
        keep_query_y.wait()
        keep_small_y.wait()
        run_query.start(0)
        run_small.start(0)
        pick_rows(send, cot_held, cot)

        @pl.loop(0, rows_own // 16)
        def _(index):
            at = pl.ds(pl.multiple_of(index * 16, 16), 16)
            up_own[y, at, :] = up_m[at, :]

        tok_deal.got()
        pick_rows(choose, tok_got, own_tok)
        tok_run.start()
        cot_deal.start()
        for step in range(1, depth - 1):
            for run in run_outs:
                run.hop(step)
            run_kv.hop(step)
        run_query.hop(1)
        run_small.hop(1)
        run_kv.got(depth - 2)
        kv_run.start()
        for step in range(2, depth - 1):
            run_query.hop(step)
            run_small.hop(step)
        tok_run.middle()
        kv_run.middle()
        cot_deal.got()
        pick_rows(choose, cot_got, own_cot)
        tok_run.last()
        kv_run.last()
        for run in run_outs:
            run.got(depth - 2)
        keep_out.start()
        run_query.got(depth - 2)
        run_small.got(depth - 2)
        y_up.got()
        runs = (*run_outs, run_kv, run_query, run_small, tok_run, kv_run)
        for run in (*runs, tok_deal, cot_deal):
            run.finish()
        for copy in (y_query, y_small, y_up):
            copy.sent()
        keep_out.wait()

    remotes = (
        2 * DpExchange.remotes + 2 * PlaneGather.remotes + 4 + 7 * LineGather.remotes(depth)
    )
    operands = (
        tokens, cotangent, sender, chooser, query_weight, keyval_weight, output_weight, small,
        up_mine, up_other,
    )
    wide_type = jnp.float32
    return pl.pallas_call(
        kernel,
        out_shape=[
            low_shape(rows, width),
            low_shape(rows, width),
            low_shape(2, *up_mine.shape),
            low_shape(8, rows, width),
            low_shape(depth, 2, rows_own, head_cols),
            low_shape(8, depth * kv_rows, kv_cols),
            low_shape(depth, 2, *small.shape),
            low_shape(group, rows_own, width),
        ],
        in_specs=[IN_VMEM] * 4 + [ANY] * 3 + [IN_VMEM] * 3,
        out_specs=[IN_VMEM] * 3 + [ANY] * 5,
        scratch_shapes=[
            *[low_vmem(*tokens.shape)] * 4,
            low_vmem(group, rows_own, width),
            low_vmem(depth * kv_rows, kv_cols),
            low_vmem(rows_own, head_cols),
            low_vmem(rows_own, head_cols),
            low_vmem(rows_own, head_cols),
            low_vmem(*small.shape),
            pltpu.VMEM((2, rows_own, head_cols), wide_type),
            pltpu.VMEM((rows_own, width), wide_type),
            pltpu.VMEM((kv_rows, kv_cols), wide_type),
            *net_scratch(remotes, 20),
        ],
        compiler_params=comm_params(1),
        cost_estimate=lasts(75, 1 << 20),
    )(*operands)


ROWS_STEP = 32


def row_loop(count):
    def decorate(body):
        @pl.loop(0, count // ROWS_STEP)
        def _(index):
            body(pl.ds(pl.multiple_of(index * ROWS_STEP, ROWS_STEP), ROWS_STEP))

    return decorate


def feed_blocks(run, c, parts, block, prepare=None):
    width = parts.shape[-1]

    def columns(body):
        @pl.loop(0, width // 512)
        def _(index):
            body(pl.ds(pl.multiple_of(index * 512, 512), 512))

    def send(at, member):
        if prepare is not None:
            prepare(member)

        @columns
        def _(cols):
            parts[at, :, cols] = low(block(member, cols))

    def merge(member, at):
        if prepare is not None:
            prepare(member)

        @columns
        def _(cols):
            run.sums[at, :, cols] = low(wide(run.sums[at, :, cols]) + block(member, cols))

    run.compute = merge
    for key, at in (("d", run.nd), ("x", run.nx), ("y", run.ny), ("o", run.own)):
        send(at, at * 2 + 1 - c)
        run.first[key].start()


SCORE_SCALE = 1.0 / math.sqrt(HEAD)


def stacked(values):
    return jnp.concatenate([values[:, :HEAD], values[:, HEAD:]], axis=0)


def unstacked(values):
    half = values.shape[0] // 2
    return jnp.concatenate([values[:half], values[half:]], axis=1)


def softmax_of(query_2, keys, allowed):
    scores = product_cols(query_2, keys) * SCORE_SCALE
    scores = jnp.where(jnp.concatenate([allowed, allowed], axis=0) > 0.0, scores, -1e30)
    exps = jnp.exp(scores - jnp.max(scores, axis=-1, keepdims=True))
    return exps / jnp.sum(exps, axis=-1, keepdims=True)


def attend(depth, tok_all, own_tok, own_cot, w_query, w_keyval, w_output, gain_a, shift_a, bias_q, bias_kv, allowed, bias, gain, shift, up_own, down_own, down_1):
    rows, width = own_tok.shape
    total = 8 * rows
    head_cols = w_query.shape[1]
    micros = rows // PACK

    def kernel(
        tok_far, tok, cot, w_q, w_kv, w_out, gain_1, shift_1, b_q, b_kv, allow, bias_row, gain_row, shift_row,
        up, down, down_b,
        middle, normed_a, query, keyval, attended, normed_all, cot_all, up_all, down_all, down_2,
        parts, normed, sums, diag, from_x, from_y, *sems,
    ):
        spot = Spot(depth)
        net = Net(*sems)
        z = spot.z
        run = PlaneScatter(net, spot, parts, sums, diag, from_x, from_y)
        gather = PlaneGather(net, spot, normed, normed_all)
        cot_run = PlaneGather(net, spot, cot, cot_all, share=1)
        after, _ = spot.ring()

        def behind(step):
            return lax.rem(z + 2 * depth - step, depth)

        keeps = [
            net.local(up, up_all.at[z]),
            net.local(down, down_all.at[z]),
            net.local(down_b, down_all.at[behind(1)]),
        ]
        keep_2 = net.local(down_2, down_all.at[behind(2)])
        ups = [net.remote(up, up_all.at[z], after, up_all.at[behind(1)])]
        for step in range(2, depth):
            at = up_all.at[behind(step - 1)]
            ups.append(net.remote(at, at, after, up_all.at[behind(step)]))
        down_hop = net.remote(down_b, down_2, after)

        def one_member(member):
            first = pl.multiple_of(member * rows, rows)

            @pl.loop(0, rows // ROWS_STEP)
            def _(index):
                at = pl.multiple_of(index * ROWS_STEP, ROWS_STEP)
                xhat, _ = normalize(wide(tok_far[member, pl.ds(at, ROWS_STEP), :]))
                normed_a[pl.ds(first + at, ROWS_STEP), :] = low(xhat * gain_1[...] + shift_1[...])

            rows_at = pl.ds(first, rows)
            query[rows_at, :] = low(product(normed_a[rows_at, :], w_q[...]) + b_q[...])
            keyval[rows_at, :] = low(product(normed_a[rows_at, :], w_kv[...]) + b_kv[...])

            for index in range(micros):
                at = pl.ds(pl.multiple_of(first + index * PACK, PACK), PACK)
                pair = keyval[at, :]
                probs = softmax_of(
                    stacked(query[at, :]), pair[:, :HEAD], allow[member * micros + index]
                )
                attended[at, :] = low(unstacked(product(low(probs), pair[:, HEAD:])))

        def block(member, cols):
            rows_at = pl.ds(pl.multiple_of(member * rows, rows), rows)
            return product(attended[rows_at, :], w_out[:, cols])

        for copy in keeps:
            copy.start()
        spot.barrier((spot.to_c, spot.to_x, spot.to_y, *spot.ring()), False)
        ups[0].start()
        cot_run.start()
        feed_blocks(run, spot.c, parts, block, one_member)
        down_hop.start()
        cot_run.middle()
        run.middle()
        ups[0].got()
        ups[1].start()
        run.last()
        cot_run.last()
        run.finish(middle)

        @row_loop(rows)
        def _(at):
            total_rows = wide(tok[at, :]) + (middle[at, :] + bias_row[...])
            middle[at, :] = total_rows
            xhat, _ = normalize(total_rows)
            normed[at, :] = low(xhat * gain_row[...] + shift_row[...])

        gather.start()
        down_hop.got()
        keep_2.start()
        for step in range(2, depth - 1):
            ups[step - 1].got()
            ups[step].start()
        gather.middle()
        gather.last()
        gather.finish()
        cot_run.finish()
        ups[-1].got()
        for copy in (*ups, down_hop):
            copy.sent()
        for copy in (*keeps, keep_2):
            copy.wait()

    return pl.pallas_call(
        kernel,
        out_shape=[
            wide_shape(rows, width),
            low_shape(total, width),
            low_shape(total, head_cols),
            low_shape(total, 2 * HEAD),
            low_shape(total, head_cols),
            low_shape(8, rows, width),
            low_shape(8, rows, width),
            low_shape(depth, *up_own.shape),
            low_shape(depth, *down_own.shape),
            low_shape(*down_own.shape),
        ],
        in_specs=[IN_VMEM] * 17,
        out_specs=[IN_VMEM] * 5 + [ANY] * 4 + [IN_VMEM],
        scratch_shapes=[
            low_vmem(4, rows, width),
            low_vmem(rows, width),
            *PlaneScatter.buffers(rows, width),
            *net_scratch(PlaneScatter.remotes + 2 * PlaneGather.remotes + depth, 6),
        ],
        compiler_params=comm_params(3),
        cost_estimate=lasts(90, 1 << 20),
    )(
        tok_all, own_tok, own_cot, w_query, w_keyval, w_output, gain_a, shift_a, bias_q, bias_kv,
        allowed, bias, gain, shift, up_own, down_own, down_1,
    )


def attend_back(depth, branch_all, query, keyval, allowed, w_output, w_query, w_keyval, own_tok, grad_middle, gain, block, chooser, holder, d_out, up_sum, up_parts):
    group = depth // 4
    rows, width = own_tok.shape
    total, head_cols = query.shape
    micros = rows // PACK
    slots = chooser.shape[0] // 4

    def kernel(
        branch, q_all, kv_all, allow, w_out, w_q, w_kv, tok, grad_mid, gain_row, block_own, choose, hold,
        out, du, du_far,
        grad_q, kv_rows_all, vec, block_res, grad_res, out_sum, du_sum,
        parts, sums, diag, from_x, from_y, first, grad_low, block_send, grad_send, block_got, grad_got,
        out_mix, out_lo, out_hi, du_term,
        grad_kv, kv_sums, kv_diag, kv_from_x, kv_from_y, kv_wide, kv_own, *sems,
    ):
        spot = Spot(depth)
        net = Net(*sems)
        run = PlaneScatter(net, spot, parts, sums, diag, from_x, from_y)
        z = spot.z
        after, _ = spot.ring()
        deal = DpExchange(net, spot, out, out_mix)

        def mixed(at):
            return out_mix.at[at // group, at % group]

        def add2(into, other):
            add_rows(into, other, 16)

        kv_run = PlaneScatter(net, spot, grad_kv, kv_sums, kv_diag, kv_from_x, kv_from_y)
        kv_gather = PlaneGather(net, spot, kv_own, kv_rows_all)
        run_out = LineScatter(net, spot, mixed, out_lo, out_hi, add2)
        up_hop = net.remote(du, du_sum, after)
        up_term = net.local(du_far.at[z], du_term)
        back_block = DpExchange(net, spot, block_send, block_got)
        back_grad = DpExchange(net, spot, grad_send, grad_got)

        def one_member(member):
            begin = pl.multiple_of(member * rows, rows)
            grad_att = low(product_cols(branch[member], w_out[...]))
            for index in range(micros):
                at = pl.ds(pl.multiple_of(begin + index * PACK, PACK), PACK)
                pair = kv_all[at, :]
                keys, vals = pair[:, :HEAD], pair[:, HEAD:]
                q_2 = stacked(q_all[at, :])
                g_2 = stacked(grad_att[index * PACK : (index + 1) * PACK])
                probs = softmax_of(q_2, keys, allow[member * micros + index])
                grad_probs = product_cols(g_2, vals)
                inner = jnp.sum(probs * grad_probs, axis=-1, keepdims=True)
                grad_scores = low(probs * (grad_probs - inner))
                grad_q[at, :] = low(unstacked(product(grad_scores, keys) * SCORE_SCALE))
                grad_k = product_rows(grad_scores, q_2) * SCORE_SCALE
                grad_v = product_rows(low(probs), g_2)
                grad_kv[member, index * PACK : (index + 1) * PACK, :] = low(
                    jnp.concatenate([grad_k, grad_v], axis=1)
                )

        def block_of(member, cols):
            rows_at = pl.ds(pl.multiple_of(member * rows, rows), rows)
            return product_cols(grad_q[rows_at, :], w_q[cols, :]) + product_cols(
                grad_kv[member], w_kv[cols, :]
            )

        up_term.start()
        spot.barrier((spot.to_c, spot.to_x, spot.to_y, spot.to_xc, *spot.ring()), False)
        deal.start()
        up_hop.start()
        pick_rows(choose, block_own, block_send)
        back_block.start()
        feed_blocks(run, spot.c, parts, block_of, one_member)
        deal.got()
        run_out.stage(0)
        kv_run.start()
        run.middle()
        kv_run.middle()
        for step in range(1, depth - 1):
            run_out.stage(step)
        run.last()
        kv_run.last()
        run.finish(first)
        kv_run.finish(kv_wide)
        kv_own[...] = low(kv_wide[...])
        kv_gather.start()
        vec[...] = jnp.zeros_like(vec)

        @row_loop(rows)
        def _(at):
            xhat, scale = normalize(wide(tok[at, :]))
            grad = grad_mid[at, :] + norm_back(first[at, :], gain_row[...], xhat, scale)
            grad_low[at, :] = low(grad)
            vec[0:1, :] += jnp.sum(first[at, :] * xhat, axis=0, keepdims=True)
            vec[1:2, :] += jnp.sum(first[at, :], axis=0, keepdims=True)

        pick_rows(choose, grad_low, grad_send)
        back_grad.start()
        kv_gather.middle()
        run_out.total()
        out_sum[...] = mixed(z)[...]
        kv_gather.last()
        back_block.got()
        pick_rows(hold, block_got, block_res)
        up_hop.got()
        up_term.wait()
        for at in range(2):
            add_rows(du_sum.at[at], du_term.at[at], 32)
        back_grad.got()
        pick_rows(hold, grad_got, grad_res)
        for run_done in (back_block, back_grad, deal, run_out):
            run_done.finish()
        kv_gather.finish()
        up_hop.sent()

    return pl.pallas_call(
        kernel,
        out_shape=[
            low_shape(total, head_cols),
            low_shape(8, rows, 2 * HEAD),
            wide_shape(8, width),
            low_shape(4, slots, width),
            low_shape(4, slots, width),
            low_shape(*d_out.shape[2:]),
            low_shape(*up_sum.shape),
        ],
        in_specs=[IN_VMEM] * 15 + [ANY],
        out_specs=[IN_VMEM, ANY] + [IN_VMEM] * 5,
        scratch_shapes=[
            low_vmem(4, rows, width),
            *PlaneScatter.buffers(rows, width),
            pltpu.VMEM((rows, width), jnp.float32),
            low_vmem(rows, width),
            *[low_vmem(4, slots, width)] * 4,
            low_vmem(*d_out.shape),
            *[low_vmem(depth - 1, *d_out.shape[2:])] * 2,
            low_vmem(*up_sum.shape),
            low_vmem(8, rows, 2 * HEAD),
            *PlaneScatter.buffers(rows, 2 * HEAD),
            pltpu.VMEM((rows, 2 * HEAD), jnp.float32),
            low_vmem(rows, 2 * HEAD),
            *net_scratch(
                2 * PlaneScatter.remotes + PlaneGather.remotes + 3 * DpExchange.remotes + LineGather.remotes(depth) + 1, 6
            ),
        ],
        compiler_params=comm_params(4),
        cost_estimate=lasts(70, 1 << 20),
    )(
        branch_all, query, keyval, allowed, w_output, w_query, w_keyval, own_tok, grad_middle, gain,
        block, chooser, holder, d_out, up_sum, up_parts,
    )


def mlp_back(depth, grad_hidden, w_up, activated, w_down, middle, own_cot, gain, bias, down_first, d_down, d_up):
    rows, width = own_cot.shape
    up_hops = min(2, depth - 1)

    def kernel(gh, up, act_far, down_far, mid, cot, gain_row, bias_row, dd_first, dd, du,
               vec, grad_middle, branch_all, block_out, dd_sum, du_sum, dd_x,
               parts, branch, sums, diag, from_x, from_y,
               parts2, sums2, diag2, from_x2, from_y2, mlp_sum, act, down,
               dd_got, du_got, dd_term, du_term, grad_normed, *sems):
        spot = Spot(depth)
        net = Net(*sems)
        z = spot.z
        run = PlaneScatter(net, spot, parts, sums, diag, from_x, from_y)
        run2 = PlaneScatter(net, spot, parts2, sums2, diag2, from_x2, from_y2)
        gather = PlaneGather(net, spot, branch, branch_all)
        after, _ = spot.ring()

        def slot(step):
            return lax.rem(z + 2 * depth - 1 - step, depth)

        def down_at(step):
            return dd_sum if step == depth - 1 else dd_got.at[step - 1]

        def up_at(step):
            return du_sum if step == up_hops else du_got.at[step - 1]

        down_terms = [
            net.local(dd.at[slot(step)], dd_term.at[step - 1]) for step in range(1, depth)
        ]
        up_terms = [
            net.local(du.at[slot(step)], du_term.at[step - 1]) for step in range(1, up_hops + 1)
        ]
        loads = [net.local(act_far, act), net.local(down_far, down)]
        down_hops = [
            net.remote(down_at(step - 1), down_at(step), after) for step in range(2, depth)
        ]
        ups = [net.remote(du.at[slot(0)], up_at(1), after)]
        ups += [net.remote(up_at(step - 1), up_at(step), after) for step in range(2, up_hops + 1)]

        down_over = net.remote(dd_sum, dd_x, spot.to_x)

        def down_step(step):
            down_hops[step - 2].got()
            down_terms[step - 1].wait()
            add_rows(down_at(step), dd_term.at[step - 1], 32)
            if step < depth - 1:
                down_hops[step - 1].start()
            else:
                down_over.start()

        def up_step(step):
            ups[step - 1].got()
            up_terms[step - 1].wait()
            for at in range(2):
                add_rows(up_at(step).at[at], du_term.at[step - 1, at], 32)
            if step < up_hops:
                ups[step].start()

        def block(member, cols):
            rows_at = pl.ds(pl.multiple_of(member * rows, rows), rows)
            return product_cols(gh[rows_at, :], up[cols, :])

        def block2(member, cols):
            rows_at = pl.ds(pl.multiple_of(member * rows, rows), rows)
            return product(act[rows_at, :], down[:, cols])

        for copy in (*down_terms, *up_terms, *loads):
            copy.start()
        spot.barrier((spot.to_c, spot.to_x, spot.to_y, *spot.ring()), False)
        down_terms[0].wait()

        @pl.loop(0, dd_first.shape[0] // 32)
        def _(index):
            at = pl.ds(pl.multiple_of(index * 32, 32), 32)
            dd_got[0, at, :] = low(wide(dd_first[at, :]) + wide(dd_term[0, at, :]))

        down_hops[0].start()
        feed_blocks(run, spot.c, parts, block)
        run.middle()
        for copy in loads:
            copy.wait()
        feed_blocks(run2, spot.c, parts2, block2)
        run.last()
        down_step(2)
        ups[0].start()
        run.finish(grad_normed)
        vec[...] = jnp.zeros_like(vec)

        @row_loop(rows)
        def _(at):
            xhat, scale = normalize(mid[at, :])
            grad_n = grad_normed[at, :]
            grad_o = wide(cot[at, :])
            grad = grad_o + norm_back(grad_n, gain_row[...], xhat, scale)
            grad_b = low(grad)
            grad_middle[at, :] = grad
            branch[at, :] = grad_b
            for row, values in enumerate((wide(grad_b), grad_n * xhat, grad_n, grad_o)):
                vec[row : row + 1, :] += jnp.sum(values, axis=0, keepdims=True)

        gather.start()
        for step in range(3, depth):
            if step < depth - 1:
                down_step(step)
        gather.middle()
        run2.middle()
        gather.last()
        down_step(depth - 1)
        up_step(1)
        run2.last()
        gather.finish()
        run2.finish(mlp_sum)

        @row_loop(rows)
        def _(at):
            block_out[at, :] = low(mid[at, :] + (mlp_sum[at, :] + bias_row[...]))

        for step in range(2, up_hops + 1):
            up_step(step)
        down_over.got()
        for copy in (*down_hops, *ups, down_over):
            copy.sent()

    return pl.pallas_call(
        kernel,
        out_shape=[
            wide_shape(8, width),
            wide_shape(rows, width),
            low_shape(8, rows, width),
            low_shape(rows, width),
            low_shape(*d_down.shape[1:]),
            low_shape(*d_up.shape[1:]),
            low_shape(*d_down.shape[1:]),
        ],
        in_specs=[IN_VMEM] * 2 + [ANY] * 2 + [IN_VMEM] * 5 + [ANY] * 2,
        out_specs=[IN_VMEM, IN_VMEM, ANY, IN_VMEM, IN_VMEM, IN_VMEM, IN_VMEM],
        scratch_shapes=[
            low_vmem(4, rows, width),
            low_vmem(rows, width),
            *PlaneScatter.buffers(rows, width),
            low_vmem(4, rows, width),
            *PlaneScatter.buffers(rows, width),
            pltpu.VMEM((rows, width), jnp.float32),
            low_vmem(*activated.shape),
            low_vmem(*w_down.shape),
            low_vmem(depth - 2, *d_down.shape[1:]),
            low_vmem(max(up_hops - 1, 1), *d_up.shape[1:]),
            low_vmem(depth - 1, *d_down.shape[1:]),
            low_vmem(up_hops, *d_up.shape[1:]),
            pltpu.VMEM((rows, width), jnp.float32),
            *net_scratch(
                2 * PlaneScatter.remotes + PlaneGather.remotes + depth + up_hops + 1,
                depth + up_hops + 3,
            ),
        ],
        compiler_params=comm_params(5),
        cost_estimate=lasts(95, 1 << 20),
    )(
        grad_hidden, w_up, activated, w_down, middle, own_cot, gain, bias, down_first, d_down, d_up
    )


def closing(depth, up_own, down_own, down_x, d_query, d_keyval, d_vec, out_own):
    kv_rows, kv_cols = d_keyval.shape[0] // depth, d_keyval.shape[1]

    def add2(into, other):
        add_rows(into, other, 16)

    def add3(into, other):
        for at in range(2):
            add_rows(into.at[at], other.at[at], 16)

    def kernel(
        up, down, down_x_in, query, kv, vec, out,
        up_all, down_all, query_all, kv_all, vec_all, out_all,
        query_lo, query_hi, kv_lo, kv_hi, vec_lo, vec_hi,
        up_got, query_got, vec_got, *sems,
    ):
        spot = Spot(depth)
        net = Net(*sems)
        z, y = spot.z, spot.y
        xc, on_x = spot.x * 2 + spot.c, (1 - spot.x) * 2 + spot.c
        def kv_part(at):
            return kv.at[pl.ds(pl.multiple_of(at * kv_rows, kv_rows), kv_rows)]

        run_query = LineScatter(net, spot, lambda at: query.at[at], query_lo, query_hi, add3)
        run_kv = LineScatter(net, spot, kv_part, kv_lo, kv_hi, add2)
        run_vec = LineScatter(net, spot, lambda at: vec.at[at], vec_lo, vec_hi, add3)
        y_up = net.remote(up.at[1 - y], up_got, spot.to_y)
        y_query = net.remote(query.at[z, 1 - y], query_got, spot.to_y)
        y_vec = net.remote(vec.at[z, 1 - y], vec_got, spot.to_y)
        dp_up = DpGather(net, spot, up.at[y], up_all.at[y])
        dp_up2 = DpGather(net, spot, up_got, up_all.at[1 - y])
        dp_query = DpGather(net, spot, query.at[z, y], query_all.at[y])
        dp_query2 = DpGather(net, spot, query_got, query_all.at[1 - y])
        dp_kv = DpGather(net, spot, kv_part(z), kv_all)
        dp_vec = DpGather(net, spot, vec.at[z, y], vec_all)
        dp_out = DpGather(net, spot, out, out_all)
        keep_down = [
            net.local(down, down_all.at[xc]),
            net.local(down_x_in, down_all.at[on_x]),
        ]
        down_moves = [
            net.remote(down, down_all.at[xc], spot.to_c, down_all.at[spot.x * 2 + 1 - spot.c]),
            net.remote(
                down_x_in,
                down_all.at[on_x],
                spot.to_c,
                down_all.at[(1 - spot.x) * 2 + 1 - spot.c],
            ),
        ]
        spot.barrier((spot.to_c, spot.to_x, spot.to_y), True)
        run_query.stage(0)
        run_vec.stage(0)
        run_kv.stage(0)
        y_up.start()
        dp_up.start()
        dp_out.start()
        for copy in (*down_moves, *keep_down):
            copy.start()
        for step in range(1, depth - 1):
            run_query.stage(step)
            run_vec.stage(step)
            run_kv.stage(step)
            if step == 1:
                y_up.got()
                dp_up2.start()
        run_query.total()
        y_query.start()
        dp_query.start()
        run_vec.total()
        y_vec.start()
        run_kv.total()
        dp_kv.start()
        dp_up.last()
        y_query.got()
        dp_query2.start()
        y_vec.got()
        y_vec.sent()
        add_rows(vec.at[z, y], vec_got, 16)
        dp_vec.start()
        dp_up2.last()
        dps = (dp_query, dp_out, dp_kv, dp_query2, dp_vec)
        for run in dps:
            run.last()
        for run in (dp_up, dp_up2, *dps):
            run.finish()
        for copy in down_moves:
            copy.got()
            copy.sent()
        for copy in keep_down:
            copy.wait()
        for run in (run_query, run_kv, run_vec):
            run.finish()
        for copy in (y_up, y_query):
            copy.sent()

    remotes = (
        3 * LineGather.remotes(depth)
        + 5
        + 7 * DpGather.remotes
    )
    one = depth - 1

    def twice(*dims):
        return [low_vmem(*dims)] * 2

    return pl.pallas_call(
        kernel,
        out_shape=[
            low_shape(2, 4, *up_own.shape[1:]),
            low_shape(4, *down_own.shape),
            low_shape(2, 4, *d_query.shape[2:]),
            low_shape(4, kv_rows, kv_cols),
            low_shape(4, *d_vec.shape[2:]),
            low_shape(4, *out_own.shape),
        ],
        in_specs=[IN_VMEM] * 7,
        out_specs=[ANY] * 6,
        scratch_shapes=[
            *twice(one, *d_query.shape[1:]),
            *twice(one, kv_rows, kv_cols),
            *twice(one, *d_vec.shape[1:]),
            low_vmem(*up_own.shape[1:]),
            low_vmem(*d_query.shape[2:]),
            low_vmem(*d_vec.shape[2:]),
            *net_scratch(remotes, 10),
        ],
        compiler_params=comm_params(2),
        cost_estimate=lasts(70, 1 << 20),
    )(up_own, down_own, down_x, d_query, d_keyval, d_vec, out_own)


def widen(depth, y_slow, up_all, query_all, down_all, out_all, kv_all):
    rows = up_all.shape[2]
    seg = up_all.shape[3] // depth
    head_cols = query_all.shape[3]
    down_rows, width = down_all.shape
    steps = rows // 16

    def kernel(up, query, down, out, kv, up_w, query_w, down_w, out_w, kv_w):
        for y in range(2):
            for xc in range(4):
                for z in range(depth):
                    owner = y * depth + z if y_slow else z * 2 + y
                    at = (owner * 4 + xc) * seg
                    up_w[:, at : at + seg] = wide(up[y, xc, :, z * seg : (z + 1) * seg])
                at = (y * 4 + xc if y_slow else xc * 2 + y) * head_cols
                query_w[:, at : at + head_cols] = wide(query[y, xc])
        down_w[...] = wide(down[...])
        out_w[...] = wide(out[...])
        kv_w[...] = wide(kv[...])

    def rows_of(array):
        return pl.BlockSpec((array.shape[0] // steps, array.shape[1]), lambda index: (index, 0))

    def blocks_of(array):
        return pl.BlockSpec((2, 4, 16, array.shape[3]), lambda index: (0, 0, index, 0))

    shapes = [
        wide_shape(rows, 8 * depth * seg),
        wide_shape(rows, width),
        wide_shape(down_rows, width),
        wide_shape(*out_all.shape),
        wide_shape(*kv_all.shape),
    ]
    return pl.pallas_call(
        kernel,
        grid=(steps,),
        in_specs=[
            blocks_of(up_all),
            blocks_of(query_all),
            rows_of(down_all),
            rows_of(out_all),
            rows_of(kv_all),
        ],
        out_specs=[rows_of(item) for item in shapes],
        out_shape=shapes,
        compiler_params=pltpu.CompilerParams(vmem_limit_bytes=VMEM_LIMIT),
    )(up_all, query_all, down_all, out_all, kv_all)


def build(mesh):
    fsdp_size = mesh.shape["fsdp"]
    depth = fsdp_size // 2
    y_slow = depth != 4
    owner_axes = ("y", "z") if y_slow else ("z", "y")

    def owner(z_at, y_at):
        return y_at * depth + z_at if y_slow else z_at * 2 + y_at

    def shards(
        tokens,
        cotangent,
        lengths,
        dealing,
        attn_gain,
        attn_shift,
        query_weight,
        query_bias,
        keyval_weight,
        value_bias,
        output_weight,
        output_bias,
        mlp_gain,
        mlp_shift,
        up_weight,
        up_bias,
        down_weight,
        down_bias,
    ):
        held, slot_len, width = tokens.shape
        my_z = lax.axis_index("z")
        my_y = lax.axis_index("y")
        my_xc = lax.axis_index("x") * 2 + lax.axis_index("c")
        member = my_y * 4 + my_xc
        rows_own = query_weight.shape[0]
        ff = up_weight.shape[1]
        ff_own = down_weight.shape[0]
        ff_seg = ff_own // 4
        out_seg = rows_own // 4
        head_cols = width // 8
        group_seqs = held * 4

        def plane_table(table):
            parts = [
                lax.dynamic_slice_in_dim(table, owner(my_z, y_at) * group_seqs, group_seqs)
                for y_at in range(2)
            ]
            return jnp.stack(parts)

        micro = 2 * 4 * MB
        dealt_here = (
            lax.dynamic_slice_in_dim(dealing, owner(my_z, my_y) * group_seqs, group_seqs)
            - owner(my_z, my_y) * group_seqs
        )
        holders = (dealt_here // held).reshape(4, held)
        slots = (dealt_here % held).reshape(4, held)
        slot_for = jnp.sum(jnp.where(holders == my_xc, slots, 0), axis=1)
        my_holders = lax.dynamic_index_in_dim(holders, my_xc, 0, keepdims=False)
        lens = plane_table(lengths).reshape(micro, SEATS)
        ends = jnp.concatenate([lens[:, :1], lens[:, :1] + lens[:, 1:]], axis=1)
        starts = ends - lens
        at = jnp.arange(PACK)
        inside = (at[None, :, None] >= starts[:, None, :]) & (at[None, :, None] < ends[:, None, :])
        row_valid = jnp.any(inside, axis=2)
        seat = jnp.sum(jnp.where(inside, jnp.arange(SEATS)[None, None, :], 0), axis=2)
        segment = jnp.where(row_valid, seat, -1)
        allowed = (
            (at[None, :, None] >= at[None, None, :])
            & (segment[:, :, None] == segment[:, None, :])
            & row_valid[:, None, :]
        )
        my_inside = lax.dynamic_slice_in_dim(inside, member * MB, MB)
        my_starts = lax.dynamic_slice_in_dim(starts, member * MB, MB)
        my_lens = lax.dynamic_slice_in_dim(lens, member * MB, MB).reshape(held)
        offset = at[None, :] - jnp.sum(jnp.where(my_inside, my_starts[:, None, :], 0), axis=2)
        from_dev = jnp.sum(
            jnp.where(my_inside, my_holders.reshape(MB, 1, SEATS), 0), axis=2
        )
        own_count = MB * PACK
        own_valid = jnp.any(my_inside, axis=2).reshape(own_count)[:, None]
        source_row = jnp.where(
            own_valid[:, 0], (from_dev * slot_len + offset).reshape(own_count), 0
        )

        def up_columns(y_at):
            cols = [
                lax.dynamic_slice_in_dim(
                    up_weight, owner(z_at, y_at) * ff_own + my_xc * ff_seg, ff_seg, axis=1
                )
                for z_at in range(depth)
            ]
            return low(jnp.concatenate(cols, axis=1))

        def head_base(y_at):
            return owner(my_xc * (depth // 4), y_at) * rows_own

        def query_columns(y_at):
            return low(lax.dynamic_slice_in_dim(query_weight, head_base(y_at), head_cols, axis=1))

        small_parts = [
            attn_gain,
            attn_shift,
            output_bias,
            mlp_gain,
            mlp_shift,
            down_bias,
            query_bias,
            up_bias,
            value_bias,
        ]
        small = low(lax.optimization_barrier(jnp.concatenate(small_parts)))
        small_count = small.shape[0]
        small = jnp.pad(small, (0, 16 * 256 - small_count)).reshape(16, 256)
        down_own = low(lax.dynamic_slice_in_dim(down_weight, my_xc * ff_seg, ff_seg, axis=0))
        ring = [(index, (index + 1) % depth) for index in range(depth)]

        def ring_slot(buffer, piece, step):
            at = (my_z - step + depth) % depth
            return lax.dynamic_update_slice(
                buffer, piece[None], (at,) + (0,) * piece.ndim
            )

        down_hop_1 = lax.ppermute(down_own, "z", ring)
        flat = held * slot_len
        places = jnp.arange(flat)
        from_slot = jnp.repeat(slot_for, slot_len) * slot_len + places % slot_len
        sender = low(from_slot[:, None] == places[None, :])
        holder = low(places[:, None] == from_slot[None, :])
        chooser = low((source_row[:, None] == jnp.arange(flat)[None, :]) & own_valid)
        (
            own_low,
            own_cot,
            up_piece,
            tokens_all,
            query_all,
            keyval_all,
            small_all,
            w_output,
        ) = opening(
            depth,
            owner,
            tokens,
            cotangent,
            sender,
            chooser,
            query_weight,
            keyval_weight,
            output_weight,
            small,
            up_columns(my_y),
            up_columns(1 - my_y),
        )
        w_output = w_output.reshape(head_cols, width)

        if y_slow:
            small_all = jnp.transpose(small_all, (1, 0, 2, 3))
        gathered_small = wide(small_all.reshape(fsdp_size, 16 * 256)[:, :small_count])
        sizes = [item.shape[0] for item in small_parts]
        begins = [sum(sizes[:index]) for index in range(len(sizes))]
        (
            gain_a,
            shift_a,
            bias_o,
            gain_m,
            shift_m,
            bias_d,
            bias_q,
            bias_u,
            bias_v,
        ) = [
            gathered_small[:, start : start + size].reshape(-1)
            for start, size in zip(begins, sizes)
        ]
        my_bias_q = lax.dynamic_slice_in_dim(bias_q, head_base(my_y), head_cols)
        my_bias_u = jnp.concatenate(
            [
                lax.dynamic_slice_in_dim(
                    bias_u, owner(z_at, my_y) * ff_own + my_xc * ff_seg, ff_seg
                )
                for z_at in range(depth)
            ]
        )
        bias_kv = jnp.concatenate([jnp.zeros((HEAD,), jnp.float32), bias_v])

        def rows_in_order(gathered):
            if y_slow:
                gathered = jnp.transpose(gathered, (1, 0, 2, 3))
            return gathered.reshape(width, gathered.shape[-1])

        def rows_by_z(values):
            if y_slow:
                return jnp.transpose(
                    values.reshape(2, depth, rows_own, values.shape[-1]), (1, 0, 2, 3)
                )
            return values.reshape(depth, 2, rows_own, values.shape[-1])

        w_query = rows_in_order(query_all)
        keyval_all = keyval_all.reshape(2, 4, depth, out_seg, 2 * HEAD)
        order = (0, 2, 1, 3, 4) if y_slow else (2, 0, 1, 3, 4)
        w_keyval = jnp.transpose(keyval_all, order).reshape(width, 2 * HEAD)
        (
            middle,
            normed_attn,
            query,
            keyval,
            attended,
            normed_mlp,
            cotangent_all,
            up_all,
            down_all,
            down_piece,
        ) = attend(
            depth,
            tokens_all,
            own_low,
            own_cot,
            w_query,
            w_keyval,
            w_output,
            gain_a[None],
            shift_a[None],
            my_bias_q[None],
            bias_kv[None],
            wide(allowed),
            bias_o[None],
            gain_m[None],
            shift_m[None],
            up_piece,
            down_own,
            down_hop_1,
        )
        normed_mlp = normed_mlp.reshape(micro * PACK, width)
        grad_mixed = cotangent_all.reshape(micro * PACK, width)
        for step in range(3, depth):
            down_piece = lax.ppermute(down_piece, "z", ring)
            down_all = ring_slot(down_all, down_piece, step)
        w_up = rows_in_order(up_all)
        hidden = product(normed_mlp, w_up) + my_bias_u
        activated, slope = gelu_parts(hidden)
        activated = low(activated)

        down_parts = low(product_rows(activated, grad_mixed)).reshape(depth, ff_seg, width)
        down_first = lax.ppermute(
            lax.dynamic_index_in_dim(down_parts, (my_z + depth - 1) % depth, 0, keepdims=False),
            "z",
            ring,
        )
        mixed_later, down_parts = lax.optimization_barrier((grad_mixed, down_parts))
        w_down = down_all.reshape(depth * ff_seg, width)
        grad_act = product_cols(mixed_later, w_down)
        grad_hidden = low(slope * grad_act)
        up_parts = rows_by_z(low(product_rows(normed_mlp, grad_hidden)))
        second_sums, grad_middle, grad_branch, block_own, d_down, d_up, down_x = mlp_back(
            depth,
            grad_hidden,
            w_up,
            activated,
            w_down,
            middle,
            own_cot,
            gain_m[None],
            bias_d[None],
            down_first,
            down_parts,
            up_parts,
        )
        grad_flat = grad_branch.reshape(micro * PACK, width)
        for step in range(3, depth - 1):
            d_up = lax.ppermute(d_up, "z", ring)
            at = (my_z - 1 - step + 2 * depth) % depth
            term = lax.dynamic_index_in_dim(up_parts, at, 0, keepdims=False)
            d_up = low(wide(d_up) + wide(term))
        d_output = low(product_rows(attended, grad_flat))
        hits = my_holders[None, :] == jnp.arange(4)[:, None]
        seq_starts = (my_starts + jnp.arange(MB)[:, None] * PACK).reshape(held)
        send_lens = jnp.sum(jnp.where(hits, my_lens[None, :], 0), axis=1)
        send_starts = jnp.sum(jnp.where(hits, seq_starts[None, :], 0), axis=1)
        pos = jnp.arange(slot_len)
        live = pos[None, :] < send_lens[:, None]
        send_rows = jnp.where(live, send_starts[:, None] + pos[None, :], -1)
        back_chooser = low(send_rows.reshape(flat)[:, None] == jnp.arange(own_count)[None, :])
        d_out_parts = jnp.transpose(
            d_output.reshape(depth // 4, 4, out_seg, width), (1, 0, 2, 3)
        )
        grad_query, grad_keyval, first_sums, block_out, input_grad, out_own, d_up = attend_back(
            depth,
            grad_branch,
            query,
            keyval,
            wide(allowed),
            w_output,
            w_query,
            w_keyval,
            own_low,
            grad_middle,
            gain_a[None],
            block_own,
            back_chooser,
            holder,
            d_out_parts,
            d_up,
            up_parts,
        )
        d_query = low(product_rows(normed_attn, grad_query))
        grad_keyval = grad_keyval.reshape(micro * PACK, 2 * HEAD)
        d_keyval = low(product_rows(normed_attn, grad_keyval))
        own_keyval = lax.dynamic_slice_in_dim(grad_keyval, member * own_count, own_count)

        def colsum(values):
            return jnp.sum(wide(values), axis=0)

        def spread_vec(values, parts, size, full):
            out = jnp.zeros((full,), jnp.float32)
            for index, begin in enumerate(parts):
                out = lax.dynamic_update_slice(
                    out, values[index * size : (index + 1) * size], (begin,)
                )
            return out

        vec_query = spread_vec(colsum(grad_query), [head_base(my_y)], head_cols, width)
        vec_up = spread_vec(
            colsum(grad_hidden),
            [owner(z_at, my_y) * ff_own + my_xc * ff_seg for z_at in range(depth)],
            ff_seg,
            ff,
        )
        vectors = [
            first_sums[0],
            first_sums[1],
            second_sums[0],
            second_sums[1],
            second_sums[2],
            second_sums[3],
            vec_query,
            vec_up,
            colsum(own_keyval[:, HEAD:]),
        ]
        vectors = jnp.concatenate([item.reshape(fsdp_size, -1) for item in vectors], axis=1)
        vectors = jnp.pad(low(vectors), ((0, 0), (0, 16 * 256 - small_count)))
        if y_slow:
            d_vec = jnp.transpose(vectors.reshape(2, depth, 16, 256), (1, 0, 2, 3))
        else:
            d_vec = vectors.reshape(depth, 2, 16, 256)

        if y_slow:
            d_keyval = d_keyval.reshape(2, depth, 4, out_seg, 2 * HEAD)
            d_keyval = lax.dynamic_index_in_dim(d_keyval, my_y, 0, keepdims=False)
        else:
            d_keyval = d_keyval.reshape(depth, 2, 4, out_seg, 2 * HEAD)
            d_keyval = lax.dynamic_index_in_dim(d_keyval, my_y, 1, keepdims=False)
        d_keyval = lax.dynamic_index_in_dim(d_keyval, my_xc, 1, keepdims=False)
        d_keyval = d_keyval.reshape(depth * out_seg, 2 * HEAD)
        up_all, down_all, query_sum, kv_sum, vec_all, out_all = closing(
            depth, d_up, d_down, down_x, rows_by_z(d_query), d_keyval, d_vec, out_own
        )
        up_grad, query_grad, down_grad, output_grad, keyval_grad = widen(
            depth,
            y_slow,
            up_all,
            query_sum,
            down_all.reshape(ff_own, width),
            out_all.reshape(rows_own, width),
            kv_sum.reshape(rows_own, 2 * HEAD),
        )
        vec_own = jnp.sum(wide(vec_all), axis=0).reshape(16 * 256)
        (
            gain_a_grad,
            shift_a_grad,
            bias_o_grad,
            gain_m_grad,
            shift_m_grad,
            bias_d_grad,
            bias_q_grad,
            bias_u_grad,
            bias_v_grad,
        ) = [vec_own[start : start + size] for start, size in zip(begins, sizes)]

        return (
            block_out,
            input_grad,
            gain_a_grad,
            shift_a_grad,
            query_grad,
            bias_q_grad,
            keyval_grad,
            bias_v_grad,
            output_grad,
            bias_o_grad,
            gain_m_grad,
            shift_m_grad,
            up_grad,
            bias_u_grad,
            down_grad,
            bias_d_grad,
        )

    return shards, depth, owner_axes


def solution(mesh):
    shards, depth, owner_axes = build(mesh)
    sizes = {"z": depth, "y": 2}
    fine = Mesh(
        mesh.devices.reshape(sizes[owner_axes[0]], sizes[owner_axes[1]], 2, 2),
        owner_axes + ("x", "c"),
    )
    rows = P(owner_axes + ("x", "c"), None, None)
    vec = P(owner_axes)
    mat = P(owner_axes, None)
    in_specs = (
        rows, rows, P(), P(),
        vec, vec, mat, vec, mat, vec, mat, vec, vec, vec, mat, vec, mat, vec,
    )
    out_specs = (
        rows, rows,
        vec, vec, mat, vec, mat, vec, mat, vec, vec, vec, mat, vec, mat, vec,
    )
    return jax.shard_map(shards, mesh=fine, in_specs=in_specs, out_specs=out_specs, check_vma=False)
```

```python
import math

import jax
import jax.numpy as jnp
from jax import lax
from jax.experimental import pallas as pl
from jax.experimental.pallas import tpu as pltpu
from jax.sharding import Mesh
from jax.sharding import PartitionSpec as P

HEADS = 16
HEAD = 128
MB = 2
SEATS = 2
PACK = 80

epsilon = 1e-05
gelu_scale = 0.7978845608028654
gelu_cubic = 0.044715

DP = ("x", "c")


def low(values):
    return values.astype(jnp.bfloat16)


def wide(values):
    return values.astype(jnp.float32)


def product(left_mat, right_mat):
    return jnp.dot(left_mat, right_mat, preferred_element_type=jnp.float32)


def product_rows(left_mat, right_mat):
    return lax.dot_general(
        left_mat, right_mat, (((0,), (0,)), ((), ())), preferred_element_type=jnp.float32
    )


def product_cols(left_mat, right_mat):
    return lax.dot_general(
        left_mat, right_mat, (((1,), (1,)), ((), ())), preferred_element_type=jnp.float32
    )


def normalize(rows):
    center = rows - jnp.mean(rows, axis=-1, keepdims=True)
    spread = jnp.mean(center * center, axis=-1, keepdims=True)
    scale = lax.rsqrt(spread + epsilon)
    return center * scale, scale


def norm_back(grad_normed, gain, xhat, scale):
    g = grad_normed * gain
    inner = jnp.mean(g * xhat, axis=-1, keepdims=True)
    return scale * (g - jnp.mean(g, axis=-1, keepdims=True) - xhat * inner)


def gelu_parts(values):
    inner = jnp.tanh(gelu_scale * (values + gelu_cubic * values * values * values))
    activated = 0.5 * values * (1.0 + inner)
    slope = 0.5 * (1.0 + inner) + 0.5 * values * (1.0 - inner * inner) * gelu_scale * (
        1.0 + 3.0 * gelu_cubic * values * values
    )
    return activated, slope


MESH_ID = pl.DeviceIdType.MESH
VMEM_LIMIT = 56 * 1024 * 1024


class Spot:
    def __init__(self, depth):
        self.depth = depth
        self.z = lax.axis_index("z")
        self.y = lax.axis_index("y")
        self.x = lax.axis_index("x")
        self.c = lax.axis_index("c")
        self.to_c = {"c": 1 - self.c}
        self.to_x = {"x": 1 - self.x}
        self.to_y = {"y": 1 - self.y}
        self.to_xc = {"x": 1 - self.x, "c": 1 - self.c}
        self.up = {"z": self.z + 1}
        self.down = {"z": self.z - 1}

    def ring(self):
        before = {"z": lax.rem(self.z + self.depth - 1, self.depth)}
        return ({"z": lax.rem(self.z + 1, self.depth)}, before)

    def barrier(self, plane, line):
        bar = pltpu.get_barrier_semaphore()
        for to in plane:
            pl.semaphore_signal(bar, inc=1, device_id=to, device_id_type=MESH_ID)
        if line:

            @pl.when(self.z > 0)
            def _():
                pl.semaphore_signal(bar, inc=1, device_id=self.down, device_id_type=MESH_ID)

            @pl.when(self.z < self.depth - 1)
            def _():
                pl.semaphore_signal(bar, inc=1, device_id=self.up, device_id_type=MESH_ID)

        count = len(plane)
        if line:
            lower = jnp.where(self.z > 0, 1, 0)
            upper = jnp.where(self.z < self.depth - 1, 1, 0)
            count = count + lower + upper
        pl.semaphore_wait(bar, count)


class Net:
    def __init__(self, send_sems, recv_sems, local_sems):
        self.send_sems = send_sems
        self.recv_sems = recv_sems
        self.local_sems = local_sems
        self.count = 0
        self.local_count = 0
        self.open = []

    def remote(self, src, dst, to, arrives=None):
        copy = Copy(self, self.count, src, dst, to, arrives)
        self.count += 1
        return copy

    def local(self, src, dst):
        copy = pltpu.make_async_copy(src, dst, self.local_sems.at[self.local_count])
        self.local_count += 1
        return copy


class Copy:
    def __init__(self, net, index, src, dst, to, arrives):
        def make(target):
            return pltpu.make_async_remote_copy(
                src_ref=src,
                dst_ref=target,
                send_sem=net.send_sems.at[index],
                recv_sem=net.recv_sems.at[index],
                device_id=to,
                device_id_type=MESH_ID,
            )

        self.out = make(dst)
        self.into = make(dst if arrives is None else arrives)

    def start(self):
        self.out.start()

    def got(self):
        self.into.wait_recv()

    def sent(self):
        self.out.wait_send()


class PlaneGather:
    def __init__(self, net, spot, own, slots, share=2):
        def at(y, x, c):
            return y * 4 + x * 2 + c

        y, x, c = spot.y, spot.x, spot.c
        self.both = share == 2
        half = own.shape[0] // share
        lo, hi = pl.ds(0, half), pl.ds(half * (share - 1), half)
        me = at(y, x, c)
        on_x, on_y, on_d = at(y, 1 - x, c), at(1 - y, x, c), at(1 - y, 1 - x, c)
        peer = [at(y, x, 1 - c), at(y, 1 - x, 1 - c), at(1 - y, x, 1 - c), at(1 - y, 1 - x, 1 - c)]

        def slot(index):
            return slots.at[index]

        self.keep = net.local(own, slot(me))
        self.x = net.remote(own, slot(me), spot.to_x, slot(on_x))
        self.y = net.remote(own, slot(me), spot.to_y, slot(on_y))
        self.c = net.remote(own, slot(me), spot.to_c, slot(peer[0]))
        self.x_on_y = net.remote(
            slots.at[on_x, lo], slots.at[on_x, lo], spot.to_y, slots.at[on_d, lo]
        )
        self.x_on_c = net.remote(slot(on_x), slot(on_x), spot.to_c, slot(peer[1]))
        self.y_on_c = net.remote(slot(on_y), slot(on_y), spot.to_c, slot(peer[2]))
        self.lo_on_c = net.remote(
            slots.at[on_d, lo], slots.at[on_d, lo], spot.to_c, slots.at[peer[3], lo]
        )
        if self.both:
            self.y_on_x = net.remote(
                slots.at[on_y, hi], slots.at[on_y, hi], spot.to_x, slots.at[on_d, hi]
            )
            self.hi_on_c = net.remote(
                slots.at[on_d, hi], slots.at[on_d, hi], spot.to_c, slots.at[peer[3], hi]
            )

    def start(self):
        self.x.start()
        self.y.start()
        self.c.start()
        self.keep.start()

    def middle(self):
        self.x.got()
        self.x_on_y.start()
        self.x_on_c.start()
        self.y.got()
        if self.both:
            self.y_on_x.start()
        self.y_on_c.start()

    def last(self):
        self.x_on_y.got()
        self.lo_on_c.start()
        if self.both:
            self.y_on_x.got()
            self.hi_on_c.start()

    def finish(self):
        second = (self.y_on_x, self.hi_on_c) if self.both else ()
        for copy in (self.c, self.x_on_c, self.y_on_c, self.lo_on_c, *second[1:]):
            copy.got()
        firsts = (self.x, self.y, self.c, self.x_on_y, self.x_on_c, self.y_on_c, self.lo_on_c)
        for copy in (*firsts, *second):
            copy.sent()
        self.keep.wait()

    remotes = 9
    locals = 1


def add_rows(into, other, step=32):
    rows = into.shape[0]

    @pl.loop(0, rows // step)
    def _(index):
        at = pl.ds(pl.multiple_of(index * step, step), step)
        into[at, :] = low(wide(into[at, :]) + wide(other[at, :]))


class PlaneScatter:
    remotes = 10

    @staticmethod
    def buffers(rows, width):
        return [
            pltpu.VMEM((4, rows, width), jnp.bfloat16),
            pltpu.VMEM((rows, width), jnp.bfloat16),
            pltpu.VMEM((rows, width), jnp.bfloat16),
            pltpu.VMEM((rows, width), jnp.bfloat16),
        ]

    def __init__(self, net, spot, parts, sums, diag, from_x, from_y, share=2):
        y, x, c = spot.y, spot.x, spot.c
        self.both = share == 2
        half = parts.shape[1] // share
        lo, hi = pl.ds(0, half), pl.ds(half * (share - 1), half)
        self.own, self.nx, self.ny, self.nd = (
            y * 2 + x,
            y * 2 + 1 - x,
            (1 - y) * 2 + x,
            (1 - y) * 2 + 1 - x,
        )
        self.parts, self.sums, self.diag = parts, sums, diag
        self.stacked = parts.shape[0] == 4
        self.from_x, self.from_y, self.c = from_x, from_y, c
        self.lo, self.hi = lo, hi
        self.first = {
            key: net.remote(
                parts.at[at] if self.stacked else parts.at[at * 2 + 1 - c], sums.at[at], spot.to_c
            )
            for key, at in (("d", self.nd), ("x", self.nx), ("y", self.ny), ("o", self.own))
        }
        self.d_hi = net.remote(sums.at[self.nd, hi], diag.at[hi], spot.to_y)
        self.y_hi = net.remote(sums.at[self.ny, hi], from_y.at[hi], spot.to_y)
        self.x_hi = net.remote(sums.at[self.nx, hi], from_x.at[hi], spot.to_x)
        if self.both:
            self.d_lo = net.remote(sums.at[self.nd, lo], diag.at[lo], spot.to_x)
            self.x_lo = net.remote(sums.at[self.nx, lo], from_x.at[lo], spot.to_x)
            self.y_lo = net.remote(sums.at[self.ny, lo], from_y.at[lo], spot.to_y)

    def start(self):
        for copy in self.first.values():
            copy.start()

    def give(self, key, at):
        if self.stacked:
            self.send(at, at * 2 + 1 - self.c)
            self.first[key].start()

    def pair(self, key, at):
        if self.stacked:
            self.prepare(at * 2 + self.c)
            self.first[key].got()
            self.merge(at * 2 + self.c, at)
        else:
            self.first[key].got()
            add_rows(self.sums.at[at], self.parts.at[at * 2 + self.c])

    def middle(self):
        self.give("d", self.nd)
        self.give("x", self.nx)
        self.pair("d", self.nd)
        if self.both:
            self.d_lo.start()
        self.d_hi.start()
        self.give("y", self.ny)
        self.pair("x", self.nx)
        if self.both:
            self.x_lo.start()
        self.give("o", self.own)
        self.pair("y", self.ny)
        self.y_hi.start()
        self.pair("o", self.own)

    def last(self):
        if self.both:
            self.d_lo.got()
            add_rows(self.sums.at[self.ny, self.lo], self.diag.at[self.lo], 16)
            self.y_lo.start()
        self.d_hi.got()
        add_rows(self.sums.at[self.nx, self.hi], self.diag.at[self.hi], 16)
        self.x_hi.start()

    def finish(self, result):
        second = (self.x_lo, self.y_lo) if self.both else ()
        for copy in (self.y_hi, self.x_hi, *second):
            copy.got()

        @pl.loop(0, result.shape[0] // 16)
        def _(index):
            at = pl.ds(pl.multiple_of(index * 16, 16), 16)
            result[at, :] = (
                wide(self.sums[self.own, at, :]) + wide(self.from_x[at, :]) + wide(self.from_y[at, :])
            )

        for copy in (
            *self.first.values(),
            self.d_hi,
            self.x_hi,
            self.y_hi,
            *((self.d_lo, *second) if self.both else ()),
        ):
            copy.sent()


class LineGather:
    def __init__(self, net, spot, slots, moves=None):
        self.spot, depth, z = spot, spot.depth, spot.z
        self.moves = moves
        self.hops = []
        for step in range(depth - 1):
            lower = jnp.maximum(z - step, 0)
            upper = jnp.minimum(z + step, depth - 1)
            from_low = jnp.maximum(z - 1 - step, 0)
            from_high = jnp.minimum(z + 1 + step, depth - 1)
            self.hops.append(
                (
                    net.remote(slots(lower), slots(lower), spot.up, slots(from_low)),
                    net.remote(slots(upper), slots(upper), spot.down, slots(from_high)),
                )
            )

    @staticmethod
    def remotes(depth):
        return 2 * (depth - 1)

    def pick(self, cond, slot):
        return cond if self.moves is None else cond & self.moves(slot)

    def sends(self, step):
        z, last = self.spot.z, self.spot.depth - 1
        return (
            (self.pick((z >= step) & (z < last), z - step), self.hops[step][0]),
            (self.pick((z + step <= last) & (z > 0), z + step), self.hops[step][1]),
        )

    def takes(self, step):
        z, last = self.spot.z, self.spot.depth - 1
        return (
            (self.pick(z >= step + 1, z - 1 - step), self.hops[step][0]),
            (self.pick(z + step + 1 <= last, z + 1 + step), self.hops[step][1]),
        )

    def start(self, step):
        for cond, copy in self.sends(step):
            pl.when(cond)(copy.start)

    def got(self, step):
        for cond, copy in self.takes(step):
            pl.when(cond)(copy.got)

    def hop(self, step):
        for (came, old), (goes, new) in zip(self.takes(step - 1), self.sends(step)):
            pl.when(came)(old.got)
            pl.when(goes)(new.start)

    def finish(self):
        for step in range(self.spot.depth - 1):
            for cond, copy in self.sends(step):
                pl.when(cond)(copy.sent)


class LineScatter:
    def __init__(self, net, spot, parts, from_low, from_high, add):
        self.net, self.spot, self.parts, self.add = net, spot, parts, add
        self.boxes = (from_low, from_high)
        self.first = net.count
        net.count += 2 * (spot.depth - 1)

    @staticmethod
    def remotes(depth):
        return 2 * (depth - 1)

    def copy(self, side, message):
        last = self.spot.depth - 1
        slot = self.parts(last - message if side == 0 else message)
        at = self.first + side * last + message
        copy = pltpu.make_async_remote_copy(
            src_ref=slot,
            dst_ref=self.boxes[side].at[message],
            send_sem=self.net.send_sems.at[at],
            recv_sem=self.net.recv_sems.at[at],
            device_id=(self.spot.up, self.spot.down)[side],
            device_id_type=MESH_ID,
        )
        return copy, slot, self.boxes[side].at[message]

    def take(self, side, message):
        copy, slot, box = self.copy(side, message)
        copy.wait_recv()
        self.add(slot, box)

    def place(self, side):
        return self.spot.z if side == 0 else self.spot.depth - 1 - self.spot.z

    def stage(self, step):
        for side in range(2):
            behind = self.place(side)

            @pl.when(behind <= step)
            def _():
                message = step - behind

                @pl.when(behind > 0)
                def _():
                    self.take(side, message)

                self.copy(side, message)[0].start()

    def total(self):
        last = self.spot.depth - 1
        for side in range(2):
            behind = self.place(side)

            @pl.when(behind > 0)
            def _():
                self.take(side, last - behind)

    def finish(self):
        for side in range(2):
            behind = self.place(side)
            for message in range(self.spot.depth - 1):

                @pl.when(behind + message < self.spot.depth - 1)
                def _():
                    self.copy(side, message)[0].wait_send()


class DpGather:
    remotes = 3

    def __init__(self, net, spot, own, slots):
        me = spot.x * 2 + spot.c
        on_x = (1 - spot.x) * 2 + spot.c
        self.keep = net.local(own, slots.at[me])
        self.x = net.remote(own, slots.at[me], spot.to_x, slots.at[on_x])
        self.c = net.remote(own, slots.at[me], spot.to_c, slots.at[spot.x * 2 + 1 - spot.c])
        self.x_on_c = net.remote(
            slots.at[on_x],
            slots.at[on_x],
            spot.to_c,
            slots.at[(1 - spot.x) * 2 + 1 - spot.c],
        )

    def start(self):
        self.x.start()
        self.c.start()
        self.keep.start()

    def last(self):
        self.x.got()
        self.x_on_c.start()

    def finish(self):
        self.c.got()
        self.x_on_c.got()
        for copy in (self.x, self.c, self.x_on_c):
            copy.sent()
        self.keep.wait()


class DpExchange:
    remotes = 3

    def __init__(self, net, spot, parts, slots):
        me = spot.x * 2 + spot.c
        on_x = (1 - spot.x) * 2 + spot.c
        on_c = spot.x * 2 + 1 - spot.c
        on_xc = (1 - spot.x) * 2 + 1 - spot.c
        self.keep = net.local(parts.at[me], slots.at[me])
        self.moves = [
            net.remote(parts.at[at], slots.at[me], to, slots.at[at])
            for at, to in ((on_xc, spot.to_xc), (on_x, spot.to_x), (on_c, spot.to_c))
        ]

    def start(self):
        for copy in self.moves:
            copy.start()
        self.keep.start()

    def got(self):
        for copy in self.moves:
            copy.got()
        self.keep.wait()

    def finish(self):
        for copy in self.moves:
            copy.sent()


def net_scratch(remotes, locals_):
    return [
        pltpu.SemaphoreType.DMA((remotes,)),
        pltpu.SemaphoreType.DMA((remotes,)),
        pltpu.SemaphoreType.DMA((max(locals_, 1),)),
    ]


ANY = pl.BlockSpec(memory_space=pl.ANY)
IN_VMEM = pl.BlockSpec(memory_space=pltpu.VMEM)


def lasts(micros, moved):
    return pl.CostEstimate(
        flops=int(micros * 1e9), bytes_accessed=int(moved), transcendentals=0
    )


def comm_params(collective_id):
    return pltpu.CompilerParams(
        collective_id=collective_id, has_side_effects=True, vmem_limit_bytes=VMEM_LIMIT
    )


def low_shape(*dims):
    return jax.ShapeDtypeStruct(dims, jnp.bfloat16)


def wide_shape(*dims):
    return jax.ShapeDtypeStruct(dims, jnp.float32)


def low_vmem(*dims):
    return pltpu.VMEM(dims, jnp.bfloat16)


def pick_rows(chooser, source, result, step=512):
    width = result.shape[-1]

    @pl.loop(0, width // step)
    def _(index):
        at = pl.ds(pl.multiple_of(index * step, step), step)
        rows = source[..., at].reshape(chooser.shape[1], step)
        result[..., at] = low(product(chooser[...], rows)).reshape(*result.shape[:-1], step)


def opening(depth, owner, tokens, cotangent, sender, chooser, query_weight, keyval_weight, output_weight, small, up_mine, up_other):
    rows = chooser.shape[0]
    width = tokens.shape[-1]
    group = depth // 4
    rows_own = query_weight.shape[0]
    head_cols = width // 8
    kv_rows = rows_own // 4
    kv_cols = keyval_weight.shape[1]

    def kernel(
        tok_held, cot_held, send, choose, query_w, kv_w, out_w, small_m, up_m, up_o,
        own_tok, own_cot, up_own, small_rows, w_keyval,
        tok_all, query_all, out_all,
        kv_all, small_all, tok, cot, tok_got, cot_got, out_v, kv_line, query_m, query_o, query_y, small_y,
        query_f, out_f, kv_f, *sems,
    ):
        spot = Spot(depth)
        net = Net(*sems)
        z, y = spot.z, spot.y
        xc = spot.x * 2 + spot.c
        source = z // group == xc

        def head_base(y_at):
            return pl.multiple_of(owner(xc * group, y_at) * rows_own, 128)

        def strip(ref, size):
            return ref.at[pl.ds(pl.multiple_of(xc * size, size), size)]

        def z_slot(at):
            return kv_line.at[pl.ds(pl.multiple_of(at * kv_rows, kv_rows), kv_rows)]

        read_query_o = net.local(query_w.at[:, pl.ds(head_base(1 - y), head_cols)], query_f.at[0])
        read_out = net.local(out_w, out_f)
        read_kv = net.local(strip(kv_w, kv_rows), kv_f)
        read_query = net.local(query_w.at[:, pl.ds(head_base(y), head_cols)], query_f.at[1])
        tok_deal = DpExchange(net, spot, tok, tok_got)
        cot_deal = DpExchange(net, spot, cot, cot_got)
        tok_run = PlaneGather(net, spot, own_tok, tok_all)
        kv_run = PlaneGather(net, spot, kv_line, kv_all)
        y_query = net.remote(query_o, query_y, spot.to_y)
        y_small = net.remote(small_m, small_y, spot.to_y)
        y_up = net.remote(up_o, up_own.at[y], spot.to_y, up_own.at[1 - y])
        keep_query = net.local(query_m, query_all.at[z, y])
        keep_query_y = net.local(query_y, query_all.at[z, 1 - y])
        keep_out = net.local(out_v, out_all)
        run_kv = LineGather(net, spot, z_slot)
        run_query = LineGather(net, spot, lambda at: query_all.at[at])
        run_small = LineGather(net, spot, lambda at: small_all.at[at])

        def piece_of_out(piece):
            rows_at = pl.ds(piece * kv_rows, kv_rows)
            return LineGather(
                net,
                spot,
                lambda at: out_v.at[at % group, rows_at],
                lambda at: at // group == xc,
            )

        run_outs = [piece_of_out(piece) for piece in range(4)]
        read_query_o.start()
        pl.when(source)(read_out.start)
        read_kv.start()
        read_query.start()
        small_all[z, y] = small_m[...]
        spot.barrier((spot.to_c, spot.to_x, spot.to_y, spot.to_xc), True)
        pick_rows(send, tok_held, tok)
        tok_deal.start()
        read_query_o.wait()
        query_o[...] = low(query_f[0])
        y_query.start()
        y_small.start()
        y_up.start()

        @pl.when(source)
        def _():
            read_out.wait()

            @pl.loop(0, rows_own // 16)
            def _(index):
                at = pl.ds(pl.multiple_of(index * 16, 16), 16)
                out_v[z % group, at, :] = low(out_f[at, :])

        for run in run_outs:
            run.start(0)
        read_kv.wait()
        z_slot(z)[...] = low(kv_f[...])
        run_kv.start(0)
        read_query.wait()
        query_m[...] = low(query_f[1])
        keep_query.start()
        keep_query.wait()
        y_query.got()
        keep_query_y.start()
        y_small.got()
        small_all[z, 1 - y] = small_y[...]
        keep_query_y.wait()
        run_query.start(0)
        run_small.start(0)
        pick_rows(send, cot_held, cot)

        @pl.loop(0, rows_own // 16)
        def _(index):
            at = pl.ds(pl.multiple_of(index * 16, 16), 16)
            up_own[y, at, :] = up_m[at, :]

        tok_deal.got()
        pick_rows(choose, tok_got, own_tok)
        tok_run.start()
        cot_deal.start()
        for step in range(1, depth - 1):
            for run in run_outs:
                run.hop(step)
            run_kv.hop(step)
        run_query.hop(1)
        run_small.hop(1)
        run_kv.got(depth - 2)
        kv_run.start()
        for step in range(2, depth - 1):
            run_query.hop(step)
            run_small.hop(step)
        tok_run.middle()
        kv_run.middle()
        cot_deal.got()
        pick_rows(choose, cot_got, own_cot)
        tok_run.last()
        kv_run.last()
        for run in run_outs:
            run.got(depth - 2)
        keep_out.start()
        run_query.got(depth - 2)
        run_small.got(depth - 2)
        for z_at in range(depth):
            for y_at in range(2):
                at = owner(z_at, y_at) * rows_own
                small_rows[:, at : at + rows_own] = wide(small_all[z_at, y_at])
        y_up.got()
        runs = (*run_outs, run_kv, run_query, run_small, tok_run, kv_run)
        for run in (*runs, tok_deal, cot_deal):
            run.finish()
        for y_at in range(2):
            for xc_at in range(4):
                for z_at in range(depth):
                    at = owner(z_at, y_at) * rows_own + xc_at * kv_rows
                    w_keyval[at : at + kv_rows, :] = kv_all[
                        y_at * 4 + xc_at, z_at * kv_rows : (z_at + 1) * kv_rows, :
                    ]
        for copy in (y_query, y_small, y_up):
            copy.sent()
        keep_out.wait()

    remotes = (
        2 * DpExchange.remotes + 2 * PlaneGather.remotes + 4 + 7 * LineGather.remotes(depth)
    )
    operands = (
        tokens, cotangent, sender, chooser, query_weight, keyval_weight, output_weight, small,
        up_mine, up_other,
    )
    wide_type = jnp.float32
    return pl.pallas_call(
        kernel,
        out_shape=[
            low_shape(rows, width),
            low_shape(rows, width),
            low_shape(2, *up_mine.shape),
            wide_shape(small.shape[0], width),
            low_shape(width, kv_cols),
            low_shape(8, rows, width),
            low_shape(depth, 2, rows_own, head_cols),
            low_shape(group, rows_own, width),
        ],
        in_specs=[IN_VMEM] * 4 + [ANY] * 3 + [IN_VMEM] * 3,
        out_specs=[IN_VMEM] * 5 + [ANY] * 3,
        scratch_shapes=[
            low_vmem(8, depth * kv_rows, kv_cols),
            low_vmem(depth, 2, *small.shape),
            *[low_vmem(*tokens.shape)] * 4,
            low_vmem(group, rows_own, width),
            low_vmem(depth * kv_rows, kv_cols),
            low_vmem(rows_own, head_cols),
            low_vmem(rows_own, head_cols),
            low_vmem(rows_own, head_cols),
            low_vmem(*small.shape),
            pltpu.VMEM((2, rows_own, head_cols), wide_type),
            pltpu.VMEM((rows_own, width), wide_type),
            pltpu.VMEM((kv_rows, kv_cols), wide_type),
            *net_scratch(remotes, 20),
        ],
        compiler_params=comm_params(1),
        cost_estimate=lasts(75, 1 << 20),
    )(*operands)


ROWS_STEP = 32


def row_loop(count):
    def decorate(body):
        @pl.loop(0, count // ROWS_STEP)
        def _(index):
            body(pl.ds(pl.multiple_of(index * ROWS_STEP, ROWS_STEP), ROWS_STEP))

    return decorate


class Loads:
    def __init__(self, net, far, near):
        self.net, self.far, self.near = net, far, near
        self.first = net.local_count
        net.local_count += 8

    def copy(self, member):
        return pltpu.make_async_copy(
            self.far.at[member], self.near.at[member], self.net.local_sems.at[self.first + member]
        )

    def start(self, spot):
        def at(y, x, c):
            return y * 4 + x * 2 + c

        y, x, c = spot.y, spot.x, spot.c
        for y_at, x_at in ((1 - y, 1 - x), (y, 1 - x), (1 - y, x), (y, x)):
            for c_at in (1 - c, c):
                self.copy(at(y_at, x_at, c_at)).start()

    def wait(self, member):
        self.copy(member).wait()


def feed_blocks(run, parts, block, prepare=None):
    width = parts.shape[-1]

    def columns(body):
        @pl.loop(0, width // 512)
        def _(index):
            body(pl.ds(pl.multiple_of(index * 512, 512), 512))

    def ready(member):
        if prepare is not None:
            prepare(member)

    def send(at, member):
        ready(member)

        @columns
        def _(cols):
            parts[at, :, cols] = low(block(member, cols))

    def merge(member, at):
        @columns
        def _(cols):
            run.sums[at, :, cols] = low(wide(run.sums[at, :, cols]) + block(member, cols))

    run.send, run.merge, run.prepare = send, merge, ready


SCORE_SCALE = 1.0 / math.sqrt(HEAD)


def stacked(values):
    return jnp.concatenate([values[:, :HEAD], values[:, HEAD:]], axis=0)


def unstacked(values):
    half = values.shape[0] // 2
    return jnp.concatenate([values[:half], values[half:]], axis=1)


def softmax_of(query_2, keys, allowed):
    scores = product_cols(query_2, keys) * SCORE_SCALE
    scores = jnp.where(jnp.concatenate([allowed, allowed], axis=0) > 0.0, scores, -1e30)
    exps = jnp.exp(scores - jnp.max(scores, axis=-1, keepdims=True))
    return exps / jnp.sum(exps, axis=-1, keepdims=True)


def attend(depth, tok_all, own_tok, own_cot, w_query, w_keyval, w_output, bias_q, bias_kv, allowed, small, up_own, down_own, down_1):
    rows, width = own_tok.shape
    total = 8 * rows
    head_cols = w_query.shape[1]
    micros = rows // PACK

    def kernel(
        tok_far, tok, cot, w_q, w_kv, w_out, b_q, b_kv, allow, small,
        up, down, down_b,
        middle, normed_a, query, keyval, attended, normed_all, cot_all, up_all, down_all, down_2,
        tok_near, parts, normed, sums, diag, from_x, from_y, *sems,
    ):
        spot = Spot(depth)
        net = Net(*sems)
        z = spot.z
        run = PlaneScatter(net, spot, parts, sums, diag, from_x, from_y)
        gather = PlaneGather(net, spot, normed, normed_all)
        cot_run = PlaneGather(net, spot, cot, cot_all, share=1)
        after, _ = spot.ring()

        def behind(step):
            return lax.rem(z + 2 * depth - step, depth)

        keeps = [
            net.local(up, up_all.at[z]),
            net.local(down, down_all.at[z]),
            net.local(down_b, down_all.at[behind(1)]),
        ]
        keep_2 = net.local(down_2, down_all.at[behind(2)])
        ups = [net.remote(up, up_all.at[z], after, up_all.at[behind(1)])]
        for step in range(2, depth):
            at = up_all.at[behind(step - 1)]
            ups.append(net.remote(at, at, after, up_all.at[behind(step)]))
        down_hop = net.remote(down_b, down_2, after)

        tok_loads = Loads(net, tok_far, tok_near)

        def one_member(member):
            tok_loads.wait(member)
            first = pl.multiple_of(member * rows, rows)

            @pl.loop(0, rows // ROWS_STEP)
            def _(index):
                at = pl.multiple_of(index * ROWS_STEP, ROWS_STEP)
                xhat, _ = normalize(wide(tok_near[member, pl.ds(at, ROWS_STEP), :]))
                normed_a[pl.ds(first + at, ROWS_STEP), :] = low(xhat * small[0:1, :] + small[1:2, :])

            rows_at = pl.ds(first, rows)
            query[rows_at, :] = low(product(normed_a[rows_at, :], w_q[...]) + b_q[...])
            keyval[rows_at, :] = low(product(normed_a[rows_at, :], w_kv[...]) + b_kv[...])

            for index in range(micros):
                at = pl.ds(pl.multiple_of(first + index * PACK, PACK), PACK)
                pair = keyval[at, :]
                probs = softmax_of(
                    stacked(query[at, :]), pair[:, :HEAD], allow[member * micros + index]
                )
                attended[at, :] = low(unstacked(product(low(probs), pair[:, HEAD:])))

        def block(member, cols):
            rows_at = pl.ds(pl.multiple_of(member * rows, rows), rows)
            return product(attended[rows_at, :], w_out[:, cols])

        tok_loads.start(spot)
        for copy in keeps:
            copy.start()
        spot.barrier((spot.to_c, spot.to_x, spot.to_y, *spot.ring()), False)
        ups[0].start()
        cot_run.start()
        feed_blocks(run, parts, block, one_member)
        run.middle()
        down_hop.start()
        cot_run.middle()
        ups[0].got()
        ups[1].start()
        run.last()
        cot_run.last()
        run.finish(middle)

        @row_loop(rows)
        def _(at):
            total_rows = wide(tok[at, :]) + (middle[at, :] + small[2:3, :])
            middle[at, :] = total_rows
            xhat, _ = normalize(total_rows)
            normed[at, :] = low(xhat * small[3:4, :] + small[4:5, :])

        gather.start()
        down_hop.got()
        keep_2.start()
        for step in range(2, depth - 1):
            ups[step - 1].got()
            ups[step].start()
        gather.middle()
        gather.last()
        gather.finish()
        cot_run.finish()
        ups[-1].got()
        for copy in (*ups, down_hop):
            copy.sent()
        for copy in (*keeps, keep_2):
            copy.wait()

    return pl.pallas_call(
        kernel,
        out_shape=[
            wide_shape(rows, width),
            low_shape(total, width),
            low_shape(total, head_cols),
            low_shape(total, 2 * HEAD),
            low_shape(total, head_cols),
            low_shape(8, rows, width),
            low_shape(8, rows, width),
            low_shape(depth, *up_own.shape),
            low_shape(depth, *down_own.shape),
            low_shape(*down_own.shape),
        ],
        in_specs=[ANY] + [IN_VMEM] * 12,
        out_specs=[IN_VMEM] * 5 + [ANY] * 4 + [IN_VMEM],
        scratch_shapes=[
            low_vmem(8, rows, width),
            low_vmem(4, rows, width),
            low_vmem(rows, width),
            *PlaneScatter.buffers(rows, width),
            *net_scratch(PlaneScatter.remotes + 2 * PlaneGather.remotes + depth, 14),
        ],
        compiler_params=comm_params(3),
        cost_estimate=lasts(90, 1 << 20),
    )(
        tok_all, own_tok, own_cot, w_query, w_keyval, w_output, bias_q, bias_kv, allowed, small,
        up_own, down_own, down_1,
    )


def attend_back(depth, branch_all, query, keyval, allowed, w_output, w_query, w_keyval, own_tok, grad_middle, gain, block, chooser, holder, d_out, up_sum, up_parts, down_sum):
    group = depth // 4
    rows, width = own_tok.shape
    total, head_cols = query.shape
    micros = rows // PACK
    slots = chooser.shape[0] // 4

    def kernel(
        branch_far, q_all, kv_all, allow, w_out, w_q, w_kv, tok, grad_mid, small, block_own, choose, hold,
        out, du, dd, du_far,
        grad_q, kv_rows_all, vec, block_res, grad_res, out_sum, du_sum, dd_x,
        parts, sums, diag, from_x, from_y, first, grad_low, block_send, grad_send, block_got, grad_got,
        branch, out_mix, out_lo, out_hi, du_term, du_mid,
        grad_kv, kv_sums, kv_diag, kv_from_x, kv_from_y, kv_wide, kv_own, *sems,
    ):
        spot = Spot(depth)
        net = Net(*sems)
        run = PlaneScatter(net, spot, parts, sums, diag, from_x, from_y, share=1)
        down_over = net.remote(dd, dd_x, spot.to_x)
        z = spot.z
        after, _ = spot.ring()
        deal = DpExchange(net, spot, out, out_mix)

        def mixed(at):
            return out_mix.at[at // group, at % group]

        def add2(into, other):
            add_rows(into, other, 16)

        kv_run = PlaneScatter(net, spot, grad_kv, kv_sums, kv_diag, kv_from_x, kv_from_y)
        kv_gather = PlaneGather(net, spot, kv_own, kv_rows_all)
        run_out = LineScatter(net, spot, mixed, out_lo, out_hi, add2)
        hops = [net.remote(du, du_mid, after), net.remote(du_mid, du_sum, after)]
        terms = [
            net.local(du_far.at[lax.rem(z + 1, depth)], du_term.at[0]),
            net.local(du_far.at[z], du_term.at[1]),
        ]

        def up_step(step):
            into = (du_mid, du_sum)[step]
            hops[step].got()
            terms[step].wait()
            for at in range(2):
                add_rows(into.at[at], du_term.at[step, at], 32)
            if step == 0:
                hops[1].start()

        back_block = DpExchange(net, spot, block_send, block_got)
        back_grad = DpExchange(net, spot, grad_send, grad_got)

        branch_loads = Loads(net, branch_far, branch)

        def one_member(member):
            branch_loads.wait(member)
            begin = pl.multiple_of(member * rows, rows)
            grad_att = low(product_cols(branch[member], w_out[...]))
            for index in range(micros):
                at = pl.ds(pl.multiple_of(begin + index * PACK, PACK), PACK)
                pair = kv_all[at, :]
                keys, vals = pair[:, :HEAD], pair[:, HEAD:]
                q_2 = stacked(q_all[at, :])
                g_2 = stacked(grad_att[index * PACK : (index + 1) * PACK])
                probs = softmax_of(q_2, keys, allow[member * micros + index])
                grad_probs = product_cols(g_2, vals)
                inner = jnp.sum(probs * grad_probs, axis=-1, keepdims=True)
                grad_scores = low(probs * (grad_probs - inner))
                grad_q[at, :] = low(unstacked(product(grad_scores, keys) * SCORE_SCALE))
                grad_k = product_rows(grad_scores, q_2) * SCORE_SCALE
                grad_v = product_rows(low(probs), g_2)
                grad_kv[member, index * PACK : (index + 1) * PACK, :] = low(
                    jnp.concatenate([grad_k, grad_v], axis=1)
                )

        def block_of(member, cols):
            rows_at = pl.ds(pl.multiple_of(member * rows, rows), rows)
            return product_cols(grad_q[rows_at, :], w_q[cols, :]) + product_cols(
                grad_kv[member], w_kv[cols, :]
            )

        branch_loads.start(spot)
        for copy in terms:
            copy.start()
        spot.barrier((spot.to_c, spot.to_x, spot.to_y, spot.to_xc, *spot.ring()), False)
        deal.start()
        hops[0].start()
        down_over.start()
        pick_rows(choose, block_own, block_send)
        feed_blocks(run, parts, block_of, one_member)
        run.middle()
        kv_run.start()
        deal.got()
        run_out.stage(0)
        up_step(0)
        kv_run.middle()
        run.last()
        run_out.stage(1)
        kv_run.last()
        run.finish(first)
        kv_run.finish(kv_wide)
        back_block.start()
        kv_own[...] = low(kv_wide[...])
        kv_gather.start()
        vec[...] = jnp.zeros_like(vec)

        @row_loop(rows)
        def _(at):
            xhat, scale = normalize(wide(tok[at, :]))
            grad = grad_mid[at, :] + norm_back(first[at, :], small[0:1, :], xhat, scale)
            grad_low[at, :] = low(grad)
            vec[0:1, :] += jnp.sum(first[at, :] * xhat, axis=0, keepdims=True)
            vec[1:2, :] += jnp.sum(first[at, :], axis=0, keepdims=True)

        pick_rows(choose, grad_low, grad_send)
        back_grad.start()
        for step in range(2, depth - 1):
            run_out.stage(step)
        kv_gather.middle()
        run_out.total()
        out_sum[...] = mixed(z)[...]
        kv_gather.last()
        back_block.got()
        pick_rows(hold, block_got, block_res)
        back_grad.got()
        pick_rows(hold, grad_got, grad_res)
        up_step(1)
        for run_done in (back_block, back_grad, deal, run_out):
            run_done.finish()
        kv_gather.finish()
        down_over.got()
        for copy in (*hops, down_over):
            copy.sent()

    return pl.pallas_call(
        kernel,
        out_shape=[
            low_shape(total, head_cols),
            low_shape(8, rows, 2 * HEAD),
            wide_shape(8, width),
            low_shape(4, slots, width),
            low_shape(4, slots, width),
            low_shape(*d_out.shape[2:]),
            low_shape(*up_sum.shape),
            low_shape(*down_sum.shape),
        ],
        in_specs=[ANY] + [IN_VMEM] * 15 + [ANY],
        out_specs=[IN_VMEM, ANY] + [IN_VMEM] * 6,
        scratch_shapes=[
            low_vmem(4, rows, width),
            *PlaneScatter.buffers(rows, width),
            pltpu.VMEM((rows, width), jnp.float32),
            low_vmem(rows, width),
            *[low_vmem(4, slots, width)] * 4,
            low_vmem(8, rows, width),
            low_vmem(*d_out.shape),
            *[low_vmem(depth - 1, *d_out.shape[2:])] * 2,
            low_vmem(2, *up_sum.shape),
            low_vmem(*up_sum.shape),
            low_vmem(8, rows, 2 * HEAD),
            *PlaneScatter.buffers(rows, 2 * HEAD),
            pltpu.VMEM((rows, 2 * HEAD), jnp.float32),
            low_vmem(rows, 2 * HEAD),
            *net_scratch(
                2 * PlaneScatter.remotes + PlaneGather.remotes + 3 * DpExchange.remotes + LineGather.remotes(depth) + 3, 14
            ),
        ],
        compiler_params=comm_params(4),
        cost_estimate=lasts(70, 1 << 20),
    )(
        branch_all, query, keyval, allowed, w_output, w_query, w_keyval, own_tok, grad_middle, gain,
        block, chooser, holder, d_out, up_sum, down_sum, up_parts,
    )


def mlp_back(depth, grad_hidden, w_up, activated, w_down, middle, own_cot, small, down_first, d_down, d_up):
    rows, width = own_cot.shape
    up_hops = 1

    def kernel(gh, up, act_far, down_far, mid, cot, small, dd_first, dd, du,
               vec, grad_middle, branch_all, block_out, dd_sum, du_sum,
               parts, branch, sums, diag, from_x, from_y,
               parts2, sums2, diag2, from_x2, from_y2, mlp_sum, act, down,
               dd_got, du_got, dd_term, du_term, grad_normed, *sems):
        spot = Spot(depth)
        net = Net(*sems)
        z = spot.z
        run = PlaneScatter(net, spot, parts, sums, diag, from_x, from_y)
        run2 = PlaneScatter(net, spot, parts2, sums2, diag2, from_x2, from_y2)
        gather = PlaneGather(net, spot, branch, branch_all)
        after, _ = spot.ring()

        def slot(step):
            return lax.rem(z + 2 * depth - 1 - step, depth)

        def down_at(step):
            return dd_sum if step == depth - 1 else dd_got.at[step - 1]

        def up_at(step):
            return du_sum if step == up_hops else du_got.at[step - 1]

        down_terms = [
            net.local(dd.at[slot(step)], dd_term.at[step - 1]) for step in range(1, depth)
        ]
        up_terms = [
            net.local(du.at[slot(step)], du_term.at[step - 1]) for step in range(1, up_hops + 1)
        ]
        loads = [net.local(act_far, act), net.local(down_far, down)]
        down_hops = [
            net.remote(down_at(step - 1), down_at(step), after) for step in range(2, depth)
        ]
        ups = [net.remote(du.at[slot(0)], up_at(1), after)]
        ups += [net.remote(up_at(step - 1), up_at(step), after) for step in range(2, up_hops + 1)]

        def down_step(step):
            down_hops[step - 2].got()
            down_terms[step - 1].wait()
            add_rows(down_at(step), dd_term.at[step - 1], 32)
            if step < depth - 1:
                down_hops[step - 1].start()

        def up_step(step):
            ups[step - 1].got()
            up_terms[step - 1].wait()
            for at in range(2):
                add_rows(up_at(step).at[at], du_term.at[step - 1, at], 32)
            if step < up_hops:
                ups[step].start()

        def block(member, cols):
            rows_at = pl.ds(pl.multiple_of(member * rows, rows), rows)
            return product_cols(gh[rows_at, :], up[cols, :])

        def block2(member, cols):
            rows_at = pl.ds(pl.multiple_of(member * rows, rows), rows)
            return product(act[rows_at, :], down[:, cols])

        for copy in (*down_terms, *up_terms, *loads):
            copy.start()
        spot.barrier((spot.to_c, spot.to_x, spot.to_y, *spot.ring()), False)
        down_terms[0].wait()

        @pl.loop(0, dd_first.shape[0] // 32)
        def _(index):
            at = pl.ds(pl.multiple_of(index * 32, 32), 32)
            dd_got[0, at, :] = low(wide(dd_first[at, :]) + wide(dd_term[0, at, :]))

        down_hops[0].start()
        feed_blocks(run, parts, block)
        run.middle()
        for copy in loads:
            copy.wait()
        feed_blocks(run2, parts2, block2)
        run.last()
        down_step(2)
        run.finish(grad_normed)
        vec[...] = jnp.zeros_like(vec)

        @row_loop(rows)
        def _(at):
            xhat, scale = normalize(mid[at, :])
            grad_n = grad_normed[at, :]
            grad_o = wide(cot[at, :])
            grad = grad_o + norm_back(grad_n, small[3:4, :], xhat, scale)
            grad_b = low(grad)
            grad_middle[at, :] = grad
            branch[at, :] = grad_b
            for row, values in enumerate((wide(grad_b), grad_n * xhat, grad_n, grad_o)):
                vec[row : row + 1, :] += jnp.sum(values, axis=0, keepdims=True)

        gather.start()
        for step in range(3, depth - 1):
            down_step(step)
        run2.middle()
        down_step(depth - 1)
        ups[0].start()
        gather.middle()
        gather.last()
        run2.last()
        gather.finish()
        run2.finish(mlp_sum)

        @row_loop(rows)
        def _(at):
            block_out[at, :] = low(mid[at, :] + (mlp_sum[at, :] + small[5:6, :]))

        for step in range(1, up_hops + 1):
            up_step(step)
        for copy in (*down_hops, *ups):
            copy.sent()

    return pl.pallas_call(
        kernel,
        out_shape=[
            wide_shape(8, width),
            wide_shape(rows, width),
            low_shape(8, rows, width),
            low_shape(rows, width),
            low_shape(*d_down.shape[1:]),
            low_shape(*d_up.shape[1:]),
        ],
        in_specs=[IN_VMEM] * 2 + [ANY] * 2 + [IN_VMEM] * 4 + [ANY] * 2,
        out_specs=[IN_VMEM, IN_VMEM, ANY, IN_VMEM, IN_VMEM, IN_VMEM],
        scratch_shapes=[
            low_vmem(4, rows, width),
            low_vmem(rows, width),
            *PlaneScatter.buffers(rows, width),
            low_vmem(4, rows, width),
            *PlaneScatter.buffers(rows, width),
            pltpu.VMEM((rows, width), jnp.float32),
            low_vmem(*activated.shape),
            low_vmem(*w_down.shape),
            low_vmem(depth - 2, *d_down.shape[1:]),
            low_vmem(max(up_hops - 1, 1), *d_up.shape[1:]),
            low_vmem(depth - 1, *d_down.shape[1:]),
            low_vmem(up_hops, *d_up.shape[1:]),
            pltpu.VMEM((rows, width), jnp.float32),
            *net_scratch(
                2 * PlaneScatter.remotes + PlaneGather.remotes + depth + up_hops,
                depth + up_hops + 3,
            ),
        ],
        compiler_params=comm_params(5),
        cost_estimate=lasts(95, 1 << 20),
    )(
        grad_hidden, w_up, activated, w_down, middle, own_cot, small, down_first, d_down, d_up
    )


def closing(depth, up_own, down_own, down_x, d_query, d_keyval, d_vec, out_own):
    kv_rows, kv_cols = d_keyval.shape[0] // depth, d_keyval.shape[1]

    def add2(into, other):
        add_rows(into, other, 16)

    def add3(into, other):
        for at in range(2):
            add_rows(into.at[at], other.at[at], 16)

    def kernel(
        up, down, down_x_in, query, kv, vec, out,
        up_all, down_all, query_all, kv_all, vec_all, out_all,
        query_lo, query_hi, kv_lo, kv_hi, vec_lo, vec_hi,
        up_got, query_got, vec_got, *sems,
    ):
        spot = Spot(depth)
        net = Net(*sems)
        z, y = spot.z, spot.y
        xc, on_x = spot.x * 2 + spot.c, (1 - spot.x) * 2 + spot.c
        def kv_part(at):
            return kv.at[pl.ds(pl.multiple_of(at * kv_rows, kv_rows), kv_rows)]

        run_query = LineScatter(net, spot, lambda at: query.at[at], query_lo, query_hi, add3)
        run_kv = LineScatter(net, spot, kv_part, kv_lo, kv_hi, add2)
        run_vec = LineScatter(net, spot, lambda at: vec.at[at], vec_lo, vec_hi, add3)
        y_up = net.remote(up.at[1 - y], up_got, spot.to_y)
        y_query = net.remote(query.at[z, 1 - y], query_got, spot.to_y)
        y_vec = net.remote(vec.at[z, 1 - y], vec_got, spot.to_y)
        dp_up = DpGather(net, spot, up.at[y], up_all.at[y])
        dp_up2 = DpGather(net, spot, up_got, up_all.at[1 - y])
        dp_query = DpGather(net, spot, query.at[z, y], query_all.at[y])
        dp_query2 = DpGather(net, spot, query_got, query_all.at[1 - y])
        dp_kv = DpGather(net, spot, kv_part(z), kv_all)
        dp_vec = DpGather(net, spot, vec.at[z, y], vec_all)
        dp_out = DpGather(net, spot, out, out_all)
        keep_down = [
            net.local(down, down_all.at[xc]),
            net.local(down_x_in, down_all.at[on_x]),
        ]
        down_moves = [
            net.remote(down, down_all.at[xc], spot.to_c, down_all.at[spot.x * 2 + 1 - spot.c]),
            net.remote(
                down_x_in,
                down_all.at[on_x],
                spot.to_c,
                down_all.at[(1 - spot.x) * 2 + 1 - spot.c],
            ),
        ]
        spot.barrier((spot.to_c, spot.to_x, spot.to_y), True)
        run_query.stage(0)
        run_vec.stage(0)
        run_kv.stage(0)
        y_up.start()
        dp_up.start()
        dp_out.start()
        for copy in (*down_moves, *keep_down):
            copy.start()
        for step in range(1, depth - 1):
            run_query.stage(step)
            run_vec.stage(step)
            run_kv.stage(step)
            if step == 1:
                y_up.got()
                dp_up2.start()
        run_query.total()
        y_query.start()
        dp_query.start()
        run_vec.total()
        y_vec.start()
        run_kv.total()
        dp_kv.start()
        dp_up.last()
        y_query.got()
        dp_query2.start()
        y_vec.got()
        y_vec.sent()
        add_rows(vec.at[z, y], vec_got, 16)
        dp_vec.start()
        dp_up2.last()
        dps = (dp_query, dp_out, dp_kv, dp_query2, dp_vec)
        for run in dps:
            run.last()
        for run in (dp_up, dp_up2, *dps):
            run.finish()
        for copy in down_moves:
            copy.got()
            copy.sent()
        for copy in keep_down:
            copy.wait()
        for run in (run_query, run_kv, run_vec):
            run.finish()
        for copy in (y_up, y_query):
            copy.sent()

    remotes = (
        3 * LineGather.remotes(depth)
        + 5
        + 7 * DpGather.remotes
    )
    one = depth - 1

    def twice(*dims):
        return [low_vmem(*dims)] * 2

    return pl.pallas_call(
        kernel,
        out_shape=[
            low_shape(2, 4, *up_own.shape[1:]),
            low_shape(4, *down_own.shape),
            low_shape(2, 4, *d_query.shape[2:]),
            low_shape(4, kv_rows, kv_cols),
            low_shape(4, *d_vec.shape[2:]),
            low_shape(4, *out_own.shape),
        ],
        in_specs=[IN_VMEM] * 7,
        out_specs=[ANY] * 6,
        scratch_shapes=[
            *twice(one, *d_query.shape[1:]),
            *twice(one, kv_rows, kv_cols),
            *twice(one, *d_vec.shape[1:]),
            low_vmem(*up_own.shape[1:]),
            low_vmem(*d_query.shape[2:]),
            low_vmem(*d_vec.shape[2:]),
            *net_scratch(remotes, 10),
        ],
        compiler_params=comm_params(2),
        cost_estimate=lasts(70, 1 << 20),
    )(up_own, down_own, down_x, d_query, d_keyval, d_vec, out_own)


def widen(depth, y_slow, up_all, query_all, down_all, out_all, kv_all):
    rows = up_all.shape[2]
    seg = up_all.shape[3] // depth
    head_cols = query_all.shape[3]
    down_rows, width = down_all.shape
    steps = rows // 32

    def kernel(up, query, down, out, kv, up_w, query_w, down_w, out_w, kv_w):
        for y in range(2):
            for xc in range(4):
                for z in range(depth):
                    owner = y * depth + z if y_slow else z * 2 + y
                    at = (owner * 4 + xc) * seg
                    up_w[:, at : at + seg] = wide(up[y, xc, :, z * seg : (z + 1) * seg])
                at = (y * 4 + xc if y_slow else xc * 2 + y) * head_cols
                query_w[:, at : at + head_cols] = wide(query[y, xc])
        down_w[...] = wide(down[...])
        out_w[...] = wide(out[...])
        kv_w[...] = wide(kv[...])

    def rows_of(array):
        return pl.BlockSpec((array.shape[0] // steps, array.shape[1]), lambda index: (index, 0))

    def blocks_of(array):
        return pl.BlockSpec((2, 4, 32, array.shape[3]), lambda index: (0, 0, index, 0))

    shapes = [
        wide_shape(rows, 8 * depth * seg),
        wide_shape(rows, width),
        wide_shape(down_rows, width),
        wide_shape(*out_all.shape),
        wide_shape(*kv_all.shape),
    ]
    return pl.pallas_call(
        kernel,
        grid=(steps,),
        in_specs=[
            blocks_of(up_all),
            blocks_of(query_all),
            rows_of(down_all),
            rows_of(out_all),
            rows_of(kv_all),
        ],
        out_specs=[rows_of(item) for item in shapes],
        out_shape=shapes,
        compiler_params=pltpu.CompilerParams(vmem_limit_bytes=VMEM_LIMIT),
    )(up_all, query_all, down_all, out_all, kv_all)


def build(mesh):
    fsdp_size = mesh.shape["fsdp"]
    depth = fsdp_size // 2
    y_slow = depth != 4
    owner_axes = ("y", "z") if y_slow else ("z", "y")

    def owner(z_at, y_at):
        return y_at * depth + z_at if y_slow else z_at * 2 + y_at

    def shards(
        tokens,
        cotangent,
        lengths,
        dealing,
        attn_gain,
        attn_shift,
        query_weight,
        query_bias,
        keyval_weight,
        value_bias,
        output_weight,
        output_bias,
        mlp_gain,
        mlp_shift,
        up_weight,
        up_bias,
        down_weight,
        down_bias,
    ):
        held, slot_len, width = tokens.shape
        my_z = lax.axis_index("z")
        my_y = lax.axis_index("y")
        my_xc = lax.axis_index("x") * 2 + lax.axis_index("c")
        member = my_y * 4 + my_xc
        rows_own = query_weight.shape[0]
        ff = up_weight.shape[1]
        ff_own = down_weight.shape[0]
        ff_seg = ff_own // 4
        out_seg = rows_own // 4
        head_cols = width // 8
        group_seqs = held * 4

        def plane_table(table):
            parts = [
                lax.dynamic_slice_in_dim(table, owner(my_z, y_at) * group_seqs, group_seqs)
                for y_at in range(2)
            ]
            return jnp.stack(parts)

        micro = 2 * 4 * MB
        dealt_here = (
            lax.dynamic_slice_in_dim(dealing, owner(my_z, my_y) * group_seqs, group_seqs)
            - owner(my_z, my_y) * group_seqs
        )
        holders = (dealt_here // held).reshape(4, held)
        slots = (dealt_here % held).reshape(4, held)
        slot_for = jnp.sum(jnp.where(holders == my_xc, slots, 0), axis=1)
        my_holders = lax.dynamic_index_in_dim(holders, my_xc, 0, keepdims=False)
        lens = plane_table(lengths).reshape(micro, SEATS)
        ends = jnp.concatenate([lens[:, :1], lens[:, :1] + lens[:, 1:]], axis=1)
        starts = ends - lens
        at = jnp.arange(PACK)
        inside = (at[None, :, None] >= starts[:, None, :]) & (at[None, :, None] < ends[:, None, :])
        row_valid = jnp.any(inside, axis=2)
        seat = jnp.sum(jnp.where(inside, jnp.arange(SEATS)[None, None, :], 0), axis=2)
        segment = jnp.where(row_valid, seat, -1)
        allowed = (
            (at[None, :, None] >= at[None, None, :])
            & (segment[:, :, None] == segment[:, None, :])
            & row_valid[:, None, :]
        )
        my_inside = lax.dynamic_slice_in_dim(inside, member * MB, MB)
        my_starts = lax.dynamic_slice_in_dim(starts, member * MB, MB)
        my_lens = lax.dynamic_slice_in_dim(lens, member * MB, MB).reshape(held)
        offset = at[None, :] - jnp.sum(jnp.where(my_inside, my_starts[:, None, :], 0), axis=2)
        from_dev = jnp.sum(
            jnp.where(my_inside, my_holders.reshape(MB, 1, SEATS), 0), axis=2
        )
        own_count = MB * PACK
        own_valid = jnp.any(my_inside, axis=2).reshape(own_count)[:, None]
        source_row = jnp.where(
            own_valid[:, 0], (from_dev * slot_len + offset).reshape(own_count), 0
        )

        def up_columns(y_at):
            cols = [
                lax.dynamic_slice_in_dim(
                    up_weight, owner(z_at, y_at) * ff_own + my_xc * ff_seg, ff_seg, axis=1
                )
                for z_at in range(depth)
            ]
            return low(jnp.concatenate(cols, axis=1))

        def head_base(y_at):
            return owner(my_xc * (depth // 4), y_at) * rows_own

        def query_columns(y_at):
            return low(lax.dynamic_slice_in_dim(query_weight, head_base(y_at), head_cols, axis=1))

        small_parts = [
            attn_gain,
            attn_shift,
            output_bias,
            mlp_gain,
            mlp_shift,
            down_bias,
            query_bias,
            up_bias,
            value_bias,
        ]
        sizes = [item.shape[0] for item in small_parts]
        begins = [sum(sizes[:index]) for index in range(len(sizes))]
        small_count = sum(sizes)
        small_size = 16 * rows_own
        small = sum(
            jnp.pad(item, (begin, small_size - begin - size))
            for item, begin, size in zip(small_parts, begins, sizes)
        )
        small = low(small).reshape(16, rows_own)
        down_own = low(lax.dynamic_slice_in_dim(down_weight, my_xc * ff_seg, ff_seg, axis=0))
        ring = [(index, (index + 1) % depth) for index in range(depth)]

        def ring_slot(buffer, piece, step):
            at = (my_z - step + depth) % depth
            return lax.dynamic_update_slice(
                buffer, piece[None], (at,) + (0,) * piece.ndim
            )

        down_hop_1 = lax.ppermute(down_own, "z", ring)
        flat = held * slot_len
        places = jnp.arange(flat)
        from_slot = jnp.repeat(slot_for, slot_len) * slot_len + places % slot_len
        sender = low(from_slot[:, None] == places[None, :])
        holder = low(places[:, None] == from_slot[None, :])
        chooser = low((source_row[:, None] == jnp.arange(flat)[None, :]) & own_valid)
        (
            own_low,
            own_cot,
            up_piece,
            small_rows,
            w_keyval,
            tokens_all,
            query_all,
            w_output,
        ) = opening(
            depth,
            owner,
            tokens,
            cotangent,
            sender,
            chooser,
            query_weight,
            keyval_weight,
            output_weight,
            small,
            up_columns(my_y),
            up_columns(1 - my_y),
        )
        w_output = w_output.reshape(head_cols, width)

        my_bias_q = lax.dynamic_slice(small_rows, (6, head_base(my_y)), (1, head_cols))
        bias_u = lax.dynamic_slice_in_dim(small_rows, 7 + my_xc, 1)
        bias_u = bias_u.reshape((2, depth, ff_seg) if y_slow else (depth, 2, ff_seg))
        my_bias_u = lax.dynamic_index_in_dim(
            bias_u, my_y, 0 if y_slow else 1, keepdims=False
        ).reshape(depth * ff_seg)
        bias_v = small_rows[11].reshape(fsdp_size, rows_own)[:, : HEAD // fsdp_size].reshape(HEAD)
        bias_kv = jnp.concatenate([jnp.zeros((HEAD,), jnp.float32), bias_v])

        def rows_in_order(gathered):
            if y_slow:
                gathered = jnp.transpose(gathered, (1, 0, 2, 3))
            return gathered.reshape(width, gathered.shape[-1])

        def rows_by_z(values):
            if y_slow:
                return jnp.transpose(
                    values.reshape(2, depth, rows_own, values.shape[-1]), (1, 0, 2, 3)
                )
            return values.reshape(depth, 2, rows_own, values.shape[-1])

        w_query = rows_in_order(query_all)
        (
            middle,
            normed_attn,
            query,
            keyval,
            attended,
            normed_mlp,
            cotangent_all,
            up_all,
            down_all,
            down_piece,
        ) = attend(
            depth,
            tokens_all,
            own_low,
            own_cot,
            w_query,
            w_keyval,
            w_output,
            my_bias_q,
            bias_kv[None],
            wide(allowed),
            small_rows,
            up_piece,
            down_own,
            down_hop_1,
        )
        normed_mlp = normed_mlp.reshape(micro * PACK, width)
        grad_mixed = cotangent_all.reshape(micro * PACK, width)
        for step in range(3, depth):
            down_piece = lax.ppermute(down_piece, "z", ring)
            down_all = ring_slot(down_all, down_piece, step)
        w_up = rows_in_order(up_all)
        hidden = product(normed_mlp, w_up) + my_bias_u
        activated, slope = gelu_parts(hidden)
        activated = low(activated)

        down_parts = low(product_rows(activated, grad_mixed)).reshape(depth, ff_seg, width)
        down_first = lax.ppermute(
            lax.dynamic_index_in_dim(down_parts, (my_z + depth - 1) % depth, 0, keepdims=False),
            "z",
            ring,
        )
        mixed_later, down_parts = lax.optimization_barrier((grad_mixed, down_parts))
        w_down = down_all.reshape(depth * ff_seg, width)
        grad_act = product_cols(mixed_later, w_down)
        grad_hidden = low(slope * grad_act)
        up_parts = rows_by_z(low(product_rows(normed_mlp, grad_hidden)))
        second_sums, grad_middle, grad_branch, block_own, d_down, d_up = mlp_back(
            depth,
            grad_hidden,
            w_up,
            activated,
            w_down,
            middle,
            own_cot,
            small_rows,
            down_first,
            down_parts,
            up_parts,
        )
        grad_flat = grad_branch.reshape(micro * PACK, width)
        for step in range(2, depth - 2):
            d_up = lax.ppermute(d_up, "z", ring)
            at = (my_z - 1 - step + 2 * depth) % depth
            term = lax.dynamic_index_in_dim(up_parts, at, 0, keepdims=False)
            d_up = low(wide(d_up) + wide(term))
        d_output = low(product_rows(attended, grad_flat))
        hits = my_holders[None, :] == jnp.arange(4)[:, None]
        seq_starts = (my_starts + jnp.arange(MB)[:, None] * PACK).reshape(held)
        send_lens = jnp.sum(jnp.where(hits, my_lens[None, :], 0), axis=1)
        send_starts = jnp.sum(jnp.where(hits, seq_starts[None, :], 0), axis=1)
        pos = jnp.arange(slot_len)
        live = pos[None, :] < send_lens[:, None]
        send_rows = jnp.where(live, send_starts[:, None] + pos[None, :], -1)
        back_chooser = low(send_rows.reshape(flat)[:, None] == jnp.arange(own_count)[None, :])
        d_out_parts = jnp.transpose(
            d_output.reshape(depth // 4, 4, out_seg, width), (1, 0, 2, 3)
        )
        grad_query, grad_keyval, first_sums, block_out, input_grad, out_own, d_up, down_x = attend_back(
            depth,
            grad_branch,
            query,
            keyval,
            wide(allowed),
            w_output,
            w_query,
            w_keyval,
            own_low,
            grad_middle,
            small_rows,
            block_own,
            back_chooser,
            holder,
            d_out_parts,
            d_up,
            up_parts,
            d_down,
        )
        d_query = low(product_rows(normed_attn, grad_query))
        grad_keyval = grad_keyval.reshape(micro * PACK, 2 * HEAD)
        d_keyval = low(product_rows(normed_attn, grad_keyval))
        own_keyval = lax.dynamic_slice_in_dim(grad_keyval, member * own_count, own_count)

        def colsum(values):
            return jnp.sum(wide(values), axis=0)

        def spread_vec(values, parts, size, full):
            out = jnp.zeros((full,), jnp.float32)
            for index, begin in enumerate(parts):
                out = lax.dynamic_update_slice(
                    out, values[index * size : (index + 1) * size], (begin,)
                )
            return out

        vec_query = spread_vec(colsum(grad_query), [head_base(my_y)], head_cols, width)
        vec_up = spread_vec(
            colsum(grad_hidden),
            [owner(z_at, my_y) * ff_own + my_xc * ff_seg for z_at in range(depth)],
            ff_seg,
            ff,
        )
        vectors = [
            first_sums[0],
            first_sums[1],
            second_sums[0],
            second_sums[1],
            second_sums[2],
            second_sums[3],
            vec_query,
            vec_up,
            colsum(own_keyval[:, HEAD:]),
        ]
        vectors = jnp.concatenate([item.reshape(fsdp_size, -1) for item in vectors], axis=1)
        vectors = jnp.pad(low(vectors), ((0, 0), (0, small_size - small_count)))
        if y_slow:
            d_vec = jnp.transpose(vectors.reshape(2, depth, 16, rows_own), (1, 0, 2, 3))
        else:
            d_vec = vectors.reshape(depth, 2, 16, rows_own)

        if y_slow:
            d_keyval = d_keyval.reshape(2, depth, 4, out_seg, 2 * HEAD)
            d_keyval = lax.dynamic_index_in_dim(d_keyval, my_y, 0, keepdims=False)
        else:
            d_keyval = d_keyval.reshape(depth, 2, 4, out_seg, 2 * HEAD)
            d_keyval = lax.dynamic_index_in_dim(d_keyval, my_y, 1, keepdims=False)
        d_keyval = lax.dynamic_index_in_dim(d_keyval, my_xc, 1, keepdims=False)
        d_keyval = d_keyval.reshape(depth * out_seg, 2 * HEAD)
        up_all, down_all, query_sum, kv_sum, vec_all, out_all = closing(
            depth, d_up, d_down, down_x, rows_by_z(d_query), d_keyval, d_vec, out_own
        )
        up_grad, query_grad, down_grad, output_grad, keyval_grad = widen(
            depth,
            y_slow,
            up_all,
            query_sum,
            down_all.reshape(ff_own, width),
            out_all.reshape(rows_own, width),
            kv_sum.reshape(rows_own, 2 * HEAD),
        )
        vec_own = jnp.sum(wide(vec_all), axis=0).reshape(small_size)
        (
            gain_a_grad,
            shift_a_grad,
            bias_o_grad,
            gain_m_grad,
            shift_m_grad,
            bias_d_grad,
            bias_q_grad,
            bias_u_grad,
            bias_v_grad,
        ) = [vec_own[start : start + size] for start, size in zip(begins, sizes)]

        return (
            block_out,
            input_grad,
            gain_a_grad,
            shift_a_grad,
            query_grad,
            bias_q_grad,
            keyval_grad,
            bias_v_grad,
            output_grad,
            bias_o_grad,
            gain_m_grad,
            shift_m_grad,
            up_grad,
            bias_u_grad,
            down_grad,
            bias_d_grad,
        )

    return shards, depth, owner_axes


def solution(mesh):
    shards, depth, owner_axes = build(mesh)
    sizes = {"z": depth, "y": 2}
    fine = Mesh(
        mesh.devices.reshape(sizes[owner_axes[0]], sizes[owner_axes[1]], 2, 2),
        owner_axes + ("x", "c"),
    )
    rows = P(owner_axes + ("x", "c"), None, None)
    vec = P(owner_axes)
    mat = P(owner_axes, None)
    in_specs = (
        rows, rows, P(), P(),
        vec, vec, mat, vec, mat, vec, mat, vec, vec, vec, mat, vec, mat, vec,
    )
    out_specs = (
        rows, rows,
        vec, vec, mat, vec, mat, vec, mat, vec, vec, vec, mat, vec, mat, vec,
    )
    return jax.shard_map(shards, mesh=fine, in_specs=in_specs, out_specs=out_specs, check_vma=False)
```

```python
import math

import jax
import jax.numpy as jnp
from jax import lax
from jax.experimental import pallas as pl
from jax.experimental.pallas import tpu as pltpu
from jax.sharding import Mesh
from jax.sharding import PartitionSpec as P

HEADS = 16
HEAD = 128
MB = 2
SEATS = 2
PACK = 80

epsilon = 1e-05
gelu_scale = 0.7978845608028654
gelu_cubic = 0.044715

DP = ("x", "c")


def low(values):
    return values.astype(jnp.bfloat16)


def wide(values):
    return values.astype(jnp.float32)


def product(left_mat, right_mat):
    return jnp.dot(left_mat, right_mat, preferred_element_type=jnp.float32)


def product_rows(left_mat, right_mat):
    return lax.dot_general(
        left_mat, right_mat, (((0,), (0,)), ((), ())), preferred_element_type=jnp.float32
    )


def product_cols(left_mat, right_mat):
    return lax.dot_general(
        left_mat, right_mat, (((1,), (1,)), ((), ())), preferred_element_type=jnp.float32
    )


def normalize(rows):
    center = rows - jnp.mean(rows, axis=-1, keepdims=True)
    spread = jnp.mean(center * center, axis=-1, keepdims=True)
    scale = lax.rsqrt(spread + epsilon)
    return center * scale, scale


def norm_back(grad_normed, gain, xhat, scale):
    g = grad_normed * gain
    inner = jnp.mean(g * xhat, axis=-1, keepdims=True)
    return scale * (g - jnp.mean(g, axis=-1, keepdims=True) - xhat * inner)


def gelu_parts(values):
    inner = jnp.tanh(gelu_scale * (values + gelu_cubic * values * values * values))
    activated = 0.5 * values * (1.0 + inner)
    slope = 0.5 * (1.0 + inner) + 0.5 * values * (1.0 - inner * inner) * gelu_scale * (
        1.0 + 3.0 * gelu_cubic * values * values
    )
    return activated, slope


MESH_ID = pl.DeviceIdType.MESH
VMEM_LIMIT = 56 * 1024 * 1024


class Spot:
    def __init__(self, depth):
        self.depth = depth
        self.z = lax.axis_index("z")
        self.y = lax.axis_index("y")
        self.x = lax.axis_index("x")
        self.c = lax.axis_index("c")
        self.to_c = {"c": 1 - self.c}
        self.to_x = {"x": 1 - self.x}
        self.to_y = {"y": 1 - self.y}
        self.to_xc = {"x": 1 - self.x, "c": 1 - self.c}
        self.up = {"z": self.z + 1}
        self.down = {"z": self.z - 1}

    def ring(self):
        before = {"z": lax.rem(self.z + self.depth - 1, self.depth)}
        return ({"z": lax.rem(self.z + 1, self.depth)}, before)

    def barrier(self, plane, line):
        bar = pltpu.get_barrier_semaphore()
        for to in plane:
            pl.semaphore_signal(bar, inc=1, device_id=to, device_id_type=MESH_ID)
        if line:

            @pl.when(self.z > 0)
            def _():
                pl.semaphore_signal(bar, inc=1, device_id=self.down, device_id_type=MESH_ID)

            @pl.when(self.z < self.depth - 1)
            def _():
                pl.semaphore_signal(bar, inc=1, device_id=self.up, device_id_type=MESH_ID)

        count = len(plane)
        if line:
            lower = jnp.where(self.z > 0, 1, 0)
            upper = jnp.where(self.z < self.depth - 1, 1, 0)
            count = count + lower + upper
        pl.semaphore_wait(bar, count)


class Net:
    def __init__(self, send_sems, recv_sems, local_sems):
        self.send_sems = send_sems
        self.recv_sems = recv_sems
        self.local_sems = local_sems
        self.count = 0
        self.local_count = 0
        self.open = []

    def remote(self, src, dst, to, arrives=None):
        copy = Copy(self, self.count, src, dst, to, arrives)
        self.count += 1
        return copy

    def local(self, src, dst):
        copy = pltpu.make_async_copy(src, dst, self.local_sems.at[self.local_count])
        self.local_count += 1
        return copy


class Copy:
    def __init__(self, net, index, src, dst, to, arrives):
        def make(target):
            return pltpu.make_async_remote_copy(
                src_ref=src,
                dst_ref=target,
                send_sem=net.send_sems.at[index],
                recv_sem=net.recv_sems.at[index],
                device_id=to,
                device_id_type=MESH_ID,
            )

        self.out = make(dst)
        self.into = make(dst if arrives is None else arrives)

    def start(self):
        self.out.start()

    def got(self):
        self.into.wait_recv()

    def sent(self):
        self.out.wait_send()


class PlaneGather:
    def __init__(self, net, spot, own, slots, share=2):
        def at(y, x, c):
            return y * 4 + x * 2 + c

        y, x, c = spot.y, spot.x, spot.c
        self.both = share == 2
        half = own.shape[0] // share
        lo, hi = pl.ds(0, half), pl.ds(half * (share - 1), half)
        me = at(y, x, c)
        on_x, on_y, on_d = at(y, 1 - x, c), at(1 - y, x, c), at(1 - y, 1 - x, c)
        peer = [at(y, x, 1 - c), at(y, 1 - x, 1 - c), at(1 - y, x, 1 - c), at(1 - y, 1 - x, 1 - c)]

        def slot(index):
            return slots.at[index]

        self.keep = net.local(own, slot(me))
        self.x = net.remote(own, slot(me), spot.to_x, slot(on_x))
        self.y = net.remote(own, slot(me), spot.to_y, slot(on_y))
        self.c = net.remote(own, slot(me), spot.to_c, slot(peer[0]))
        self.x_on_y = net.remote(
            slots.at[on_x, lo], slots.at[on_x, lo], spot.to_y, slots.at[on_d, lo]
        )
        self.x_on_c = net.remote(slot(on_x), slot(on_x), spot.to_c, slot(peer[1]))
        self.y_on_c = net.remote(slot(on_y), slot(on_y), spot.to_c, slot(peer[2]))
        self.lo_on_c = net.remote(
            slots.at[on_d, lo], slots.at[on_d, lo], spot.to_c, slots.at[peer[3], lo]
        )
        if self.both:
            self.y_on_x = net.remote(
                slots.at[on_y, hi], slots.at[on_y, hi], spot.to_x, slots.at[on_d, hi]
            )
            self.hi_on_c = net.remote(
                slots.at[on_d, hi], slots.at[on_d, hi], spot.to_c, slots.at[peer[3], hi]
            )

    def start(self):
        self.x.start()
        self.y.start()
        self.c.start()
        self.keep.start()

    def middle(self):
        self.x.got()
        self.x_on_y.start()
        self.x_on_c.start()
        self.y.got()
        if self.both:
            self.y_on_x.start()
        self.y_on_c.start()

    def last(self):
        self.x_on_y.got()
        self.lo_on_c.start()
        if self.both:
            self.y_on_x.got()
            self.hi_on_c.start()

    def finish(self):
        second = (self.y_on_x, self.hi_on_c) if self.both else ()
        for copy in (self.c, self.x_on_c, self.y_on_c, self.lo_on_c, *second[1:]):
            copy.got()
        firsts = (self.x, self.y, self.c, self.x_on_y, self.x_on_c, self.y_on_c, self.lo_on_c)
        for copy in (*firsts, *second):
            copy.sent()
        self.keep.wait()

    remotes = 9
    locals = 1


def add_rows(into, other, step=32):
    rows = into.shape[0]

    @pl.loop(0, rows // step)
    def _(index):
        at = pl.ds(pl.multiple_of(index * step, step), step)
        into[at, :] = low(wide(into[at, :]) + wide(other[at, :]))


class PlaneScatter:
    remotes = 10

    @staticmethod
    def buffers(rows, width):
        return [
            pltpu.VMEM((4, rows, width), jnp.bfloat16),
            pltpu.VMEM((rows, width), jnp.bfloat16),
            pltpu.VMEM((rows, width), jnp.bfloat16),
            pltpu.VMEM((rows, width), jnp.bfloat16),
        ]

    def __init__(self, net, spot, parts, sums, diag, from_x, from_y, share=2):
        y, x, c = spot.y, spot.x, spot.c
        self.both = share == 2
        half = parts.shape[1] // share
        lo, hi = pl.ds(0, half), pl.ds(half * (share - 1), half)
        self.own, self.nx, self.ny, self.nd = (
            y * 2 + x,
            y * 2 + 1 - x,
            (1 - y) * 2 + x,
            (1 - y) * 2 + 1 - x,
        )
        self.parts, self.sums, self.diag = parts, sums, diag
        self.stacked = parts.shape[0] == 4
        self.from_x, self.from_y, self.c = from_x, from_y, c
        self.lo, self.hi = lo, hi
        self.first = {
            key: net.remote(
                parts.at[at] if self.stacked else parts.at[at * 2 + 1 - c], sums.at[at], spot.to_c
            )
            for key, at in (("d", self.nd), ("x", self.nx), ("y", self.ny), ("o", self.own))
        }
        self.d_hi = net.remote(sums.at[self.nd, hi], diag.at[hi], spot.to_y)
        self.y_hi = net.remote(sums.at[self.ny, hi], from_y.at[hi], spot.to_y)
        self.x_hi = net.remote(sums.at[self.nx, hi], from_x.at[hi], spot.to_x)
        if self.both:
            self.d_lo = net.remote(sums.at[self.nd, lo], diag.at[lo], spot.to_x)
            self.x_lo = net.remote(sums.at[self.nx, lo], from_x.at[lo], spot.to_x)
            self.y_lo = net.remote(sums.at[self.ny, lo], from_y.at[lo], spot.to_y)

    def start(self):
        for copy in self.first.values():
            copy.start()

    def give(self, key, at):
        if self.stacked:
            self.send(at, at * 2 + 1 - self.c)
            self.first[key].start()

    def pair(self, key, at):
        if self.stacked:
            self.prepare(at * 2 + self.c)
            self.first[key].got()
            self.merge(at * 2 + self.c, at)
        else:
            self.first[key].got()
            add_rows(self.sums.at[at], self.parts.at[at * 2 + self.c])

    def middle(self):
        self.give("d", self.nd)
        self.give("x", self.nx)
        self.pair("d", self.nd)
        if self.both:
            self.d_lo.start()
        self.d_hi.start()
        self.give("y", self.ny)
        self.pair("x", self.nx)
        if self.both:
            self.x_lo.start()
        self.give("o", self.own)
        self.pair("y", self.ny)
        self.y_hi.start()
        self.pair("o", self.own)

    def last(self):
        if self.both:
            self.d_lo.got()
            add_rows(self.sums.at[self.ny, self.lo], self.diag.at[self.lo], 16)
            self.y_lo.start()
        self.d_hi.got()
        add_rows(self.sums.at[self.nx, self.hi], self.diag.at[self.hi], 16)
        self.x_hi.start()

    def finish(self, result):
        second = (self.x_lo, self.y_lo) if self.both else ()
        for copy in (self.y_hi, self.x_hi, *second):
            copy.got()

        @pl.loop(0, result.shape[0] // 16)
        def _(index):
            at = pl.ds(pl.multiple_of(index * 16, 16), 16)
            result[at, :] = (
                wide(self.sums[self.own, at, :]) + wide(self.from_x[at, :]) + wide(self.from_y[at, :])
            )

        for copy in (
            *self.first.values(),
            self.d_hi,
            self.x_hi,
            self.y_hi,
            *((self.d_lo, *second) if self.both else ()),
        ):
            copy.sent()


class LineGather:
    def __init__(self, net, spot, slots, moves=None):
        self.spot, depth, z = spot, spot.depth, spot.z
        self.moves = moves
        self.hops = []
        for step in range(depth - 1):
            lower = jnp.maximum(z - step, 0)
            upper = jnp.minimum(z + step, depth - 1)
            from_low = jnp.maximum(z - 1 - step, 0)
            from_high = jnp.minimum(z + 1 + step, depth - 1)
            self.hops.append(
                (
                    net.remote(slots(lower), slots(lower), spot.up, slots(from_low)),
                    net.remote(slots(upper), slots(upper), spot.down, slots(from_high)),
                )
            )

    @staticmethod
    def remotes(depth):
        return 2 * (depth - 1)

    def pick(self, cond, slot):
        return cond if self.moves is None else cond & self.moves(slot)

    def sends(self, step):
        z, last = self.spot.z, self.spot.depth - 1
        return (
            (self.pick((z >= step) & (z < last), z - step), self.hops[step][0]),
            (self.pick((z + step <= last) & (z > 0), z + step), self.hops[step][1]),
        )

    def takes(self, step):
        z, last = self.spot.z, self.spot.depth - 1
        return (
            (self.pick(z >= step + 1, z - 1 - step), self.hops[step][0]),
            (self.pick(z + step + 1 <= last, z + 1 + step), self.hops[step][1]),
        )

    def start(self, step):
        for cond, copy in self.sends(step):
            pl.when(cond)(copy.start)

    def got(self, step):
        for cond, copy in self.takes(step):
            pl.when(cond)(copy.got)

    def hop(self, step):
        for (came, old), (goes, new) in zip(self.takes(step - 1), self.sends(step)):
            pl.when(came)(old.got)
            pl.when(goes)(new.start)

    def finish(self):
        for step in range(self.spot.depth - 1):
            for cond, copy in self.sends(step):
                pl.when(cond)(copy.sent)


class LineScatter:
    def __init__(self, net, spot, parts, from_low, from_high, add):
        self.net, self.spot, self.parts, self.add = net, spot, parts, add
        self.boxes = (from_low, from_high)
        self.first = net.count
        net.count += 2 * (spot.depth - 1)

    @staticmethod
    def remotes(depth):
        return 2 * (depth - 1)

    def copy(self, side, message):
        last = self.spot.depth - 1
        slot = self.parts(last - message if side == 0 else message)
        at = self.first + side * last + message
        copy = pltpu.make_async_remote_copy(
            src_ref=slot,
            dst_ref=self.boxes[side].at[message],
            send_sem=self.net.send_sems.at[at],
            recv_sem=self.net.recv_sems.at[at],
            device_id=(self.spot.up, self.spot.down)[side],
            device_id_type=MESH_ID,
        )
        return copy, slot, self.boxes[side].at[message]

    def take(self, side, message):
        copy, slot, box = self.copy(side, message)
        copy.wait_recv()
        self.add(slot, box)

    def place(self, side):
        return self.spot.z if side == 0 else self.spot.depth - 1 - self.spot.z

    def stage(self, step):
        for side in range(2):
            behind = self.place(side)

            @pl.when(behind <= step)
            def _():
                message = step - behind

                @pl.when(behind > 0)
                def _():
                    self.take(side, message)

                self.copy(side, message)[0].start()

    def total(self):
        last = self.spot.depth - 1
        for side in range(2):
            behind = self.place(side)

            @pl.when(behind > 0)
            def _():
                self.take(side, last - behind)

    def finish(self):
        for side in range(2):
            behind = self.place(side)
            for message in range(self.spot.depth - 1):

                @pl.when(behind + message < self.spot.depth - 1)
                def _():
                    self.copy(side, message)[0].wait_send()


class DpGather:
    remotes = 3

    def __init__(self, net, spot, own, slots):
        me = spot.x * 2 + spot.c
        on_x = (1 - spot.x) * 2 + spot.c
        self.keep = net.local(own, slots.at[me])
        self.x = net.remote(own, slots.at[me], spot.to_x, slots.at[on_x])
        self.c = net.remote(own, slots.at[me], spot.to_c, slots.at[spot.x * 2 + 1 - spot.c])
        self.x_on_c = net.remote(
            slots.at[on_x],
            slots.at[on_x],
            spot.to_c,
            slots.at[(1 - spot.x) * 2 + 1 - spot.c],
        )

    def start(self):
        self.x.start()
        self.c.start()
        self.keep.start()

    def last(self):
        self.x.got()
        self.x_on_c.start()

    def finish(self):
        self.c.got()
        self.x_on_c.got()
        for copy in (self.x, self.c, self.x_on_c):
            copy.sent()
        self.keep.wait()


class DpExchange:
    remotes = 3

    def __init__(self, net, spot, parts, slots):
        me = spot.x * 2 + spot.c
        on_x = (1 - spot.x) * 2 + spot.c
        on_c = spot.x * 2 + 1 - spot.c
        on_xc = (1 - spot.x) * 2 + 1 - spot.c
        self.keep = net.local(parts.at[me], slots.at[me])
        self.moves = [
            net.remote(parts.at[at], slots.at[me], to, slots.at[at])
            for at, to in ((on_xc, spot.to_xc), (on_x, spot.to_x), (on_c, spot.to_c))
        ]

    def start(self):
        for copy in self.moves:
            copy.start()
        self.keep.start()

    def got(self):
        for copy in self.moves:
            copy.got()
        self.keep.wait()

    def finish(self):
        for copy in self.moves:
            copy.sent()


def net_scratch(remotes, locals_):
    return [
        pltpu.SemaphoreType.DMA((remotes,)),
        pltpu.SemaphoreType.DMA((remotes,)),
        pltpu.SemaphoreType.DMA((max(locals_, 1),)),
    ]


ANY = pl.BlockSpec(memory_space=pl.ANY)
IN_VMEM = pl.BlockSpec(memory_space=pltpu.VMEM)


def lasts(micros, moved):
    return pl.CostEstimate(
        flops=int(micros * 1e9), bytes_accessed=int(moved), transcendentals=0
    )


def comm_params(collective_id):
    return pltpu.CompilerParams(
        collective_id=collective_id, has_side_effects=True, vmem_limit_bytes=VMEM_LIMIT
    )


def low_shape(*dims):
    return jax.ShapeDtypeStruct(dims, jnp.bfloat16)


def wide_shape(*dims):
    return jax.ShapeDtypeStruct(dims, jnp.float32)


def low_vmem(*dims):
    return pltpu.VMEM(dims, jnp.bfloat16)


def pick_rows(chooser, source, result, step=512):
    width = result.shape[-1]

    @pl.loop(0, width // step)
    def _(index):
        at = pl.ds(pl.multiple_of(index * step, step), step)
        rows = source[..., at].reshape(chooser.shape[1], step)
        result[..., at] = low(product(chooser[...], rows)).reshape(*result.shape[:-1], step)


def opening(depth, owner, tokens, cotangent, sender, chooser, query_weight, keyval_weight, output_weight, small, up_mine, up_other):
    rows = chooser.shape[0]
    width = tokens.shape[-1]
    group = depth // 4
    rows_own = query_weight.shape[0]
    head_cols = width // 8
    kv_rows = rows_own // 4
    kv_cols = keyval_weight.shape[1]

    def kernel(
        tok_held, cot_held, send, choose, query_w, kv_w, out_w, small_m, up_m, up_o,
        own_tok, own_cot, up_own, small_rows, w_keyval,
        tok_all, query_all, out_all,
        kv_all, small_all, tok, cot, tok_got, cot_got, out_v, kv_line, query_m, query_o, query_y, small_y,
        query_f, out_f, kv_f, *sems,
    ):
        spot = Spot(depth)
        net = Net(*sems)
        z, y = spot.z, spot.y
        xc = spot.x * 2 + spot.c
        source = z // group == xc

        def head_base(y_at):
            return pl.multiple_of(owner(xc * group, y_at) * rows_own, 128)

        def strip(ref, size):
            return ref.at[pl.ds(pl.multiple_of(xc * size, size), size)]

        def z_slot(at):
            return kv_line.at[pl.ds(pl.multiple_of(at * kv_rows, kv_rows), kv_rows)]

        read_query_o = net.local(query_w.at[:, pl.ds(head_base(1 - y), head_cols)], query_f.at[0])
        read_out = net.local(out_w, out_f)
        read_kv = net.local(strip(kv_w, kv_rows), kv_f)
        read_query = net.local(query_w.at[:, pl.ds(head_base(y), head_cols)], query_f.at[1])
        tok_deal = DpExchange(net, spot, tok, tok_got)
        cot_deal = DpExchange(net, spot, cot, cot_got)
        tok_run = PlaneGather(net, spot, own_tok, tok_all)
        kv_run = PlaneGather(net, spot, kv_line, kv_all)
        y_query = net.remote(query_o, query_y, spot.to_y)
        y_small = net.remote(small_m, small_y, spot.to_y)
        y_up = net.remote(up_o, up_own.at[y], spot.to_y, up_own.at[1 - y])
        keep_query = net.local(query_m, query_all.at[z, y])
        keep_query_y = net.local(query_y, query_all.at[z, 1 - y])
        keep_out = net.local(out_v, out_all)
        run_kv = LineGather(net, spot, z_slot)
        run_query = LineGather(net, spot, lambda at: query_all.at[at])
        run_small = LineGather(net, spot, lambda at: small_all.at[at])

        def piece_of_out(piece):
            rows_at = pl.ds(piece * kv_rows, kv_rows)
            return LineGather(
                net,
                spot,
                lambda at: out_v.at[at % group, rows_at],
                lambda at: at // group == xc,
            )

        run_outs = [piece_of_out(piece) for piece in range(4)]
        read_query_o.start()
        pl.when(source)(read_out.start)
        read_kv.start()
        read_query.start()
        small_all[z, y] = small_m[...]
        spot.barrier((spot.to_c, spot.to_x, spot.to_y, spot.to_xc), True)
        pick_rows(send, tok_held, tok)
        tok_deal.start()
        read_query_o.wait()
        query_o[...] = low(query_f[0])
        y_query.start()
        y_small.start()
        y_up.start()

        @pl.when(source)
        def _():
            read_out.wait()

            @pl.loop(0, rows_own // 16)
            def _(index):
                at = pl.ds(pl.multiple_of(index * 16, 16), 16)
                out_v[z % group, at, :] = low(out_f[at, :])

        for run in run_outs:
            run.start(0)
        read_kv.wait()
        z_slot(z)[...] = low(kv_f[...])
        run_kv.start(0)
        read_query.wait()
        query_m[...] = low(query_f[1])
        keep_query.start()
        keep_query.wait()
        y_query.got()
        keep_query_y.start()
        y_small.got()
        small_all[z, 1 - y] = small_y[...]
        keep_query_y.wait()
        run_query.start(0)
        run_small.start(0)
        pick_rows(send, cot_held, cot)

        @pl.loop(0, rows_own // 16)
        def _(index):
            at = pl.ds(pl.multiple_of(index * 16, 16), 16)
            up_own[y, at, :] = up_m[at, :]

        tok_deal.got()
        pick_rows(choose, tok_got, own_tok)
        tok_run.start()
        cot_deal.start()
        for step in range(1, depth - 1):
            for run in run_outs:
                run.hop(step)
            run_kv.hop(step)
        run_query.hop(1)
        run_small.hop(1)
        run_kv.got(depth - 2)
        kv_run.start()
        for step in range(2, depth - 1):
            run_query.hop(step)
            run_small.hop(step)
        tok_run.middle()
        kv_run.middle()
        cot_deal.got()
        pick_rows(choose, cot_got, own_cot)
        tok_run.last()
        kv_run.last()
        for run in run_outs:
            run.got(depth - 2)
        keep_out.start()
        run_query.got(depth - 2)
        run_small.got(depth - 2)
        for z_at in range(depth):
            for y_at in range(2):
                at = owner(z_at, y_at) * rows_own
                small_rows[:, at : at + rows_own] = wide(small_all[z_at, y_at])
        y_up.got()
        runs = (*run_outs, run_kv, run_query, run_small, tok_run, kv_run)
        for run in (*runs, tok_deal, cot_deal):
            run.finish()
        for y_at in range(2):
            for xc_at in range(4):
                for z_at in range(depth):
                    at = owner(z_at, y_at) * rows_own + xc_at * kv_rows
                    w_keyval[at : at + kv_rows, :] = kv_all[
                        y_at * 4 + xc_at, z_at * kv_rows : (z_at + 1) * kv_rows, :
                    ]
        for copy in (y_query, y_small, y_up):
            copy.sent()
        keep_out.wait()

    remotes = (
        2 * DpExchange.remotes + 2 * PlaneGather.remotes + 4 + 7 * LineGather.remotes(depth)
    )
    operands = (
        tokens, cotangent, sender, chooser, query_weight, keyval_weight, output_weight, small,
        up_mine, up_other,
    )
    wide_type = jnp.float32
    return pl.pallas_call(
        kernel,
        out_shape=[
            low_shape(rows, width),
            low_shape(rows, width),
            low_shape(2, *up_mine.shape),
            wide_shape(small.shape[0], width),
            low_shape(width, kv_cols),
            low_shape(8, rows, width),
            low_shape(depth, 2, rows_own, head_cols),
            low_shape(group, rows_own, width),
        ],
        in_specs=[IN_VMEM] * 4 + [ANY] * 3 + [IN_VMEM] * 3,
        out_specs=[IN_VMEM] * 5 + [ANY] * 3,
        scratch_shapes=[
            low_vmem(8, depth * kv_rows, kv_cols),
            low_vmem(depth, 2, *small.shape),
            *[low_vmem(*tokens.shape)] * 4,
            low_vmem(group, rows_own, width),
            low_vmem(depth * kv_rows, kv_cols),
            low_vmem(rows_own, head_cols),
            low_vmem(rows_own, head_cols),
            low_vmem(rows_own, head_cols),
            low_vmem(*small.shape),
            pltpu.VMEM((2, rows_own, head_cols), wide_type),
            pltpu.VMEM((rows_own, width), wide_type),
            pltpu.VMEM((kv_rows, kv_cols), wide_type),
            *net_scratch(remotes, 20),
        ],
        compiler_params=comm_params(1),
        cost_estimate=lasts(75, 1 << 20),
    )(*operands)


ROWS_STEP = 32


def row_loop(count):
    def decorate(body):
        @pl.loop(0, count // ROWS_STEP)
        def _(index):
            body(pl.ds(pl.multiple_of(index * ROWS_STEP, ROWS_STEP), ROWS_STEP))

    return decorate


class Loads:
    def __init__(self, net, far, near):
        self.net, self.far, self.near = net, far, near
        self.first = net.local_count
        net.local_count += 8

    def copy(self, member):
        return pltpu.make_async_copy(
            self.far.at[member], self.near.at[member], self.net.local_sems.at[self.first + member]
        )

    def start(self, spot):
        def at(y, x, c):
            return y * 4 + x * 2 + c

        y, x, c = spot.y, spot.x, spot.c
        for y_at, x_at in ((1 - y, 1 - x), (y, 1 - x), (1 - y, x), (y, x)):
            for c_at in (1 - c, c):
                self.copy(at(y_at, x_at, c_at)).start()

    def wait(self, member):
        self.copy(member).wait()


def feed_blocks(run, parts, block, prepare=None):
    width = parts.shape[-1]

    def columns(body):
        @pl.loop(0, width // 512)
        def _(index):
            body(pl.ds(pl.multiple_of(index * 512, 512), 512))

    def ready(member):
        if prepare is not None:
            prepare(member)

    def send(at, member):
        ready(member)

        @columns
        def _(cols):
            parts[at, :, cols] = low(block(member, cols))

    def merge(member, at):
        @columns
        def _(cols):
            run.sums[at, :, cols] = low(wide(run.sums[at, :, cols]) + block(member, cols))

    run.send, run.merge, run.prepare = send, merge, ready


SCORE_SCALE = 1.0 / math.sqrt(HEAD)


def stacked(values):
    return jnp.concatenate([values[:, :HEAD], values[:, HEAD:]], axis=0)


def unstacked(values):
    half = values.shape[0] // 2
    return jnp.concatenate([values[:half], values[half:]], axis=1)


def softmax_of(query_2, keys, allowed):
    scores = product_cols(query_2, keys) * SCORE_SCALE
    scores = jnp.where(jnp.concatenate([allowed, allowed], axis=0) > 0.0, scores, -1e30)
    exps = jnp.exp(scores - jnp.max(scores, axis=-1, keepdims=True))
    return exps / jnp.sum(exps, axis=-1, keepdims=True)


def attend(depth, owner, tok_all, own_tok, own_cot, w_query, w_keyval, w_output, allowed, small, up_own, down_own, down_1):
    rows, width = own_tok.shape
    total = 8 * rows
    head_cols = w_query.shape[1]
    micros = rows // PACK

    def kernel(
        tok_far, tok, cot, w_q, w_kv, w_out, allow, small,
        up, down, down_b,
        middle, normed_a, query, keyval, attended, normed_all, cot_all, up_all, down_all,
        tok_near, b_kv, parts, normed, sums, diag, from_x, from_y, *sems,
    ):
        spot = Spot(depth)
        net = Net(*sems)
        z = spot.z
        run = PlaneScatter(net, spot, parts, sums, diag, from_x, from_y)
        gather = PlaneGather(net, spot, normed, normed_all)
        cot_run = PlaneGather(net, spot, cot, cot_all, share=1)
        after, _ = spot.ring()

        def behind(step):
            return lax.rem(z + 2 * depth - step, depth)

        keeps = [
            net.local(up, up_all.at[z]),
            net.local(down, down_all.at[z]),
            net.local(down_b, down_all.at[behind(1)]),
        ]
        ups = [net.remote(up, up_all.at[z], after, up_all.at[behind(1)])]
        for step in range(2, depth):
            at = up_all.at[behind(step - 1)]
            ups.append(net.remote(at, at, after, up_all.at[behind(step)]))

        xc = spot.x * 2 + spot.c
        group = depth // 4
        rows_own = width // (2 * depth)
        head_base = pl.multiple_of(owner(xc * group, spot.y) * rows_own, 128)

        tok_loads = Loads(net, tok_far, tok_near)

        def one_member(member):
            tok_loads.wait(member)
            first = pl.multiple_of(member * rows, rows)

            @pl.loop(0, rows // ROWS_STEP)
            def _(index):
                at = pl.multiple_of(index * ROWS_STEP, ROWS_STEP)
                xhat, _ = normalize(wide(tok_near[member, pl.ds(at, ROWS_STEP), :]))
                normed_a[pl.ds(first + at, ROWS_STEP), :] = low(xhat * small[0:1, :] + small[1:2, :])

            rows_at = pl.ds(first, rows)
            query[rows_at, :] = low(
                product(normed_a[rows_at, :], w_q[...])
                + small[6:7, pl.ds(head_base, head_cols)]
            )
            keyval[rows_at, :] = low(product(normed_a[rows_at, :], w_kv[...]) + b_kv[...])

            for index in range(micros):
                at = pl.ds(pl.multiple_of(first + index * PACK, PACK), PACK)
                pair = keyval[at, :]
                probs = softmax_of(
                    stacked(query[at, :]), pair[:, :HEAD], allow[member * micros + index]
                )
                attended[at, :] = low(unstacked(product(low(probs), pair[:, HEAD:])))

        def block(member, cols):
            rows_at = pl.ds(pl.multiple_of(member * rows, rows), rows)
            return product(attended[rows_at, :], w_out[:, cols])

        tok_loads.start(spot)
        each = HEAD // (2 * depth)
        lane = lax.broadcasted_iota(jnp.int32, (1, HEAD), 1)
        values = jnp.zeros((1, HEAD), jnp.float32)
        for at in range(2 * depth):
            begin = at * rows_own // HEAD * HEAD
            found = pltpu.roll(
                small[11:12, begin : begin + HEAD], (at * each - at * rows_own + begin) % HEAD, 1
            )
            values = jnp.where((lane >= at * each) & (lane < (at + 1) * each), found, values)
        b_kv[:, :HEAD] = jnp.zeros((1, HEAD), jnp.float32)
        b_kv[:, HEAD:] = values
        for copy in keeps:
            copy.start()
        spot.barrier((spot.to_c, spot.to_x, spot.to_y, *spot.ring()), False)
        ups[0].start()
        cot_run.start()
        feed_blocks(run, parts, block, one_member)
        run.middle()
        cot_run.middle()
        ups[0].got()
        ups[1].start()
        run.last()
        cot_run.last()
        run.finish(middle)

        @row_loop(rows)
        def _(at):
            total_rows = wide(tok[at, :]) + (middle[at, :] + small[2:3, :])
            middle[at, :] = total_rows
            xhat, _ = normalize(total_rows)
            normed[at, :] = low(xhat * small[3:4, :] + small[4:5, :])

        gather.start()
        for step in range(2, depth - 1):
            ups[step - 1].got()
            ups[step].start()
        gather.middle()
        gather.last()
        gather.finish()
        cot_run.finish()
        ups[-1].got()
        for copy in ups:
            copy.sent()
        for copy in keeps:
            copy.wait()

    return pl.pallas_call(
        kernel,
        out_shape=[
            wide_shape(rows, width),
            low_shape(total, width),
            low_shape(total, head_cols),
            low_shape(total, 2 * HEAD),
            low_shape(total, head_cols),
            low_shape(8, rows, width),
            low_shape(8, rows, width),
            low_shape(depth, *up_own.shape),
            low_shape(depth, *down_own.shape),
        ],
        in_specs=[ANY] + [IN_VMEM] * 10,
        out_specs=[IN_VMEM] * 5 + [ANY] * 4,
        scratch_shapes=[
            low_vmem(8, rows, width),
            pltpu.VMEM((1, 2 * HEAD), jnp.float32),
            low_vmem(4, rows, width),
            low_vmem(rows, width),
            *PlaneScatter.buffers(rows, width),
            *net_scratch(PlaneScatter.remotes + 2 * PlaneGather.remotes + depth, 14),
        ],
        compiler_params=comm_params(3),
        cost_estimate=lasts(90, 1 << 20),
    )(
        tok_all, own_tok, own_cot, w_query, w_keyval, w_output, allowed, small,
        up_own, down_own, down_1,
    )


def attend_back(depth, branch_all, query, keyval, allowed, w_output, w_query, w_keyval, own_tok, grad_middle, gain, block, chooser, holder, d_out, up_sum, up_parts, down_sum):
    group = depth // 4
    rows, width = own_tok.shape
    total, head_cols = query.shape
    micros = rows // PACK
    slots = chooser.shape[0] // 4

    def kernel(
        branch_far, q_all, kv_all, allow, w_out, w_q, w_kv, tok, grad_mid, small, block_own, choose, hold,
        out, du, dd, du_far,
        grad_q, kv_rows_all, vec, block_res, grad_res, out_sum, du_sum, dd_x,
        parts, sums, diag, from_x, from_y, first, grad_low, block_send, grad_send, block_got, grad_got,
        branch, out_mix, out_lo, out_hi, du_term, du_mid,
        grad_kv, kv_sums, kv_diag, kv_from_x, kv_from_y, kv_wide, kv_own, *sems,
    ):
        spot = Spot(depth)
        net = Net(*sems)
        run = PlaneScatter(net, spot, parts, sums, diag, from_x, from_y, share=1)
        down_over = net.remote(dd, dd_x, spot.to_x)
        z = spot.z
        after, _ = spot.ring()
        deal = DpExchange(net, spot, out, out_mix)

        def mixed(at):
            return out_mix.at[at // group, at % group]

        def add2(into, other):
            add_rows(into, other, 16)

        kv_run = PlaneScatter(net, spot, grad_kv, kv_sums, kv_diag, kv_from_x, kv_from_y)
        kv_gather = PlaneGather(net, spot, kv_own, kv_rows_all)
        run_out = LineScatter(net, spot, mixed, out_lo, out_hi, add2)
        hops = [net.remote(du, du_mid, after), net.remote(du_mid, du_sum, after)]
        terms = [
            net.local(du_far.at[lax.rem(z + 1, depth)], du_term.at[0]),
            net.local(du_far.at[z], du_term.at[1]),
        ]

        def up_step(step):
            into = (du_mid, du_sum)[step]
            hops[step].got()
            terms[step].wait()
            for at in range(2):
                add_rows(into.at[at], du_term.at[step, at], 32)
            if step == 0:
                hops[1].start()

        back_block = DpExchange(net, spot, block_send, block_got)
        back_grad = DpExchange(net, spot, grad_send, grad_got)

        branch_loads = Loads(net, branch_far, branch)

        def one_member(member):
            branch_loads.wait(member)
            begin = pl.multiple_of(member * rows, rows)
            grad_att = low(product_cols(branch[member], w_out[...]))
            for index in range(micros):
                at = pl.ds(pl.multiple_of(begin + index * PACK, PACK), PACK)
                pair = kv_all[at, :]
                keys, vals = pair[:, :HEAD], pair[:, HEAD:]
                q_2 = stacked(q_all[at, :])
                g_2 = stacked(grad_att[index * PACK : (index + 1) * PACK])
                probs = softmax_of(q_2, keys, allow[member * micros + index])
                grad_probs = product_cols(g_2, vals)
                inner = jnp.sum(probs * grad_probs, axis=-1, keepdims=True)
                grad_scores = low(probs * (grad_probs - inner))
                grad_q[at, :] = low(unstacked(product(grad_scores, keys) * SCORE_SCALE))
                grad_k = product_rows(grad_scores, q_2) * SCORE_SCALE
                grad_v = product_rows(low(probs), g_2)
                grad_kv[member, index * PACK : (index + 1) * PACK, :] = low(
                    jnp.concatenate([grad_k, grad_v], axis=1)
                )

        def block_of(member, cols):
            rows_at = pl.ds(pl.multiple_of(member * rows, rows), rows)
            return product_cols(grad_q[rows_at, :], w_q[cols, :]) + product_cols(
                grad_kv[member], w_kv[cols, :]
            )

        branch_loads.start(spot)
        for copy in terms:
            copy.start()
        spot.barrier((spot.to_c, spot.to_x, spot.to_y, spot.to_xc, *spot.ring()), False)
        deal.start()
        hops[0].start()
        down_over.start()
        pick_rows(choose, block_own, block_send)
        feed_blocks(run, parts, block_of, one_member)
        run.middle()
        kv_run.start()
        deal.got()
        run_out.stage(0)
        up_step(0)
        kv_run.middle()
        run.last()
        run_out.stage(1)
        kv_run.last()
        run.finish(first)
        kv_run.finish(kv_wide)
        back_block.start()
        kv_own[...] = low(kv_wide[...])
        kv_gather.start()
        vec[...] = jnp.zeros_like(vec)

        @row_loop(rows)
        def _(at):
            xhat, scale = normalize(wide(tok[at, :]))
            grad = grad_mid[at, :] + norm_back(first[at, :], small[0:1, :], xhat, scale)
            grad_low[at, :] = low(grad)
            vec[0:1, :] += jnp.sum(first[at, :] * xhat, axis=0, keepdims=True)
            vec[1:2, :] += jnp.sum(first[at, :], axis=0, keepdims=True)

        pick_rows(choose, grad_low, grad_send)
        back_grad.start()
        for step in range(2, depth - 1):
            run_out.stage(step)
        kv_gather.middle()
        run_out.total()
        out_sum[...] = mixed(z)[...]
        kv_gather.last()
        back_block.got()
        pick_rows(hold, block_got, block_res)
        back_grad.got()
        pick_rows(hold, grad_got, grad_res)
        up_step(1)
        for run_done in (back_block, back_grad, deal, run_out):
            run_done.finish()
        kv_gather.finish()
        down_over.got()
        for copy in (*hops, down_over):
            copy.sent()

    return pl.pallas_call(
        kernel,
        out_shape=[
            low_shape(total, head_cols),
            low_shape(8, rows, 2 * HEAD),
            wide_shape(8, width),
            low_shape(4, slots, width),
            low_shape(4, slots, width),
            low_shape(*d_out.shape[2:]),
            low_shape(*up_sum.shape),
            low_shape(*down_sum.shape),
        ],
        in_specs=[ANY] + [IN_VMEM] * 15 + [ANY],
        out_specs=[IN_VMEM, ANY] + [IN_VMEM] * 6,
        scratch_shapes=[
            low_vmem(4, rows, width),
            *PlaneScatter.buffers(rows, width),
            pltpu.VMEM((rows, width), jnp.float32),
            low_vmem(rows, width),
            *[low_vmem(4, slots, width)] * 4,
            low_vmem(8, rows, width),
            low_vmem(*d_out.shape),
            *[low_vmem(depth - 1, *d_out.shape[2:])] * 2,
            low_vmem(2, *up_sum.shape),
            low_vmem(*up_sum.shape),
            low_vmem(8, rows, 2 * HEAD),
            *PlaneScatter.buffers(rows, 2 * HEAD),
            pltpu.VMEM((rows, 2 * HEAD), jnp.float32),
            low_vmem(rows, 2 * HEAD),
            *net_scratch(
                2 * PlaneScatter.remotes + PlaneGather.remotes + 3 * DpExchange.remotes + LineGather.remotes(depth) + 3, 14
            ),
        ],
        compiler_params=comm_params(4),
        cost_estimate=lasts(70, 1 << 20),
    )(
        branch_all, query, keyval, allowed, w_output, w_query, w_keyval, own_tok, grad_middle, gain,
        block, chooser, holder, d_out, up_sum, down_sum, up_parts,
    )


def mlp_back(depth, grad_hidden, w_up, activated, w_down, middle, own_cot, small, down_first, d_down, d_up):
    rows, width = own_cot.shape
    up_hops = 1

    def kernel(gh, up, act_far, down_far, mid, cot, small, dd_first, dd, du,
               vec, grad_middle, branch_all, block_out, dd_sum, du_sum,
               parts, branch, sums, diag, from_x, from_y,
               parts2, sums2, diag2, from_x2, from_y2, mlp_sum, act, down,
               dd_got, du_got, dd_term, du_term, grad_normed, *sems):
        spot = Spot(depth)
        net = Net(*sems)
        z = spot.z
        run = PlaneScatter(net, spot, parts, sums, diag, from_x, from_y)
        run2 = PlaneScatter(net, spot, parts2, sums2, diag2, from_x2, from_y2)
        gather = PlaneGather(net, spot, branch, branch_all)
        after, _ = spot.ring()

        def slot(step):
            return lax.rem(z + 2 * depth - 1 - step, depth)

        def down_at(step):
            return dd_sum if step == depth - 1 else dd_got.at[step - 1]

        def up_at(step):
            return du_sum if step == up_hops else du_got.at[step - 1]

        down_terms = [
            net.local(dd.at[slot(step)], dd_term.at[step - 1]) for step in range(1, depth)
        ]
        up_terms = [
            net.local(du.at[slot(step)], du_term.at[step - 1]) for step in range(1, up_hops + 1)
        ]
        loads = [net.local(act_far, act), net.local(down_far, down)]
        down_hops = [
            net.remote(down_at(step - 1), down_at(step), after) for step in range(2, depth)
        ]
        ups = [net.remote(du.at[slot(0)], up_at(1), after)]
        ups += [net.remote(up_at(step - 1), up_at(step), after) for step in range(2, up_hops + 1)]

        def down_step(step):
            down_hops[step - 2].got()
            down_terms[step - 1].wait()
            add_rows(down_at(step), dd_term.at[step - 1], 32)
            if step < depth - 1:
                down_hops[step - 1].start()

        def up_step(step):
            ups[step - 1].got()
            up_terms[step - 1].wait()
            for at in range(2):
                add_rows(up_at(step).at[at], du_term.at[step - 1, at], 32)
            if step < up_hops:
                ups[step].start()

        def block(member, cols):
            rows_at = pl.ds(pl.multiple_of(member * rows, rows), rows)
            return product_cols(gh[rows_at, :], up[cols, :])

        def block2(member, cols):
            rows_at = pl.ds(pl.multiple_of(member * rows, rows), rows)
            return product(act[rows_at, :], down[:, cols])

        for copy in (*down_terms, *up_terms, *loads):
            copy.start()
        spot.barrier((spot.to_c, spot.to_x, spot.to_y, *spot.ring()), False)
        down_terms[0].wait()

        @pl.loop(0, dd_first.shape[0] // 32)
        def _(index):
            at = pl.ds(pl.multiple_of(index * 32, 32), 32)
            dd_got[0, at, :] = low(wide(dd_first[at, :]) + wide(dd_term[0, at, :]))

        down_hops[0].start()
        feed_blocks(run, parts, block)
        run.middle()
        for copy in loads:
            copy.wait()
        feed_blocks(run2, parts2, block2)
        run.last()
        down_step(2)
        run.finish(grad_normed)
        vec[...] = jnp.zeros_like(vec)

        @row_loop(rows)
        def _(at):
            xhat, scale = normalize(mid[at, :])
            grad_n = grad_normed[at, :]
            grad_o = wide(cot[at, :])
            grad = grad_o + norm_back(grad_n, small[3:4, :], xhat, scale)
            grad_b = low(grad)
            grad_middle[at, :] = grad
            branch[at, :] = grad_b
            for row, values in enumerate((wide(grad_b), grad_n * xhat, grad_n, grad_o)):
                vec[row : row + 1, :] += jnp.sum(values, axis=0, keepdims=True)

        gather.start()
        for step in range(3, depth - 1):
            down_step(step)
        run2.middle()
        down_step(depth - 1)
        ups[0].start()
        gather.middle()
        gather.last()
        run2.last()
        gather.finish()
        run2.finish(mlp_sum)

        @row_loop(rows)
        def _(at):
            block_out[at, :] = low(mid[at, :] + (mlp_sum[at, :] + small[5:6, :]))

        for step in range(1, up_hops + 1):
            up_step(step)
        for copy in (*down_hops, *ups):
            copy.sent()

    return pl.pallas_call(
        kernel,
        out_shape=[
            wide_shape(8, width),
            wide_shape(rows, width),
            low_shape(8, rows, width),
            low_shape(rows, width),
            low_shape(*d_down.shape[1:]),
            low_shape(*d_up.shape[1:]),
        ],
        in_specs=[IN_VMEM] * 2 + [ANY] * 2 + [IN_VMEM] * 4 + [ANY] * 2,
        out_specs=[IN_VMEM, IN_VMEM, ANY, IN_VMEM, IN_VMEM, IN_VMEM],
        scratch_shapes=[
            low_vmem(4, rows, width),
            low_vmem(rows, width),
            *PlaneScatter.buffers(rows, width),
            low_vmem(4, rows, width),
            *PlaneScatter.buffers(rows, width),
            pltpu.VMEM((rows, width), jnp.float32),
            low_vmem(*activated.shape),
            low_vmem(*w_down.shape),
            low_vmem(depth - 2, *d_down.shape[1:]),
            low_vmem(max(up_hops - 1, 1), *d_up.shape[1:]),
            low_vmem(depth - 1, *d_down.shape[1:]),
            low_vmem(up_hops, *d_up.shape[1:]),
            pltpu.VMEM((rows, width), jnp.float32),
            *net_scratch(
                2 * PlaneScatter.remotes + PlaneGather.remotes + depth + up_hops,
                depth + up_hops + 3,
            ),
        ],
        compiler_params=comm_params(5),
        cost_estimate=lasts(95, 1 << 20),
    )(
        grad_hidden, w_up, activated, w_down, middle, own_cot, small, down_first, d_down, d_up
    )


def closing(depth, up_own, down_own, down_x, d_query, d_keyval, d_vec, out_own):
    kv_rows, kv_cols = d_keyval.shape[0] // depth, d_keyval.shape[1]

    def add2(into, other):
        add_rows(into, other, 16)

    def add3(into, other):
        for at in range(2):
            add_rows(into.at[at], other.at[at], 16)

    def kernel(
        up, down, down_x_in, query, kv, vec, out,
        up_all, down_all, query_all, kv_all, vec_all, out_all,
        query_lo, query_hi, kv_lo, kv_hi, vec_lo, vec_hi,
        up_got, query_got, vec_got, *sems,
    ):
        spot = Spot(depth)
        net = Net(*sems)
        z, y = spot.z, spot.y
        xc, on_x = spot.x * 2 + spot.c, (1 - spot.x) * 2 + spot.c
        def kv_part(at):
            return kv.at[pl.ds(pl.multiple_of(at * kv_rows, kv_rows), kv_rows)]

        run_query = LineScatter(net, spot, lambda at: query.at[at], query_lo, query_hi, add3)
        run_kv = LineScatter(net, spot, kv_part, kv_lo, kv_hi, add2)
        run_vec = LineScatter(net, spot, lambda at: vec.at[at], vec_lo, vec_hi, add3)
        y_up = net.remote(up.at[1 - y], up_got, spot.to_y)
        y_query = net.remote(query.at[z, 1 - y], query_got, spot.to_y)
        y_vec = net.remote(vec.at[z, 1 - y], vec_got, spot.to_y)
        dp_up = DpGather(net, spot, up.at[y], up_all.at[y])
        dp_up2 = DpGather(net, spot, up_got, up_all.at[1 - y])
        dp_query = DpGather(net, spot, query.at[z, y], query_all.at[y])
        dp_query2 = DpGather(net, spot, query_got, query_all.at[1 - y])
        dp_kv = DpGather(net, spot, kv_part(z), kv_all)
        dp_vec = DpGather(net, spot, vec.at[z, y], vec_all)
        dp_out = DpGather(net, spot, out, out_all)
        keep_down = [
            net.local(down, down_all.at[xc]),
            net.local(down_x_in, down_all.at[on_x]),
        ]
        down_moves = [
            net.remote(down, down_all.at[xc], spot.to_c, down_all.at[spot.x * 2 + 1 - spot.c]),
            net.remote(
                down_x_in,
                down_all.at[on_x],
                spot.to_c,
                down_all.at[(1 - spot.x) * 2 + 1 - spot.c],
            ),
        ]
        spot.barrier((spot.to_c, spot.to_x, spot.to_y), True)
        run_query.stage(0)
        run_vec.stage(0)
        run_kv.stage(0)
        y_up.start()
        dp_up.start()
        dp_out.start()
        for copy in (*down_moves, *keep_down):
            copy.start()
        for step in range(1, depth - 1):
            run_query.stage(step)
            run_vec.stage(step)
            run_kv.stage(step)
            if step == 1:
                y_up.got()
                dp_up2.start()
        run_query.total()
        y_query.start()
        dp_query.start()
        run_vec.total()
        y_vec.start()
        run_kv.total()
        dp_kv.start()
        dp_up.last()
        y_query.got()
        dp_query2.start()
        y_vec.got()
        y_vec.sent()
        add_rows(vec.at[z, y], vec_got, 16)
        dp_vec.start()
        dp_up2.last()
        dps = (dp_query, dp_out, dp_kv, dp_query2, dp_vec)
        for run in dps:
            run.last()
        for run in (dp_up, dp_up2, *dps):
            run.finish()
        for copy in down_moves:
            copy.got()
            copy.sent()
        for copy in keep_down:
            copy.wait()
        for run in (run_query, run_kv, run_vec):
            run.finish()
        for copy in (y_up, y_query):
            copy.sent()

    remotes = (
        3 * LineGather.remotes(depth)
        + 5
        + 7 * DpGather.remotes
    )
    one = depth - 1

    def twice(*dims):
        return [low_vmem(*dims)] * 2

    return pl.pallas_call(
        kernel,
        out_shape=[
            low_shape(2, 4, *up_own.shape[1:]),
            low_shape(4, *down_own.shape),
            low_shape(2, 4, *d_query.shape[2:]),
            low_shape(4, kv_rows, kv_cols),
            low_shape(4, *d_vec.shape[2:]),
            low_shape(4, *out_own.shape),
        ],
        in_specs=[IN_VMEM] * 7,
        out_specs=[ANY] * 6,
        scratch_shapes=[
            *twice(one, *d_query.shape[1:]),
            *twice(one, kv_rows, kv_cols),
            *twice(one, *d_vec.shape[1:]),
            low_vmem(*up_own.shape[1:]),
            low_vmem(*d_query.shape[2:]),
            low_vmem(*d_vec.shape[2:]),
            *net_scratch(remotes, 10),
        ],
        compiler_params=comm_params(2),
        cost_estimate=lasts(70, 1 << 20),
    )(up_own, down_own, down_x, d_query, d_keyval, d_vec, out_own)


def widen(depth, y_slow, up_all, query_all, down_all, out_all, kv_all):
    rows = up_all.shape[2]
    seg = up_all.shape[3] // depth
    head_cols = query_all.shape[3]
    down_rows, width = down_all.shape
    steps = rows // 32

    def kernel(up, query, down, out, kv, up_w, query_w, down_w, out_w, kv_w):
        for y in range(2):
            for xc in range(4):
                for z in range(depth):
                    owner = y * depth + z if y_slow else z * 2 + y
                    at = (owner * 4 + xc) * seg
                    up_w[:, at : at + seg] = wide(up[y, xc, :, z * seg : (z + 1) * seg])
                at = (y * 4 + xc if y_slow else xc * 2 + y) * head_cols
                query_w[:, at : at + head_cols] = wide(query[y, xc])
        down_w[...] = wide(down[...])
        out_w[...] = wide(out[...])
        kv_w[...] = wide(kv[...])

    def rows_of(array):
        return pl.BlockSpec((array.shape[0] // steps, array.shape[1]), lambda index: (index, 0))

    def blocks_of(array):
        return pl.BlockSpec((2, 4, 32, array.shape[3]), lambda index: (0, 0, index, 0))

    shapes = [
        wide_shape(rows, 8 * depth * seg),
        wide_shape(rows, width),
        wide_shape(down_rows, width),
        wide_shape(*out_all.shape),
        wide_shape(*kv_all.shape),
    ]
    return pl.pallas_call(
        kernel,
        grid=(steps,),
        in_specs=[
            blocks_of(up_all),
            blocks_of(query_all),
            rows_of(down_all),
            rows_of(out_all),
            rows_of(kv_all),
        ],
        out_specs=[rows_of(item) for item in shapes],
        out_shape=shapes,
        compiler_params=pltpu.CompilerParams(vmem_limit_bytes=VMEM_LIMIT),
    )(up_all, query_all, down_all, out_all, kv_all)


def build(mesh):
    fsdp_size = mesh.shape["fsdp"]
    depth = fsdp_size // 2
    y_slow = depth != 4
    owner_axes = ("y", "z") if y_slow else ("z", "y")

    def owner(z_at, y_at):
        return y_at * depth + z_at if y_slow else z_at * 2 + y_at

    def shards(
        tokens,
        cotangent,
        lengths,
        dealing,
        attn_gain,
        attn_shift,
        query_weight,
        query_bias,
        keyval_weight,
        value_bias,
        output_weight,
        output_bias,
        mlp_gain,
        mlp_shift,
        up_weight,
        up_bias,
        down_weight,
        down_bias,
    ):
        held, slot_len, width = tokens.shape
        my_z = lax.axis_index("z")
        my_y = lax.axis_index("y")
        my_xc = lax.axis_index("x") * 2 + lax.axis_index("c")
        member = my_y * 4 + my_xc
        rows_own = query_weight.shape[0]
        ff = up_weight.shape[1]
        ff_own = down_weight.shape[0]
        ff_seg = ff_own // 4
        out_seg = rows_own // 4
        head_cols = width // 8
        group_seqs = held * 4

        def plane_table(table):
            parts = [
                lax.dynamic_slice_in_dim(table, owner(my_z, y_at) * group_seqs, group_seqs)
                for y_at in range(2)
            ]
            return jnp.stack(parts)

        micro = 2 * 4 * MB
        dealt_here = (
            lax.dynamic_slice_in_dim(dealing, owner(my_z, my_y) * group_seqs, group_seqs)
            - owner(my_z, my_y) * group_seqs
        )
        holders = (dealt_here // held).reshape(4, held)
        slots = (dealt_here % held).reshape(4, held)
        slot_for = jnp.sum(jnp.where(holders == my_xc, slots, 0), axis=1)
        my_holders = lax.dynamic_index_in_dim(holders, my_xc, 0, keepdims=False)
        lens = plane_table(lengths).reshape(micro, SEATS)
        ends = jnp.concatenate([lens[:, :1], lens[:, :1] + lens[:, 1:]], axis=1)
        starts = ends - lens
        at = jnp.arange(PACK)
        inside = (at[None, :, None] >= starts[:, None, :]) & (at[None, :, None] < ends[:, None, :])
        row_valid = jnp.any(inside, axis=2)
        seat = jnp.sum(jnp.where(inside, jnp.arange(SEATS)[None, None, :], 0), axis=2)
        segment = jnp.where(row_valid, seat, -1)
        allowed = (
            (at[None, :, None] >= at[None, None, :])
            & (segment[:, :, None] == segment[:, None, :])
            & row_valid[:, None, :]
        )
        my_inside = lax.dynamic_slice_in_dim(inside, member * MB, MB)
        my_starts = lax.dynamic_slice_in_dim(starts, member * MB, MB)
        my_lens = lax.dynamic_slice_in_dim(lens, member * MB, MB).reshape(held)
        offset = at[None, :] - jnp.sum(jnp.where(my_inside, my_starts[:, None, :], 0), axis=2)
        from_dev = jnp.sum(
            jnp.where(my_inside, my_holders.reshape(MB, 1, SEATS), 0), axis=2
        )
        own_count = MB * PACK
        own_valid = jnp.any(my_inside, axis=2).reshape(own_count)[:, None]
        source_row = jnp.where(
            own_valid[:, 0], (from_dev * slot_len + offset).reshape(own_count), 0
        )

        def up_columns(y_at):
            cols = [
                lax.dynamic_slice_in_dim(
                    up_weight, owner(z_at, y_at) * ff_own + my_xc * ff_seg, ff_seg, axis=1
                )
                for z_at in range(depth)
            ]
            return low(jnp.concatenate(cols, axis=1))

        def head_base(y_at):
            return owner(my_xc * (depth // 4), y_at) * rows_own

        def query_columns(y_at):
            return low(lax.dynamic_slice_in_dim(query_weight, head_base(y_at), head_cols, axis=1))

        small_parts = [
            attn_gain,
            attn_shift,
            output_bias,
            mlp_gain,
            mlp_shift,
            down_bias,
            query_bias,
            up_bias,
            value_bias,
        ]
        sizes = [item.shape[0] for item in small_parts]
        begins = [sum(sizes[:index]) for index in range(len(sizes))]
        small_count = sum(sizes)
        small_size = 16 * rows_own
        small = sum(
            jnp.pad(item, (begin, small_size - begin - size))
            for item, begin, size in zip(small_parts, begins, sizes)
        )
        small = low(small).reshape(16, rows_own)
        down_own = low(lax.dynamic_slice_in_dim(down_weight, my_xc * ff_seg, ff_seg, axis=0))
        ring = [(index, (index + 1) % depth) for index in range(depth)]

        def ring_slot(buffer, piece, step):
            at = (my_z - step + depth) % depth
            return lax.dynamic_update_slice(
                buffer, piece[None], (at,) + (0,) * piece.ndim
            )

        down_hop_1 = lax.ppermute(down_own, "z", ring)
        flat = held * slot_len
        places = jnp.arange(flat)
        from_slot = jnp.repeat(slot_for, slot_len) * slot_len + places % slot_len
        sender = low(from_slot[:, None] == places[None, :])
        holder = low(places[:, None] == from_slot[None, :])
        chooser = low((source_row[:, None] == jnp.arange(flat)[None, :]) & own_valid)
        (
            own_low,
            own_cot,
            up_piece,
            small_rows,
            w_keyval,
            tokens_all,
            query_all,
            w_output,
        ) = opening(
            depth,
            owner,
            tokens,
            cotangent,
            sender,
            chooser,
            query_weight,
            keyval_weight,
            output_weight,
            small,
            up_columns(my_y),
            up_columns(1 - my_y),
        )
        w_output = w_output.reshape(head_cols, width)

        bias_u = lax.dynamic_slice_in_dim(small_rows, 7 + my_xc, 1)
        bias_u = bias_u.reshape((2, depth, ff_seg) if y_slow else (depth, 2, ff_seg))
        my_bias_u = lax.dynamic_index_in_dim(
            bias_u, my_y, 0 if y_slow else 1, keepdims=False
        ).reshape(depth * ff_seg)
        def rows_in_order(gathered):
            if y_slow:
                gathered = jnp.transpose(gathered, (1, 0, 2, 3))
            return gathered.reshape(width, gathered.shape[-1])

        def rows_by_z(values):
            if y_slow:
                return jnp.transpose(
                    values.reshape(2, depth, rows_own, values.shape[-1]), (1, 0, 2, 3)
                )
            return values.reshape(depth, 2, rows_own, values.shape[-1])

        w_query = rows_in_order(query_all)
        down_hop_1, up_piece = lax.optimization_barrier((down_hop_1, up_piece))
        down_piece = lax.ppermute(down_hop_1, "z", ring)

        (
            middle,
            normed_attn,
            query,
            keyval,
            attended,
            normed_mlp,
            cotangent_all,
            up_all,
            down_all,
        ) = attend(
            depth,
            owner,
            tokens_all,
            own_low,
            own_cot,
            w_query,
            w_keyval,
            w_output,
            wide(allowed),
            small_rows,
            up_piece,
            down_own,
            down_hop_1,
        )
        normed_mlp = normed_mlp.reshape(micro * PACK, width)
        grad_mixed = cotangent_all.reshape(micro * PACK, width)
        down_piece, normed_mlp = lax.optimization_barrier((down_piece, normed_mlp))
        down_all = ring_slot(down_all, down_piece, 2)
        for step in range(3, depth):
            down_piece = lax.ppermute(down_piece, "z", ring)
            down_all = ring_slot(down_all, down_piece, step)
        w_up = rows_in_order(up_all)
        hidden = product(normed_mlp, w_up) + my_bias_u
        activated, slope = gelu_parts(hidden)
        activated = low(activated)

        down_parts = low(product_rows(activated, grad_mixed)).reshape(depth, ff_seg, width)
        down_first = lax.ppermute(
            lax.dynamic_index_in_dim(down_parts, (my_z + depth - 1) % depth, 0, keepdims=False),
            "z",
            ring,
        )
        mixed_later, down_parts = lax.optimization_barrier((grad_mixed, down_parts))
        w_down = down_all.reshape(depth * ff_seg, width)
        grad_act = product_cols(mixed_later, w_down)
        grad_hidden = low(slope * grad_act)
        up_parts = rows_by_z(low(product_rows(normed_mlp, grad_hidden)))
        second_sums, grad_middle, grad_branch, block_own, d_down, d_up = mlp_back(
            depth,
            grad_hidden,
            w_up,
            activated,
            w_down,
            middle,
            own_cot,
            small_rows,
            down_first,
            down_parts,
            up_parts,
        )
        grad_flat = grad_branch.reshape(micro * PACK, width)
        for step in range(2, depth - 2):
            d_up = lax.ppermute(d_up, "z", ring)
            at = (my_z - 1 - step + 2 * depth) % depth
            term = lax.dynamic_index_in_dim(up_parts, at, 0, keepdims=False)
            d_up = low(wide(d_up) + wide(term))
        d_output = low(product_rows(attended, grad_flat))
        hits = my_holders[None, :] == jnp.arange(4)[:, None]
        seq_starts = (my_starts + jnp.arange(MB)[:, None] * PACK).reshape(held)
        send_lens = jnp.sum(jnp.where(hits, my_lens[None, :], 0), axis=1)
        send_starts = jnp.sum(jnp.where(hits, seq_starts[None, :], 0), axis=1)
        pos = jnp.arange(slot_len)
        live = pos[None, :] < send_lens[:, None]
        send_rows = jnp.where(live, send_starts[:, None] + pos[None, :], -1)
        back_chooser = low(send_rows.reshape(flat)[:, None] == jnp.arange(own_count)[None, :])
        d_out_parts = jnp.transpose(
            d_output.reshape(depth // 4, 4, out_seg, width), (1, 0, 2, 3)
        )
        grad_query, grad_keyval, first_sums, block_out, input_grad, out_own, d_up, down_x = attend_back(
            depth,
            grad_branch,
            query,
            keyval,
            wide(allowed),
            w_output,
            w_query,
            w_keyval,
            own_low,
            grad_middle,
            small_rows,
            block_own,
            back_chooser,
            holder,
            d_out_parts,
            d_up,
            up_parts,
            d_down,
        )
        d_query = low(product_rows(normed_attn, grad_query))
        grad_keyval = grad_keyval.reshape(micro * PACK, 2 * HEAD)
        d_keyval = low(product_rows(normed_attn, grad_keyval))
        own_keyval = lax.dynamic_slice_in_dim(grad_keyval, member * own_count, own_count)

        def colsum(values):
            return jnp.sum(wide(values), axis=0)

        def spread_vec(values, parts, size, full):
            out = jnp.zeros((full,), jnp.float32)
            for index, begin in enumerate(parts):
                out = lax.dynamic_update_slice(
                    out, values[index * size : (index + 1) * size], (begin,)
                )
            return out

        vec_query = spread_vec(colsum(grad_query), [head_base(my_y)], head_cols, width)
        vec_up = spread_vec(
            colsum(grad_hidden),
            [owner(z_at, my_y) * ff_own + my_xc * ff_seg for z_at in range(depth)],
            ff_seg,
            ff,
        )
        vectors = [
            first_sums[0],
            first_sums[1],
            second_sums[0],
            second_sums[1],
            second_sums[2],
            second_sums[3],
            vec_query,
            vec_up,
            colsum(own_keyval[:, HEAD:]),
        ]
        vectors = jnp.concatenate([item.reshape(fsdp_size, -1) for item in vectors], axis=1)
        vectors = jnp.pad(low(vectors), ((0, 0), (0, small_size - small_count)))
        if y_slow:
            d_vec = jnp.transpose(vectors.reshape(2, depth, 16, rows_own), (1, 0, 2, 3))
        else:
            d_vec = vectors.reshape(depth, 2, 16, rows_own)

        if y_slow:
            d_keyval = d_keyval.reshape(2, depth, 4, out_seg, 2 * HEAD)
            d_keyval = lax.dynamic_index_in_dim(d_keyval, my_y, 0, keepdims=False)
        else:
            d_keyval = d_keyval.reshape(depth, 2, 4, out_seg, 2 * HEAD)
            d_keyval = lax.dynamic_index_in_dim(d_keyval, my_y, 1, keepdims=False)
        d_keyval = lax.dynamic_index_in_dim(d_keyval, my_xc, 1, keepdims=False)
        d_keyval = d_keyval.reshape(depth * out_seg, 2 * HEAD)
        up_all, down_all, query_sum, kv_sum, vec_all, out_all = closing(
            depth, d_up, d_down, down_x, rows_by_z(d_query), d_keyval, d_vec, out_own
        )
        up_grad, query_grad, down_grad, output_grad, keyval_grad = widen(
            depth,
            y_slow,
            up_all,
            query_sum,
            down_all.reshape(ff_own, width),
            out_all.reshape(rows_own, width),
            kv_sum.reshape(rows_own, 2 * HEAD),
        )
        vec_own = jnp.sum(wide(vec_all), axis=0).reshape(small_size)
        (
            gain_a_grad,
            shift_a_grad,
            bias_o_grad,
            gain_m_grad,
            shift_m_grad,
            bias_d_grad,
            bias_q_grad,
            bias_u_grad,
            bias_v_grad,
        ) = [vec_own[start : start + size] for start, size in zip(begins, sizes)]

        return (
            block_out,
            input_grad,
            gain_a_grad,
            shift_a_grad,
            query_grad,
            bias_q_grad,
            keyval_grad,
            bias_v_grad,
            output_grad,
            bias_o_grad,
            gain_m_grad,
            shift_m_grad,
            up_grad,
            bias_u_grad,
            down_grad,
            bias_d_grad,
        )

    return shards, depth, owner_axes


def solution(mesh):
    shards, depth, owner_axes = build(mesh)
    sizes = {"z": depth, "y": 2}
    fine = Mesh(
        mesh.devices.reshape(sizes[owner_axes[0]], sizes[owner_axes[1]], 2, 2),
        owner_axes + ("x", "c"),
    )
    rows = P(owner_axes + ("x", "c"), None, None)
    vec = P(owner_axes)
    mat = P(owner_axes, None)
    in_specs = (
        rows, rows, P(), P(),
        vec, vec, mat, vec, mat, vec, mat, vec, vec, vec, mat, vec, mat, vec,
    )
    out_specs = (
        rows, rows,
        vec, vec, mat, vec, mat, vec, mat, vec, vec, vec, mat, vec, mat, vec,
    )
    return jax.shard_map(shards, mesh=fine, in_specs=in_specs, out_specs=out_specs, check_vma=False)
```

```python
import math

import jax
import jax.numpy as jnp
from jax import lax
from jax.experimental import pallas as pl
from jax.experimental.pallas import tpu as pltpu
from jax.sharding import Mesh
from jax.sharding import PartitionSpec as P

HEADS = 16
HEAD = 128
MB = 2
SEATS = 2
PACK = 80

epsilon = 1e-05
gelu_scale = 0.7978845608028654
gelu_cubic = 0.044715

DP = ("x", "c")


def low(values):
    return values.astype(jnp.bfloat16)


def wide(values):
    return values.astype(jnp.float32)


def product(left_mat, right_mat):
    return jnp.dot(left_mat, right_mat, preferred_element_type=jnp.float32)


def product_rows(left_mat, right_mat):
    return lax.dot_general(
        left_mat, right_mat, (((0,), (0,)), ((), ())), preferred_element_type=jnp.float32
    )


def product_cols(left_mat, right_mat):
    return lax.dot_general(
        left_mat, right_mat, (((1,), (1,)), ((), ())), preferred_element_type=jnp.float32
    )


def normalize(rows):
    center = rows - jnp.mean(rows, axis=-1, keepdims=True)
    spread = jnp.mean(center * center, axis=-1, keepdims=True)
    scale = lax.rsqrt(spread + epsilon)
    return center * scale, scale


def norm_back(grad_normed, gain, xhat, scale):
    g = grad_normed * gain
    inner = jnp.mean(g * xhat, axis=-1, keepdims=True)
    return scale * (g - jnp.mean(g, axis=-1, keepdims=True) - xhat * inner)


def gelu_parts(values):
    inner = jnp.tanh(gelu_scale * (values + gelu_cubic * values * values * values))
    activated = 0.5 * values * (1.0 + inner)
    slope = 0.5 * (1.0 + inner) + 0.5 * values * (1.0 - inner * inner) * gelu_scale * (
        1.0 + 3.0 * gelu_cubic * values * values
    )
    return activated, slope


MESH_ID = pl.DeviceIdType.MESH
VMEM_LIMIT = 56 * 1024 * 1024


class Spot:
    def __init__(self, depth):
        self.depth = depth
        self.z = lax.axis_index("z")
        self.y = lax.axis_index("y")
        self.x = lax.axis_index("x")
        self.c = lax.axis_index("c")
        self.to_c = {"c": 1 - self.c}
        self.to_x = {"x": 1 - self.x}
        self.to_y = {"y": 1 - self.y}
        self.to_xc = {"x": 1 - self.x, "c": 1 - self.c}
        self.up = {"z": self.z + 1}
        self.down = {"z": self.z - 1}

    def ring(self):
        before = {"z": lax.rem(self.z + self.depth - 1, self.depth)}
        return ({"z": lax.rem(self.z + 1, self.depth)}, before)

    def barrier(self, plane, line):
        bar = pltpu.get_barrier_semaphore()
        for to in plane:
            pl.semaphore_signal(bar, inc=1, device_id=to, device_id_type=MESH_ID)
        if line:

            @pl.when(self.z > 0)
            def _():
                pl.semaphore_signal(bar, inc=1, device_id=self.down, device_id_type=MESH_ID)

            @pl.when(self.z < self.depth - 1)
            def _():
                pl.semaphore_signal(bar, inc=1, device_id=self.up, device_id_type=MESH_ID)

        count = len(plane)
        if line:
            lower = jnp.where(self.z > 0, 1, 0)
            upper = jnp.where(self.z < self.depth - 1, 1, 0)
            count = count + lower + upper
        pl.semaphore_wait(bar, count)


class Net:
    def __init__(self, send_sems, recv_sems, local_sems):
        self.send_sems = send_sems
        self.recv_sems = recv_sems
        self.local_sems = local_sems
        self.count = 0
        self.local_count = 0
        self.open = []

    def remote(self, src, dst, to, arrives=None):
        copy = Copy(self, self.count, src, dst, to, arrives)
        self.count += 1
        return copy

    def local(self, src, dst):
        copy = pltpu.make_async_copy(src, dst, self.local_sems.at[self.local_count])
        self.local_count += 1
        return copy


class Copy:
    def __init__(self, net, index, src, dst, to, arrives):
        def make(target):
            return pltpu.make_async_remote_copy(
                src_ref=src,
                dst_ref=target,
                send_sem=net.send_sems.at[index],
                recv_sem=net.recv_sems.at[index],
                device_id=to,
                device_id_type=MESH_ID,
            )

        self.out = make(dst)
        self.into = make(dst if arrives is None else arrives)

    def start(self):
        self.out.start()

    def got(self):
        self.into.wait_recv()

    def sent(self):
        self.out.wait_send()


class PlaneGather:
    def __init__(self, net, spot, own, slots, share=2):
        def at(y, x, c):
            return y * 4 + x * 2 + c

        y, x, c = spot.y, spot.x, spot.c
        self.both = share == 2
        half = own.shape[0] // share
        lo, hi = pl.ds(0, half), pl.ds(half * (share - 1), half)
        me = at(y, x, c)
        on_x, on_y, on_d = at(y, 1 - x, c), at(1 - y, x, c), at(1 - y, 1 - x, c)
        peer = [at(y, x, 1 - c), at(y, 1 - x, 1 - c), at(1 - y, x, 1 - c), at(1 - y, 1 - x, 1 - c)]

        def slot(index):
            return slots.at[index]

        self.keep = net.local(own, slot(me))
        self.x = net.remote(own, slot(me), spot.to_x, slot(on_x))
        self.y = net.remote(own, slot(me), spot.to_y, slot(on_y))
        self.c = net.remote(own, slot(me), spot.to_c, slot(peer[0]))
        self.x_on_y = net.remote(
            slots.at[on_x, lo], slots.at[on_x, lo], spot.to_y, slots.at[on_d, lo]
        )
        self.x_on_c = net.remote(slot(on_x), slot(on_x), spot.to_c, slot(peer[1]))
        self.y_on_c = net.remote(slot(on_y), slot(on_y), spot.to_c, slot(peer[2]))
        self.lo_on_c = net.remote(
            slots.at[on_d, lo], slots.at[on_d, lo], spot.to_c, slots.at[peer[3], lo]
        )
        if self.both:
            self.y_on_x = net.remote(
                slots.at[on_y, hi], slots.at[on_y, hi], spot.to_x, slots.at[on_d, hi]
            )
            self.hi_on_c = net.remote(
                slots.at[on_d, hi], slots.at[on_d, hi], spot.to_c, slots.at[peer[3], hi]
            )

    def start(self):
        self.x.start()
        self.y.start()
        self.c.start()
        self.keep.start()

    def middle(self):
        self.x.got()
        self.x_on_y.start()
        self.x_on_c.start()
        self.y.got()
        if self.both:
            self.y_on_x.start()
        self.y_on_c.start()

    def last(self):
        self.x_on_y.got()
        self.lo_on_c.start()
        if self.both:
            self.y_on_x.got()
            self.hi_on_c.start()

    def finish(self):
        second = (self.y_on_x, self.hi_on_c) if self.both else ()
        for copy in (self.c, self.x_on_c, self.y_on_c, self.lo_on_c, *second[1:]):
            copy.got()
        firsts = (self.x, self.y, self.c, self.x_on_y, self.x_on_c, self.y_on_c, self.lo_on_c)
        for copy in (*firsts, *second):
            copy.sent()
        self.keep.wait()

    remotes = 9
    locals = 1


def add_rows(into, other, step=32):
    rows = into.shape[0]

    @pl.loop(0, rows // step)
    def _(index):
        at = pl.ds(pl.multiple_of(index * step, step), step)
        into[at, :] = low(wide(into[at, :]) + wide(other[at, :]))


class PlaneScatter:
    remotes = 10

    @staticmethod
    def buffers(rows, width):
        return [
            pltpu.VMEM((4, rows, width), jnp.bfloat16),
            pltpu.VMEM((rows, width), jnp.bfloat16),
            pltpu.VMEM((rows, width), jnp.bfloat16),
            pltpu.VMEM((rows, width), jnp.bfloat16),
        ]

    def __init__(self, net, spot, parts, sums, diag, from_x, from_y, share=2):
        y, x, c = spot.y, spot.x, spot.c
        self.both = share == 2
        half = parts.shape[1] // share
        lo, hi = pl.ds(0, half), pl.ds(half * (share - 1), half)
        self.own, self.nx, self.ny, self.nd = (
            y * 2 + x,
            y * 2 + 1 - x,
            (1 - y) * 2 + x,
            (1 - y) * 2 + 1 - x,
        )
        self.parts, self.sums, self.diag = parts, sums, diag
        self.stacked = parts.shape[0] == 4
        self.from_x, self.from_y, self.c = from_x, from_y, c
        self.lo, self.hi = lo, hi
        self.first = {
            key: net.remote(
                parts.at[at] if self.stacked else parts.at[at * 2 + 1 - c], sums.at[at], spot.to_c
            )
            for key, at in (("d", self.nd), ("x", self.nx), ("y", self.ny), ("o", self.own))
        }
        self.d_hi = net.remote(sums.at[self.nd, hi], diag.at[hi], spot.to_y)
        self.y_hi = net.remote(sums.at[self.ny, hi], from_y.at[hi], spot.to_y)
        self.x_hi = net.remote(sums.at[self.nx, hi], from_x.at[hi], spot.to_x)
        if self.both:
            self.d_lo = net.remote(sums.at[self.nd, lo], diag.at[lo], spot.to_x)
            self.x_lo = net.remote(sums.at[self.nx, lo], from_x.at[lo], spot.to_x)
            self.y_lo = net.remote(sums.at[self.ny, lo], from_y.at[lo], spot.to_y)

    def start(self):
        for copy in self.first.values():
            copy.start()

    def give(self, key, at):
        if self.stacked:
            self.send(at, at * 2 + 1 - self.c)
            self.first[key].start()

    def pair(self, key, at):
        if self.stacked:
            self.prepare(at * 2 + self.c)
            self.first[key].got()
            self.merge(at * 2 + self.c, at)
        else:
            self.first[key].got()
            add_rows(self.sums.at[at], self.parts.at[at * 2 + self.c])

    def middle(self):
        self.give("d", self.nd)
        self.give("x", self.nx)
        self.pair("d", self.nd)
        if self.both:
            self.d_lo.start()
        self.d_hi.start()
        self.give("y", self.ny)
        self.pair("x", self.nx)
        if self.both:
            self.x_lo.start()
        self.give("o", self.own)
        self.pair("y", self.ny)
        self.y_hi.start()
        self.pair("o", self.own)

    def last(self):
        if self.both:
            self.d_lo.got()
            add_rows(self.sums.at[self.ny, self.lo], self.diag.at[self.lo], 16)
            self.y_lo.start()
        self.d_hi.got()
        add_rows(self.sums.at[self.nx, self.hi], self.diag.at[self.hi], 16)
        self.x_hi.start()

    def finish(self, result):
        second = (self.x_lo, self.y_lo) if self.both else ()
        for copy in (self.y_hi, self.x_hi, *second):
            copy.got()

        @pl.loop(0, result.shape[0] // 16)
        def _(index):
            at = pl.ds(pl.multiple_of(index * 16, 16), 16)
            result[at, :] = (
                wide(self.sums[self.own, at, :]) + wide(self.from_x[at, :]) + wide(self.from_y[at, :])
            )

        for copy in (
            *self.first.values(),
            self.d_hi,
            self.x_hi,
            self.y_hi,
            *((self.d_lo, *second) if self.both else ()),
        ):
            copy.sent()


class LineGather:
    def __init__(self, net, spot, slots, moves=None):
        self.spot, depth, z = spot, spot.depth, spot.z
        self.moves = moves
        self.hops = []
        for step in range(depth - 1):
            lower = jnp.maximum(z - step, 0)
            upper = jnp.minimum(z + step, depth - 1)
            from_low = jnp.maximum(z - 1 - step, 0)
            from_high = jnp.minimum(z + 1 + step, depth - 1)
            self.hops.append(
                (
                    net.remote(slots(lower), slots(lower), spot.up, slots(from_low)),
                    net.remote(slots(upper), slots(upper), spot.down, slots(from_high)),
                )
            )

    @staticmethod
    def remotes(depth):
        return 2 * (depth - 1)

    def pick(self, cond, slot):
        return cond if self.moves is None else cond & self.moves(slot)

    def sends(self, step):
        z, last = self.spot.z, self.spot.depth - 1
        return (
            (self.pick((z >= step) & (z < last), z - step), self.hops[step][0]),
            (self.pick((z + step <= last) & (z > 0), z + step), self.hops[step][1]),
        )

    def takes(self, step):
        z, last = self.spot.z, self.spot.depth - 1
        return (
            (self.pick(z >= step + 1, z - 1 - step), self.hops[step][0]),
            (self.pick(z + step + 1 <= last, z + 1 + step), self.hops[step][1]),
        )

    def start(self, step):
        for cond, copy in self.sends(step):
            pl.when(cond)(copy.start)

    def got(self, step):
        for cond, copy in self.takes(step):
            pl.when(cond)(copy.got)

    def hop(self, step):
        for (came, old), (goes, new) in zip(self.takes(step - 1), self.sends(step)):
            pl.when(came)(old.got)
            pl.when(goes)(new.start)

    def finish(self):
        for step in range(self.spot.depth - 1):
            for cond, copy in self.sends(step):
                pl.when(cond)(copy.sent)


class LineScatter:
    def __init__(self, net, spot, parts, from_low, from_high, add):
        self.net, self.spot, self.parts, self.add = net, spot, parts, add
        self.boxes = (from_low, from_high)
        self.first = net.count
        net.count += 2 * (spot.depth - 1)

    @staticmethod
    def remotes(depth):
        return 2 * (depth - 1)

    def copy(self, side, message):
        last = self.spot.depth - 1
        slot = self.parts(last - message if side == 0 else message)
        at = self.first + side * last + message
        copy = pltpu.make_async_remote_copy(
            src_ref=slot,
            dst_ref=self.boxes[side].at[message],
            send_sem=self.net.send_sems.at[at],
            recv_sem=self.net.recv_sems.at[at],
            device_id=(self.spot.up, self.spot.down)[side],
            device_id_type=MESH_ID,
        )
        return copy, slot, self.boxes[side].at[message]

    def take(self, side, message):
        copy, slot, box = self.copy(side, message)
        copy.wait_recv()
        self.add(slot, box)

    def place(self, side):
        return self.spot.z if side == 0 else self.spot.depth - 1 - self.spot.z

    def stage(self, step):
        for side in range(2):
            behind = self.place(side)

            @pl.when(behind <= step)
            def _():
                message = step - behind

                @pl.when(behind > 0)
                def _():
                    self.take(side, message)

                self.copy(side, message)[0].start()

    def total(self):
        last = self.spot.depth - 1
        for side in range(2):
            behind = self.place(side)

            @pl.when(behind > 0)
            def _():
                self.take(side, last - behind)

    def finish(self):
        for side in range(2):
            behind = self.place(side)
            for message in range(self.spot.depth - 1):

                @pl.when(behind + message < self.spot.depth - 1)
                def _():
                    self.copy(side, message)[0].wait_send()


class DpGather:
    remotes = 3

    def __init__(self, net, spot, own, slots):
        me = spot.x * 2 + spot.c
        on_x = (1 - spot.x) * 2 + spot.c
        self.keep = net.local(own, slots.at[me])
        self.x = net.remote(own, slots.at[me], spot.to_x, slots.at[on_x])
        self.c = net.remote(own, slots.at[me], spot.to_c, slots.at[spot.x * 2 + 1 - spot.c])
        self.x_on_c = net.remote(
            slots.at[on_x],
            slots.at[on_x],
            spot.to_c,
            slots.at[(1 - spot.x) * 2 + 1 - spot.c],
        )

    def start(self):
        self.x.start()
        self.c.start()
        self.keep.start()

    def last(self):
        self.x.got()
        self.x_on_c.start()

    def finish(self):
        self.c.got()
        self.x_on_c.got()
        for copy in (self.x, self.c, self.x_on_c):
            copy.sent()
        self.keep.wait()


class DpExchange:
    remotes = 3

    def __init__(self, net, spot, parts, slots):
        me = spot.x * 2 + spot.c
        on_x = (1 - spot.x) * 2 + spot.c
        on_c = spot.x * 2 + 1 - spot.c
        on_xc = (1 - spot.x) * 2 + 1 - spot.c
        self.keep = net.local(parts.at[me], slots.at[me])
        self.moves = [
            net.remote(parts.at[at], slots.at[me], to, slots.at[at])
            for at, to in ((on_xc, spot.to_xc), (on_x, spot.to_x), (on_c, spot.to_c))
        ]

    def start(self):
        for copy in self.moves:
            copy.start()
        self.keep.start()

    def got(self):
        for copy in self.moves:
            copy.got()
        self.keep.wait()

    def finish(self):
        for copy in self.moves:
            copy.sent()


def net_scratch(remotes, locals_):
    return [
        pltpu.SemaphoreType.DMA((remotes,)),
        pltpu.SemaphoreType.DMA((remotes,)),
        pltpu.SemaphoreType.DMA((max(locals_, 1),)),
    ]


ANY = pl.BlockSpec(memory_space=pl.ANY)
IN_VMEM = pl.BlockSpec(memory_space=pltpu.VMEM)


def lasts(micros, moved):
    return pl.CostEstimate(
        flops=int(micros * 1e9), bytes_accessed=int(moved), transcendentals=0
    )


def comm_params(collective_id):
    return pltpu.CompilerParams(
        collective_id=collective_id, has_side_effects=True, vmem_limit_bytes=VMEM_LIMIT
    )


def low_shape(*dims):
    return jax.ShapeDtypeStruct(dims, jnp.bfloat16)


def wide_shape(*dims):
    return jax.ShapeDtypeStruct(dims, jnp.float32)


def low_vmem(*dims):
    return pltpu.VMEM(dims, jnp.bfloat16)


def pick_rows(chooser, source, result, step=512):
    width = result.shape[-1]

    @pl.loop(0, width // step)
    def _(index):
        at = pl.ds(pl.multiple_of(index * step, step), step)
        rows = source[..., at].reshape(chooser.shape[1], step)
        result[..., at] = low(product(chooser[...], rows)).reshape(*result.shape[:-1], step)


def opening(depth, owner, tokens, cotangent, sender, chooser, query_weight, keyval_weight, output_weight, small, up_mine, up_other):
    rows = chooser.shape[0]
    width = tokens.shape[-1]
    group = depth // 4
    rows_own = query_weight.shape[0]
    head_cols = width // 8
    kv_rows = rows_own // 4
    kv_cols = keyval_weight.shape[1]

    def kernel(
        tok_held, cot_held, send, choose, query_w, kv_w, out_w, small_m, up_m, up_o,
        own_tok, own_cot, up_own, small_rows, w_keyval,
        tok_all, query_all, out_all,
        kv_all, small_all, tok, cot, tok_got, cot_got, out_v, kv_line, query_m, query_o, query_y, small_y,
        query_f, out_f, kv_f, *sems,
    ):
        spot = Spot(depth)
        net = Net(*sems)
        z, y = spot.z, spot.y
        xc = spot.x * 2 + spot.c
        source = z // group == xc

        def head_base(y_at):
            return pl.multiple_of(owner(xc * group, y_at) * rows_own, 128)

        def strip(ref, size):
            return ref.at[pl.ds(pl.multiple_of(xc * size, size), size)]

        def z_slot(at):
            return kv_line.at[pl.ds(pl.multiple_of(at * kv_rows, kv_rows), kv_rows)]

        read_query_o = net.local(query_w.at[:, pl.ds(head_base(1 - y), head_cols)], query_f.at[0])
        read_out = net.local(out_w, out_f)
        read_kv = net.local(strip(kv_w, kv_rows), kv_f)
        read_query = net.local(query_w.at[:, pl.ds(head_base(y), head_cols)], query_f.at[1])
        tok_deal = DpExchange(net, spot, tok, tok_got)
        cot_deal = DpExchange(net, spot, cot, cot_got)
        tok_run = PlaneGather(net, spot, own_tok, tok_all)
        kv_run = PlaneGather(net, spot, kv_line, kv_all)
        y_query = net.remote(query_o, query_y, spot.to_y)
        y_small = net.remote(small_m, small_y, spot.to_y)
        y_up = net.remote(up_o, up_own.at[y], spot.to_y, up_own.at[1 - y])
        keep_query = net.local(query_m, query_all.at[z, y])
        keep_query_y = net.local(query_y, query_all.at[z, 1 - y])
        keep_out = net.local(out_v, out_all)
        run_kv = LineGather(net, spot, z_slot)
        run_query = LineGather(net, spot, lambda at: query_all.at[at])
        run_small = LineGather(net, spot, lambda at: small_all.at[at])

        def piece_of_out(piece):
            rows_at = pl.ds(piece * kv_rows, kv_rows)
            return LineGather(
                net,
                spot,
                lambda at: out_v.at[at % group, rows_at],
                lambda at: at // group == xc,
            )

        run_outs = [piece_of_out(piece) for piece in range(4)]
        read_query_o.start()
        pl.when(source)(read_out.start)
        read_kv.start()
        read_query.start()
        small_all[z, y] = small_m[...]
        spot.barrier((spot.to_c, spot.to_x, spot.to_y, spot.to_xc), True)
        pick_rows(send, tok_held, tok)
        tok_deal.start()
        read_query_o.wait()
        query_o[...] = low(query_f[0])
        y_query.start()
        y_small.start()
        y_up.start()

        @pl.when(source)
        def _():
            read_out.wait()

            @pl.loop(0, rows_own // 16)
            def _(index):
                at = pl.ds(pl.multiple_of(index * 16, 16), 16)
                out_v[z % group, at, :] = low(out_f[at, :])

        for run in run_outs:
            run.start(0)
        read_kv.wait()
        z_slot(z)[...] = low(kv_f[...])
        run_kv.start(0)
        read_query.wait()
        query_m[...] = low(query_f[1])
        keep_query.start()
        keep_query.wait()
        y_query.got()
        keep_query_y.start()
        y_small.got()
        small_all[z, 1 - y] = small_y[...]
        keep_query_y.wait()
        run_query.start(0)
        run_small.start(0)
        pick_rows(send, cot_held, cot)

        @pl.loop(0, rows_own // 16)
        def _(index):
            at = pl.ds(pl.multiple_of(index * 16, 16), 16)
            up_own[y, at, :] = up_m[at, :]

        tok_deal.got()
        pick_rows(choose, tok_got, own_tok)
        tok_run.start()
        cot_deal.start()
        for step in range(1, depth - 1):
            for run in run_outs:
                run.hop(step)
            run_kv.hop(step)
        run_query.hop(1)
        run_small.hop(1)
        run_kv.got(depth - 2)
        kv_run.start()
        for step in range(2, depth - 1):
            run_query.hop(step)
            run_small.hop(step)
        tok_run.middle()
        kv_run.middle()
        cot_deal.got()
        pick_rows(choose, cot_got, own_cot)
        tok_run.last()
        kv_run.last()
        for run in run_outs:
            run.got(depth - 2)
        keep_out.start()
        run_query.got(depth - 2)
        run_small.got(depth - 2)
        for z_at in range(depth):
            for y_at in range(2):
                at = owner(z_at, y_at) * rows_own
                small_rows[:, at : at + rows_own] = wide(small_all[z_at, y_at])
        y_up.got()
        runs = (*run_outs, run_kv, run_query, run_small, tok_run, kv_run)
        for run in (*runs, tok_deal, cot_deal):
            run.finish()
        for y_at in range(2):
            for xc_at in range(4):
                for z_at in range(depth):
                    at = owner(z_at, y_at) * rows_own + xc_at * kv_rows
                    w_keyval[at : at + kv_rows, :] = kv_all[
                        y_at * 4 + xc_at, z_at * kv_rows : (z_at + 1) * kv_rows, :
                    ]
        for copy in (y_query, y_small, y_up):
            copy.sent()
        keep_out.wait()

    remotes = (
        2 * DpExchange.remotes + 2 * PlaneGather.remotes + 4 + 7 * LineGather.remotes(depth)
    )
    operands = (
        tokens, cotangent, sender, chooser, query_weight, keyval_weight, output_weight, small,
        up_mine, up_other,
    )
    wide_type = jnp.float32
    return pl.pallas_call(
        kernel,
        out_shape=[
            low_shape(rows, width),
            low_shape(rows, width),
            low_shape(2, *up_mine.shape),
            wide_shape(small.shape[0], width),
            low_shape(width, kv_cols),
            low_shape(8, rows, width),
            low_shape(depth, 2, rows_own, head_cols),
            low_shape(group, rows_own, width),
        ],
        in_specs=[IN_VMEM] * 4 + [ANY] * 3 + [IN_VMEM] * 3,
        out_specs=[IN_VMEM] * 5 + [ANY] * 3,
        scratch_shapes=[
            low_vmem(8, depth * kv_rows, kv_cols),
            low_vmem(depth, 2, *small.shape),
            *[low_vmem(*tokens.shape)] * 4,
            low_vmem(group, rows_own, width),
            low_vmem(depth * kv_rows, kv_cols),
            low_vmem(rows_own, head_cols),
            low_vmem(rows_own, head_cols),
            low_vmem(rows_own, head_cols),
            low_vmem(*small.shape),
            pltpu.VMEM((2, rows_own, head_cols), wide_type),
            pltpu.VMEM((rows_own, width), wide_type),
            pltpu.VMEM((kv_rows, kv_cols), wide_type),
            *net_scratch(remotes, 20),
        ],
        compiler_params=comm_params(1),
        cost_estimate=lasts(75, 1 << 20),
    )(*operands)


ROWS_STEP = 32


def row_loop(count):
    def decorate(body):
        @pl.loop(0, count // ROWS_STEP)
        def _(index):
            body(pl.ds(pl.multiple_of(index * ROWS_STEP, ROWS_STEP), ROWS_STEP))

    return decorate


class Loads:
    def __init__(self, net, far, near):
        self.net, self.far, self.near = net, far, near
        self.first = net.local_count
        net.local_count += 8

    def copy(self, member):
        return pltpu.make_async_copy(
            self.far.at[member], self.near.at[member], self.net.local_sems.at[self.first + member]
        )

    def start(self, spot):
        def at(y, x, c):
            return y * 4 + x * 2 + c

        y, x, c = spot.y, spot.x, spot.c
        for y_at, x_at in ((1 - y, 1 - x), (y, 1 - x), (1 - y, x), (y, x)):
            for c_at in (1 - c, c):
                self.copy(at(y_at, x_at, c_at)).start()

    def wait(self, member):
        self.copy(member).wait()


def feed_blocks(run, parts, block, prepare=None):
    width = parts.shape[-1]

    def columns(body):
        @pl.loop(0, width // 512)
        def _(index):
            body(pl.ds(pl.multiple_of(index * 512, 512), 512))

    def ready(member):
        if prepare is not None:
            prepare(member)

    def send(at, member):
        ready(member)

        @columns
        def _(cols):
            parts[at, :, cols] = low(block(member, cols))

    def merge(member, at):
        @columns
        def _(cols):
            run.sums[at, :, cols] = low(wide(run.sums[at, :, cols]) + block(member, cols))

    run.send, run.merge, run.prepare = send, merge, ready


SCORE_SCALE = 1.0 / math.sqrt(HEAD)


def stacked(values):
    return jnp.concatenate([values[:, :HEAD], values[:, HEAD:]], axis=0)


def unstacked(values):
    half = values.shape[0] // 2
    return jnp.concatenate([values[:half], values[half:]], axis=1)


def softmax_of(query_2, keys, allowed):
    scores = product_cols(query_2, keys) * SCORE_SCALE
    scores = jnp.where(jnp.concatenate([allowed, allowed], axis=0) > 0.0, scores, -1e30)
    exps = jnp.exp(scores - jnp.max(scores, axis=-1, keepdims=True))
    return exps / jnp.sum(exps, axis=-1, keepdims=True)


def attend(depth, owner, tok_all, own_tok, own_cot, w_query, w_keyval, w_output, allowed, small, up_own, down_own, down_1):
    rows, width = own_tok.shape
    total = 8 * rows
    head_cols = w_query.shape[1]
    micros = rows // PACK

    def kernel(
        tok_far, tok, cot, w_q, w_kv, w_out, allow, small,
        up, down, down_b,
        middle, normed_a, query, keyval, attended, normed_all, cot_all, up_all, down_all,
        tok_near, b_kv, parts, normed, sums, diag, from_x, from_y, *sems,
    ):
        spot = Spot(depth)
        net = Net(*sems)
        z = spot.z
        run = PlaneScatter(net, spot, parts, sums, diag, from_x, from_y)
        gather = PlaneGather(net, spot, normed, normed_all)
        cot_run = PlaneGather(net, spot, cot, cot_all, share=1)
        after, _ = spot.ring()

        def behind(step):
            return lax.rem(z + 2 * depth - step, depth)

        keeps = [
            net.local(up, up_all.at[z]),
            net.local(down, down_all.at[z]),
            net.local(down_b, down_all.at[behind(1)]),
        ]
        ups = [net.remote(up, up_all.at[z], after, up_all.at[behind(1)])]
        for step in range(2, depth):
            at = up_all.at[behind(step - 1)]
            ups.append(net.remote(at, at, after, up_all.at[behind(step)]))

        xc = spot.x * 2 + spot.c
        group = depth // 4
        rows_own = width // (2 * depth)
        head_base = pl.multiple_of(owner(xc * group, spot.y) * rows_own, 128)

        tok_loads = Loads(net, tok_far, tok_near)

        def one_member(member):
            tok_loads.wait(member)
            first = pl.multiple_of(member * rows, rows)

            @pl.loop(0, rows // ROWS_STEP)
            def _(index):
                at = pl.multiple_of(index * ROWS_STEP, ROWS_STEP)
                xhat, _ = normalize(wide(tok_near[member, pl.ds(at, ROWS_STEP), :]))
                normed_a[pl.ds(first + at, ROWS_STEP), :] = low(xhat * small[0:1, :] + small[1:2, :])

            rows_at = pl.ds(first, rows)
            query[rows_at, :] = low(
                product(normed_a[rows_at, :], w_q[...])
                + small[6:7, pl.ds(head_base, head_cols)]
            )
            keyval[rows_at, :] = low(product(normed_a[rows_at, :], w_kv[...]) + b_kv[...])

            for index in range(micros):
                at = pl.ds(pl.multiple_of(first + index * PACK, PACK), PACK)
                pair = keyval[at, :]
                probs = softmax_of(
                    stacked(query[at, :]), pair[:, :HEAD], allow[member * micros + index]
                )
                attended[at, :] = low(unstacked(product(low(probs), pair[:, HEAD:])))

        def block(member, cols):
            rows_at = pl.ds(pl.multiple_of(member * rows, rows), rows)
            return product(attended[rows_at, :], w_out[:, cols])

        tok_loads.start(spot)
        each = HEAD // (2 * depth)
        lane = lax.broadcasted_iota(jnp.int32, (1, HEAD), 1)
        values = jnp.zeros((1, HEAD), jnp.float32)
        for at in range(2 * depth):
            begin = at * rows_own // HEAD * HEAD
            found = pltpu.roll(
                small[11:12, begin : begin + HEAD], (at * each - at * rows_own + begin) % HEAD, 1
            )
            values = jnp.where((lane >= at * each) & (lane < (at + 1) * each), found, values)
        b_kv[:, :HEAD] = jnp.zeros((1, HEAD), jnp.float32)
        b_kv[:, HEAD:] = values
        for copy in keeps:
            copy.start()
        spot.barrier((spot.to_c, spot.to_x, spot.to_y, *spot.ring()), False)
        ups[0].start()
        cot_run.start()
        feed_blocks(run, parts, block, one_member)
        run.middle()
        cot_run.middle()
        ups[0].got()
        ups[1].start()
        run.last()
        cot_run.last()
        run.finish(middle)

        @row_loop(rows)
        def _(at):
            total_rows = wide(tok[at, :]) + (middle[at, :] + small[2:3, :])
            middle[at, :] = total_rows
            xhat, _ = normalize(total_rows)
            normed[at, :] = low(xhat * small[3:4, :] + small[4:5, :])

        gather.start()
        for step in range(2, depth - 1):
            ups[step - 1].got()
            ups[step].start()
        gather.middle()
        gather.last()
        gather.finish()
        cot_run.finish()
        ups[-1].got()
        for copy in ups:
            copy.sent()
        for copy in keeps:
            copy.wait()

    return pl.pallas_call(
        kernel,
        out_shape=[
            wide_shape(rows, width),
            low_shape(total, width),
            low_shape(total, head_cols),
            low_shape(total, 2 * HEAD),
            low_shape(total, head_cols),
            low_shape(8, rows, width),
            low_shape(8, rows, width),
            low_shape(depth, *up_own.shape),
            low_shape(depth, *down_own.shape),
        ],
        in_specs=[ANY] + [IN_VMEM] * 10,
        out_specs=[IN_VMEM] * 5 + [ANY] * 4,
        scratch_shapes=[
            low_vmem(8, rows, width),
            pltpu.VMEM((1, 2 * HEAD), jnp.float32),
            low_vmem(4, rows, width),
            low_vmem(rows, width),
            *PlaneScatter.buffers(rows, width),
            *net_scratch(PlaneScatter.remotes + 2 * PlaneGather.remotes + depth, 14),
        ],
        compiler_params=comm_params(3),
        cost_estimate=lasts(90, 1 << 20),
    )(
        tok_all, own_tok, own_cot, w_query, w_keyval, w_output, allowed, small,
        up_own, down_own, down_1,
    )


def attend_back(depth, branch_all, query, keyval, allowed, w_output, w_query, w_keyval, own_tok, grad_middle, gain, block, chooser, holder, d_out, up_sum, up_parts, down_sum):
    group = depth // 4
    rows, width = own_tok.shape
    total, head_cols = query.shape
    micros = rows // PACK
    slots = chooser.shape[0] // 4

    def kernel(
        branch_far, q_all, kv_all, allow, w_out, w_q, w_kv, tok, grad_mid, small, block_own, choose, hold,
        out, du, dd, du_far,
        grad_q, kv_rows_all, vec, block_res, grad_res, out_sum, du_sum, dd_x,
        parts, sums, diag, from_x, from_y, first, grad_low, block_send, grad_send, block_got, grad_got,
        branch, out_mix, out_lo, out_hi, du_term, du_mid,
        grad_kv, kv_sums, kv_diag, kv_from_x, kv_from_y, kv_wide, kv_own, *sems,
    ):
        spot = Spot(depth)
        net = Net(*sems)
        run = PlaneScatter(net, spot, parts, sums, diag, from_x, from_y, share=1)
        down_over = net.remote(dd, dd_x, spot.to_x)
        z = spot.z
        after, _ = spot.ring()
        deal = DpExchange(net, spot, out, out_mix)

        def mixed(at):
            return out_mix.at[at // group, at % group]

        def add2(into, other):
            add_rows(into, other, 16)

        kv_run = PlaneScatter(net, spot, grad_kv, kv_sums, kv_diag, kv_from_x, kv_from_y)
        kv_gather = PlaneGather(net, spot, kv_own, kv_rows_all)
        run_out = LineScatter(net, spot, mixed, out_lo, out_hi, add2)
        hops = [net.remote(du, du_mid, after), net.remote(du_mid, du_sum, after)]
        terms = [
            net.local(du_far.at[lax.rem(z + 1, depth)], du_term.at[0]),
            net.local(du_far.at[z], du_term.at[1]),
        ]

        def up_step(step):
            into = (du_mid, du_sum)[step]
            hops[step].got()
            terms[step].wait()
            for at in range(2):
                add_rows(into.at[at], du_term.at[step, at], 32)
            if step == 0:
                hops[1].start()

        back_block = DpExchange(net, spot, block_send, block_got)
        back_grad = DpExchange(net, spot, grad_send, grad_got)

        branch_loads = Loads(net, branch_far, branch)

        def one_member(member):
            branch_loads.wait(member)
            begin = pl.multiple_of(member * rows, rows)
            grad_att = low(product_cols(branch[member], w_out[...]))
            for index in range(micros):
                at = pl.ds(pl.multiple_of(begin + index * PACK, PACK), PACK)
                pair = kv_all[at, :]
                keys, vals = pair[:, :HEAD], pair[:, HEAD:]
                q_2 = stacked(q_all[at, :])
                g_2 = stacked(grad_att[index * PACK : (index + 1) * PACK])
                probs = softmax_of(q_2, keys, allow[member * micros + index])
                grad_probs = product_cols(g_2, vals)
                inner = jnp.sum(probs * grad_probs, axis=-1, keepdims=True)
                grad_scores = low(probs * (grad_probs - inner))
                grad_q[at, :] = low(unstacked(product(grad_scores, keys) * SCORE_SCALE))
                grad_k = product_rows(grad_scores, q_2) * SCORE_SCALE
                grad_v = product_rows(low(probs), g_2)
                grad_kv[member, index * PACK : (index + 1) * PACK, :] = low(
                    jnp.concatenate([grad_k, grad_v], axis=1)
                )

        def block_of(member, cols):
            rows_at = pl.ds(pl.multiple_of(member * rows, rows), rows)
            return product_cols(grad_q[rows_at, :], w_q[cols, :]) + product_cols(
                grad_kv[member], w_kv[cols, :]
            )

        branch_loads.start(spot)
        for copy in terms:
            copy.start()
        spot.barrier((spot.to_c, spot.to_x, spot.to_y, spot.to_xc, *spot.ring()), False)
        deal.start()
        hops[0].start()
        down_over.start()
        pick_rows(choose, block_own, block_send)
        feed_blocks(run, parts, block_of, one_member)
        run.middle()
        kv_run.start()
        deal.got()
        run_out.stage(0)
        up_step(0)
        kv_run.middle()
        run.last()
        run_out.stage(1)
        kv_run.last()
        run.finish(first)
        kv_run.finish(kv_wide)
        back_block.start()
        kv_own[...] = low(kv_wide[...])
        kv_gather.start()
        vec[...] = jnp.zeros_like(vec)

        @row_loop(rows)
        def _(at):
            xhat, scale = normalize(wide(tok[at, :]))
            grad = grad_mid[at, :] + norm_back(first[at, :], small[0:1, :], xhat, scale)
            grad_low[at, :] = low(grad)
            vec[0:1, :] += jnp.sum(first[at, :] * xhat, axis=0, keepdims=True)
            vec[1:2, :] += jnp.sum(first[at, :], axis=0, keepdims=True)

        pick_rows(choose, grad_low, grad_send)
        back_grad.start()
        for step in range(2, depth - 1):
            run_out.stage(step)
        kv_gather.middle()
        run_out.total()
        out_sum[...] = mixed(z)[...]
        kv_gather.last()
        back_block.got()
        pick_rows(hold, block_got, block_res)
        back_grad.got()
        pick_rows(hold, grad_got, grad_res)
        up_step(1)
        for run_done in (back_block, back_grad, deal, run_out):
            run_done.finish()
        kv_gather.finish()
        down_over.got()
        for copy in (*hops, down_over):
            copy.sent()

    return pl.pallas_call(
        kernel,
        out_shape=[
            low_shape(total, head_cols),
            low_shape(8, rows, 2 * HEAD),
            wide_shape(8, width),
            low_shape(4, slots, width),
            low_shape(4, slots, width),
            low_shape(*d_out.shape[2:]),
            low_shape(*up_sum.shape),
            low_shape(*down_sum.shape),
        ],
        in_specs=[ANY] + [IN_VMEM] * 15 + [ANY],
        out_specs=[IN_VMEM, ANY] + [IN_VMEM] * 6,
        scratch_shapes=[
            low_vmem(4, rows, width),
            *PlaneScatter.buffers(rows, width),
            pltpu.VMEM((rows, width), jnp.float32),
            low_vmem(rows, width),
            *[low_vmem(4, slots, width)] * 4,
            low_vmem(8, rows, width),
            low_vmem(*d_out.shape),
            *[low_vmem(depth - 1, *d_out.shape[2:])] * 2,
            low_vmem(2, *up_sum.shape),
            low_vmem(*up_sum.shape),
            low_vmem(8, rows, 2 * HEAD),
            *PlaneScatter.buffers(rows, 2 * HEAD),
            pltpu.VMEM((rows, 2 * HEAD), jnp.float32),
            low_vmem(rows, 2 * HEAD),
            *net_scratch(
                2 * PlaneScatter.remotes + PlaneGather.remotes + 3 * DpExchange.remotes + LineGather.remotes(depth) + 3, 14
            ),
        ],
        compiler_params=comm_params(4),
        cost_estimate=lasts(70, 1 << 20),
    )(
        branch_all, query, keyval, allowed, w_output, w_query, w_keyval, own_tok, grad_middle, gain,
        block, chooser, holder, d_out, up_sum, down_sum, up_parts,
    )


def mlp_back(depth, grad_hidden, w_up, activated, w_down, middle, own_cot, small, down_first, d_down, d_up):
    rows, width = own_cot.shape
    up_hops = 1

    def kernel(gh, up, act_far, down_far, mid, cot, small, dd_first, dd, du,
               vec, grad_middle, branch_all, block_out, dd_sum, du_sum,
               parts, branch, sums, diag, from_x, from_y,
               parts2, sums2, diag2, from_x2, from_y2, mlp_sum, act, down,
               dd_got, du_got, dd_term, du_term, grad_normed, *sems):
        spot = Spot(depth)
        net = Net(*sems)
        z = spot.z
        run = PlaneScatter(net, spot, parts, sums, diag, from_x, from_y)
        run2 = PlaneScatter(net, spot, parts2, sums2, diag2, from_x2, from_y2)
        gather = PlaneGather(net, spot, branch, branch_all)
        after, _ = spot.ring()

        def slot(step):
            return lax.rem(z + 2 * depth - 1 - step, depth)

        def down_at(step):
            return dd_sum if step == depth - 1 else dd_got.at[step - 1]

        def up_at(step):
            return du_sum if step == up_hops else du_got.at[step - 1]

        down_terms = [
            net.local(dd.at[slot(step)], dd_term.at[step - 1]) for step in range(1, depth)
        ]
        up_terms = [
            net.local(du.at[slot(step)], du_term.at[step - 1]) for step in range(1, up_hops + 1)
        ]
        loads = [net.local(act_far, act), net.local(down_far, down)]
        down_hops = [
            net.remote(down_at(step - 1), down_at(step), after) for step in range(2, depth)
        ]
        ups = [net.remote(du.at[slot(0)], up_at(1), after)]
        ups += [net.remote(up_at(step - 1), up_at(step), after) for step in range(2, up_hops + 1)]

        def down_step(step):
            down_hops[step - 2].got()
            down_terms[step - 1].wait()
            add_rows(down_at(step), dd_term.at[step - 1], 32)
            if step < depth - 1:
                down_hops[step - 1].start()

        def up_step(step):
            ups[step - 1].got()
            up_terms[step - 1].wait()
            for at in range(2):
                add_rows(up_at(step).at[at], du_term.at[step - 1, at], 32)
            if step < up_hops:
                ups[step].start()

        def block(member, cols):
            rows_at = pl.ds(pl.multiple_of(member * rows, rows), rows)
            return product_cols(gh[rows_at, :], up[cols, :])

        def block2(member, cols):
            rows_at = pl.ds(pl.multiple_of(member * rows, rows), rows)
            return product(act[rows_at, :], down[:, cols])

        for copy in (*down_terms, *up_terms, *loads):
            copy.start()
        spot.barrier((spot.to_c, spot.to_x, spot.to_y, *spot.ring()), False)
        down_terms[0].wait()

        @pl.loop(0, dd_first.shape[0] // 32)
        def _(index):
            at = pl.ds(pl.multiple_of(index * 32, 32), 32)
            dd_got[0, at, :] = low(wide(dd_first[at, :]) + wide(dd_term[0, at, :]))

        down_hops[0].start()
        feed_blocks(run, parts, block)
        run.middle()
        for copy in loads:
            copy.wait()
        feed_blocks(run2, parts2, block2)
        run.last()
        down_step(2)
        run.finish(grad_normed)
        vec[...] = jnp.zeros_like(vec)

        @row_loop(rows)
        def _(at):
            xhat, scale = normalize(mid[at, :])
            grad_n = grad_normed[at, :]
            grad_o = wide(cot[at, :])
            grad = grad_o + norm_back(grad_n, small[3:4, :], xhat, scale)
            grad_b = low(grad)
            grad_middle[at, :] = grad
            branch[at, :] = grad_b
            for row, values in enumerate((wide(grad_b), grad_n * xhat, grad_n, grad_o)):
                vec[row : row + 1, :] += jnp.sum(values, axis=0, keepdims=True)

        gather.start()
        for step in range(3, depth - 1):
            down_step(step)
        run2.middle()
        down_step(depth - 1)
        ups[0].start()
        gather.middle()
        gather.last()
        run2.last()
        gather.finish()
        run2.finish(mlp_sum)

        @row_loop(rows)
        def _(at):
            block_out[at, :] = low(mid[at, :] + (mlp_sum[at, :] + small[5:6, :]))

        for step in range(1, up_hops + 1):
            up_step(step)
        for copy in (*down_hops, *ups):
            copy.sent()

    return pl.pallas_call(
        kernel,
        out_shape=[
            wide_shape(8, width),
            wide_shape(rows, width),
            low_shape(8, rows, width),
            low_shape(rows, width),
            low_shape(*d_down.shape[1:]),
            low_shape(*d_up.shape[1:]),
        ],
        in_specs=[IN_VMEM] * 2 + [ANY] * 2 + [IN_VMEM] * 4 + [ANY] * 2,
        out_specs=[IN_VMEM, IN_VMEM, ANY, IN_VMEM, IN_VMEM, IN_VMEM],
        scratch_shapes=[
            low_vmem(4, rows, width),
            low_vmem(rows, width),
            *PlaneScatter.buffers(rows, width),
            low_vmem(4, rows, width),
            *PlaneScatter.buffers(rows, width),
            pltpu.VMEM((rows, width), jnp.float32),
            low_vmem(*activated.shape),
            low_vmem(*w_down.shape),
            low_vmem(depth - 2, *d_down.shape[1:]),
            low_vmem(max(up_hops - 1, 1), *d_up.shape[1:]),
            low_vmem(depth - 1, *d_down.shape[1:]),
            low_vmem(up_hops, *d_up.shape[1:]),
            pltpu.VMEM((rows, width), jnp.float32),
            *net_scratch(
                2 * PlaneScatter.remotes + PlaneGather.remotes + depth + up_hops,
                depth + up_hops + 3,
            ),
        ],
        compiler_params=comm_params(5),
        cost_estimate=lasts(95, 1 << 20),
    )(
        grad_hidden, w_up, activated, w_down, middle, own_cot, small, down_first, d_down, d_up
    )


def closing(depth, up_own, down_own, down_x, d_query, d_keyval, d_vec, out_own):
    kv_rows, kv_cols = d_keyval.shape[0] // depth, d_keyval.shape[1]

    def add2(into, other):
        add_rows(into, other, 16)

    def add3(into, other):
        for at in range(2):
            add_rows(into.at[at], other.at[at], 16)

    def kernel(
        up, down, down_x_in, query, kv, vec, out,
        up_all, down_all, query_all, kv_all, vec_all, out_all,
        query_lo, query_hi, kv_lo, kv_hi, vec_lo, vec_hi,
        up_got, query_got, vec_got, *sems,
    ):
        spot = Spot(depth)
        net = Net(*sems)
        z, y = spot.z, spot.y
        xc, on_x = spot.x * 2 + spot.c, (1 - spot.x) * 2 + spot.c
        def kv_part(at):
            return kv.at[pl.ds(pl.multiple_of(at * kv_rows, kv_rows), kv_rows)]

        run_query = LineScatter(net, spot, lambda at: query.at[at], query_lo, query_hi, add3)
        run_kv = LineScatter(net, spot, kv_part, kv_lo, kv_hi, add2)
        run_vec = LineScatter(net, spot, lambda at: vec.at[at], vec_lo, vec_hi, add3)
        y_up = net.remote(up.at[1 - y], up_got, spot.to_y)
        y_query = net.remote(query.at[z, 1 - y], query_got, spot.to_y)
        y_vec = net.remote(vec.at[z, 1 - y], vec_got, spot.to_y)
        dp_up = DpGather(net, spot, up.at[y], up_all.at[y])
        dp_up2 = DpGather(net, spot, up_got, up_all.at[1 - y])
        dp_query = DpGather(net, spot, query.at[z, y], query_all.at[y])
        dp_query2 = DpGather(net, spot, query_got, query_all.at[1 - y])
        dp_kv = DpGather(net, spot, kv_part(z), kv_all)
        dp_vec = DpGather(net, spot, vec.at[z, y], vec_all)
        dp_out = DpGather(net, spot, out, out_all)
        keep_down = [
            net.local(down, down_all.at[xc]),
            net.local(down_x_in, down_all.at[on_x]),
        ]
        down_moves = [
            net.remote(down, down_all.at[xc], spot.to_c, down_all.at[spot.x * 2 + 1 - spot.c]),
            net.remote(
                down_x_in,
                down_all.at[on_x],
                spot.to_c,
                down_all.at[(1 - spot.x) * 2 + 1 - spot.c],
            ),
        ]
        spot.barrier((spot.to_c, spot.to_x, spot.to_y), True)
        run_query.stage(0)
        run_vec.stage(0)
        run_kv.stage(0)
        y_up.start()
        dp_up.start()
        dp_out.start()
        for copy in (*down_moves, *keep_down):
            copy.start()
        for step in range(1, depth - 1):
            run_query.stage(step)
            run_vec.stage(step)
            run_kv.stage(step)
            if step == 1:
                y_up.got()
                dp_up2.start()
        run_query.total()
        y_query.start()
        dp_query.start()
        run_vec.total()
        y_vec.start()
        run_kv.total()
        dp_kv.start()
        dp_up.last()
        y_query.got()
        dp_query2.start()
        y_vec.got()
        y_vec.sent()
        add_rows(vec.at[z, y], vec_got, 16)
        dp_vec.start()
        dp_up2.last()
        dps = (dp_query, dp_out, dp_kv, dp_query2, dp_vec)
        for run in dps:
            run.last()
        for run in (dp_up, dp_up2, *dps):
            run.finish()
        for copy in down_moves:
            copy.got()
            copy.sent()
        for copy in keep_down:
            copy.wait()
        for run in (run_query, run_kv, run_vec):
            run.finish()
        for copy in (y_up, y_query):
            copy.sent()

    remotes = (
        3 * LineGather.remotes(depth)
        + 5
        + 7 * DpGather.remotes
    )
    one = depth - 1

    def twice(*dims):
        return [low_vmem(*dims)] * 2

    return pl.pallas_call(
        kernel,
        out_shape=[
            low_shape(2, 4, *up_own.shape[1:]),
            low_shape(4, *down_own.shape),
            low_shape(2, 4, *d_query.shape[2:]),
            low_shape(4, kv_rows, kv_cols),
            low_shape(4, *d_vec.shape[2:]),
            low_shape(4, *out_own.shape),
        ],
        in_specs=[IN_VMEM] * 7,
        out_specs=[ANY] * 6,
        scratch_shapes=[
            *twice(one, *d_query.shape[1:]),
            *twice(one, kv_rows, kv_cols),
            *twice(one, *d_vec.shape[1:]),
            low_vmem(*up_own.shape[1:]),
            low_vmem(*d_query.shape[2:]),
            low_vmem(*d_vec.shape[2:]),
            *net_scratch(remotes, 10),
        ],
        compiler_params=comm_params(2),
        cost_estimate=lasts(70, 1 << 20),
    )(up_own, down_own, down_x, d_query, d_keyval, d_vec, out_own)


def widen(depth, y_slow, up_all, query_all, down_all, out_all, kv_all):
    rows = up_all.shape[2]
    seg = up_all.shape[3] // depth
    head_cols = query_all.shape[3]
    down_rows, width = down_all.shape
    steps = rows // 32

    def kernel(up, query, down, out, kv, up_w, query_w, down_w, out_w, kv_w):
        for y in range(2):
            for xc in range(4):
                for z in range(depth):
                    owner = y * depth + z if y_slow else z * 2 + y
                    at = (owner * 4 + xc) * seg
                    up_w[:, at : at + seg] = wide(up[y, xc, :, z * seg : (z + 1) * seg])
                at = (y * 4 + xc if y_slow else xc * 2 + y) * head_cols
                query_w[:, at : at + head_cols] = wide(query[y, xc])
        down_w[...] = wide(down[...])
        out_w[...] = wide(out[...])
        kv_w[...] = wide(kv[...])

    def rows_of(array):
        return pl.BlockSpec((array.shape[0] // steps, array.shape[1]), lambda index: (index, 0))

    def blocks_of(array):
        return pl.BlockSpec((2, 4, 32, array.shape[3]), lambda index: (0, 0, index, 0))

    shapes = [
        wide_shape(rows, 8 * depth * seg),
        wide_shape(rows, width),
        wide_shape(down_rows, width),
        wide_shape(*out_all.shape),
        wide_shape(*kv_all.shape),
    ]
    return pl.pallas_call(
        kernel,
        grid=(steps,),
        in_specs=[
            blocks_of(up_all),
            blocks_of(query_all),
            rows_of(down_all),
            rows_of(out_all),
            rows_of(kv_all),
        ],
        out_specs=[rows_of(item) for item in shapes],
        out_shape=shapes,
        compiler_params=pltpu.CompilerParams(vmem_limit_bytes=VMEM_LIMIT),
    )(up_all, query_all, down_all, out_all, kv_all)


def build(mesh):
    fsdp_size = mesh.shape["fsdp"]
    depth = fsdp_size // 2
    y_slow = depth != 4
    owner_axes = ("y", "z") if y_slow else ("z", "y")

    def owner(z_at, y_at):
        return y_at * depth + z_at if y_slow else z_at * 2 + y_at

    def shards(
        tokens,
        cotangent,
        lengths,
        dealing,
        attn_gain,
        attn_shift,
        query_weight,
        query_bias,
        keyval_weight,
        value_bias,
        output_weight,
        output_bias,
        mlp_gain,
        mlp_shift,
        up_weight,
        up_bias,
        down_weight,
        down_bias,
    ):
        held, slot_len, width = tokens.shape
        my_z = lax.axis_index("z")
        my_y = lax.axis_index("y")
        my_xc = lax.axis_index("x") * 2 + lax.axis_index("c")
        member = my_y * 4 + my_xc
        rows_own = query_weight.shape[0]
        ff = up_weight.shape[1]
        ff_own = down_weight.shape[0]
        ff_seg = ff_own // 4
        out_seg = rows_own // 4
        head_cols = width // 8
        group_seqs = held * 4

        def plane_table(table):
            parts = [
                lax.dynamic_slice_in_dim(table, owner(my_z, y_at) * group_seqs, group_seqs)
                for y_at in range(2)
            ]
            return jnp.stack(parts)

        micro = 2 * 4 * MB
        dealt_here = (
            lax.dynamic_slice_in_dim(dealing, owner(my_z, my_y) * group_seqs, group_seqs)
            - owner(my_z, my_y) * group_seqs
        )
        holders = (dealt_here // held).reshape(4, held)
        slots = (dealt_here % held).reshape(4, held)
        slot_for = jnp.sum(jnp.where(holders == my_xc, slots, 0), axis=1)
        my_holders = lax.dynamic_index_in_dim(holders, my_xc, 0, keepdims=False)
        lens = plane_table(lengths).reshape(micro, SEATS)
        ends = jnp.concatenate([lens[:, :1], lens[:, :1] + lens[:, 1:]], axis=1)
        starts = ends - lens
        at = jnp.arange(PACK)
        inside = (at[None, :, None] >= starts[:, None, :]) & (at[None, :, None] < ends[:, None, :])
        row_valid = jnp.any(inside, axis=2)
        seat = jnp.sum(jnp.where(inside, jnp.arange(SEATS)[None, None, :], 0), axis=2)
        segment = jnp.where(row_valid, seat, -1)
        allowed = (
            (at[None, :, None] >= at[None, None, :])
            & (segment[:, :, None] == segment[:, None, :])
            & row_valid[:, None, :]
        )
        my_inside = lax.dynamic_slice_in_dim(inside, member * MB, MB)
        my_starts = lax.dynamic_slice_in_dim(starts, member * MB, MB)
        my_lens = lax.dynamic_slice_in_dim(lens, member * MB, MB).reshape(held)
        offset = at[None, :] - jnp.sum(jnp.where(my_inside, my_starts[:, None, :], 0), axis=2)
        from_dev = jnp.sum(
            jnp.where(my_inside, my_holders.reshape(MB, 1, SEATS), 0), axis=2
        )
        own_count = MB * PACK
        own_valid = jnp.any(my_inside, axis=2).reshape(own_count)[:, None]
        source_row = jnp.where(
            own_valid[:, 0], (from_dev * slot_len + offset).reshape(own_count), 0
        )

        def up_columns(y_at):
            cols = [
                lax.dynamic_slice_in_dim(
                    up_weight, owner(z_at, y_at) * ff_own + my_xc * ff_seg, ff_seg, axis=1
                )
                for z_at in range(depth)
            ]
            return low(jnp.concatenate(cols, axis=1))

        def head_base(y_at):
            return owner(my_xc * (depth // 4), y_at) * rows_own

        def query_columns(y_at):
            return low(lax.dynamic_slice_in_dim(query_weight, head_base(y_at), head_cols, axis=1))

        small_parts = [
            attn_gain,
            attn_shift,
            output_bias,
            mlp_gain,
            mlp_shift,
            down_bias,
            query_bias,
            up_bias,
            value_bias,
        ]
        sizes = [item.shape[0] for item in small_parts]
        begins = [sum(sizes[:index]) for index in range(len(sizes))]
        small_count = sum(sizes)
        small_size = 16 * rows_own
        small = sum(
            jnp.pad(item, (begin, small_size - begin - size))
            for item, begin, size in zip(small_parts, begins, sizes)
        )
        small = low(small).reshape(16, rows_own)
        down_own = low(lax.dynamic_slice_in_dim(down_weight, my_xc * ff_seg, ff_seg, axis=0))
        ring = [(index, (index + 1) % depth) for index in range(depth)]

        def ring_slot(buffer, piece, step):
            at = (my_z - step + depth) % depth
            return lax.dynamic_update_slice(
                buffer, piece[None], (at,) + (0,) * piece.ndim
            )

        down_hop_1 = lax.ppermute(down_own, "z", ring)
        flat = held * slot_len
        places = jnp.arange(flat)
        from_slot = jnp.repeat(slot_for, slot_len) * slot_len + places % slot_len
        sender = low(from_slot[:, None] == places[None, :])
        holder = low(places[:, None] == from_slot[None, :])
        hits = my_holders[None, :] == jnp.arange(4)[:, None]
        seq_starts = (my_starts + jnp.arange(MB)[:, None] * PACK).reshape(held)
        send_lens = jnp.sum(jnp.where(hits, my_lens[None, :], 0), axis=1)
        send_starts = jnp.sum(jnp.where(hits, seq_starts[None, :], 0), axis=1)
        pos = jnp.arange(slot_len)
        live = pos[None, :] < send_lens[:, None]
        send_rows = jnp.where(live, send_starts[:, None] + pos[None, :], -1)
        back_chooser = low(send_rows.reshape(flat)[:, None] == jnp.arange(own_count)[None, :])
        chooser = low((source_row[:, None] == jnp.arange(flat)[None, :]) & own_valid)
        allow = wide(allowed)
        tokens, allow, back_chooser = lax.optimization_barrier((tokens, allow, back_chooser))
        (
            own_low,
            own_cot,
            up_piece,
            small_rows,
            w_keyval,
            tokens_all,
            query_all,
            w_output,
        ) = opening(
            depth,
            owner,
            tokens,
            cotangent,
            sender,
            chooser,
            query_weight,
            keyval_weight,
            output_weight,
            small,
            up_columns(my_y),
            up_columns(1 - my_y),
        )
        w_output = w_output.reshape(head_cols, width)

        def rows_in_order(gathered):
            if y_slow:
                gathered = jnp.transpose(gathered, (1, 0, 2, 3))
            return gathered.reshape(width, gathered.shape[-1])

        def rows_by_z(values):
            if y_slow:
                return jnp.transpose(
                    values.reshape(2, depth, rows_own, values.shape[-1]), (1, 0, 2, 3)
                )
            return values.reshape(depth, 2, rows_own, values.shape[-1])

        w_query = rows_in_order(query_all)
        down_hop_1, up_piece = lax.optimization_barrier((down_hop_1, up_piece))
        down_piece = lax.ppermute(down_hop_1, "z", ring)

        (
            middle,
            normed_attn,
            query,
            keyval,
            attended,
            normed_mlp,
            cotangent_all,
            up_all,
            down_all,
        ) = attend(
            depth,
            owner,
            tokens_all,
            own_low,
            own_cot,
            w_query,
            w_keyval,
            w_output,
            allow,
            small_rows,
            up_piece,
            down_own,
            down_hop_1,
        )
        normed_mlp = normed_mlp.reshape(micro * PACK, width)
        grad_mixed = cotangent_all.reshape(micro * PACK, width)
        down_piece, normed_mlp, late_rows = lax.optimization_barrier(
            (down_piece, normed_mlp, small_rows)
        )
        bias_u = lax.dynamic_slice_in_dim(late_rows, 7 + my_xc, 1)
        bias_u = bias_u.reshape((2, depth, ff_seg) if y_slow else (depth, 2, ff_seg))
        my_bias_u = lax.dynamic_index_in_dim(
            bias_u, my_y, 0 if y_slow else 1, keepdims=False
        ).reshape(depth * ff_seg)
        down_all = ring_slot(down_all, down_piece, 2)
        for step in range(3, depth):
            down_piece = lax.ppermute(down_piece, "z", ring)
            down_all = ring_slot(down_all, down_piece, step)
        w_up = rows_in_order(up_all)
        hidden = product(normed_mlp, w_up) + my_bias_u
        activated, slope = gelu_parts(hidden)
        activated = low(activated)

        down_parts = low(product_rows(activated, grad_mixed)).reshape(depth, ff_seg, width)
        down_first = lax.ppermute(
            lax.dynamic_index_in_dim(down_parts, (my_z + depth - 1) % depth, 0, keepdims=False),
            "z",
            ring,
        )
        mixed_later, down_parts = lax.optimization_barrier((grad_mixed, down_parts))
        w_down = down_all.reshape(depth * ff_seg, width)
        grad_act = product_cols(mixed_later, w_down)
        grad_hidden = low(slope * grad_act)
        up_parts = rows_by_z(low(product_rows(normed_mlp, grad_hidden)))
        second_sums, grad_middle, grad_branch, block_own, d_down, d_up = mlp_back(
            depth,
            grad_hidden,
            w_up,
            activated,
            w_down,
            middle,
            own_cot,
            small_rows,
            down_first,
            down_parts,
            up_parts,
        )
        grad_flat = grad_branch.reshape(micro * PACK, width)
        for step in range(2, depth - 2):
            d_up = lax.ppermute(d_up, "z", ring)
            at = (my_z - 1 - step + 2 * depth) % depth
            term = lax.dynamic_index_in_dim(up_parts, at, 0, keepdims=False)
            d_up = low(wide(d_up) + wide(term))
        d_output = low(product_rows(attended, grad_flat))
        d_out_parts = jnp.transpose(
            d_output.reshape(depth // 4, 4, out_seg, width), (1, 0, 2, 3)
        )
        grad_query, grad_keyval, first_sums, block_out, input_grad, out_own, d_up, down_x = attend_back(
            depth,
            grad_branch,
            query,
            keyval,
            allow,
            w_output,
            w_query,
            w_keyval,
            own_low,
            grad_middle,
            small_rows,
            block_own,
            back_chooser,
            holder,
            d_out_parts,
            d_up,
            up_parts,
            d_down,
        )
        d_query = low(product_rows(normed_attn, grad_query))
        grad_keyval = grad_keyval.reshape(micro * PACK, 2 * HEAD)
        d_keyval = low(product_rows(normed_attn, grad_keyval))
        own_keyval = lax.dynamic_slice_in_dim(grad_keyval, member * own_count, own_count)

        def colsum(values):
            return jnp.sum(wide(values), axis=0)

        def spread_vec(values, parts, size, full):
            out = jnp.zeros((full,), jnp.float32)
            for index, begin in enumerate(parts):
                out = lax.dynamic_update_slice(
                    out, values[index * size : (index + 1) * size], (begin,)
                )
            return out

        vec_query = spread_vec(colsum(grad_query), [head_base(my_y)], head_cols, width)
        vec_up = spread_vec(
            colsum(grad_hidden),
            [owner(z_at, my_y) * ff_own + my_xc * ff_seg for z_at in range(depth)],
            ff_seg,
            ff,
        )
        vectors = [
            first_sums[0],
            first_sums[1],
            second_sums[0],
            second_sums[1],
            second_sums[2],
            second_sums[3],
            vec_query,
            vec_up,
            colsum(own_keyval[:, HEAD:]),
        ]
        vectors = jnp.concatenate([item.reshape(fsdp_size, -1) for item in vectors], axis=1)
        vectors = jnp.pad(low(vectors), ((0, 0), (0, small_size - small_count)))
        if y_slow:
            d_vec = jnp.transpose(vectors.reshape(2, depth, 16, rows_own), (1, 0, 2, 3))
        else:
            d_vec = vectors.reshape(depth, 2, 16, rows_own)

        if y_slow:
            d_keyval = d_keyval.reshape(2, depth, 4, out_seg, 2 * HEAD)
            d_keyval = lax.dynamic_index_in_dim(d_keyval, my_y, 0, keepdims=False)
        else:
            d_keyval = d_keyval.reshape(depth, 2, 4, out_seg, 2 * HEAD)
            d_keyval = lax.dynamic_index_in_dim(d_keyval, my_y, 1, keepdims=False)
        d_keyval = lax.dynamic_index_in_dim(d_keyval, my_xc, 1, keepdims=False)
        d_keyval = d_keyval.reshape(depth * out_seg, 2 * HEAD)
        up_all, down_all, query_sum, kv_sum, vec_all, out_all = closing(
            depth, d_up, d_down, down_x, rows_by_z(d_query), d_keyval, d_vec, out_own
        )
        up_grad, query_grad, down_grad, output_grad, keyval_grad = widen(
            depth,
            y_slow,
            up_all,
            query_sum,
            down_all.reshape(ff_own, width),
            out_all.reshape(rows_own, width),
            kv_sum.reshape(rows_own, 2 * HEAD),
        )
        vec_own = jnp.sum(wide(vec_all), axis=0).reshape(small_size)
        (
            gain_a_grad,
            shift_a_grad,
            bias_o_grad,
            gain_m_grad,
            shift_m_grad,
            bias_d_grad,
            bias_q_grad,
            bias_u_grad,
            bias_v_grad,
        ) = [vec_own[start : start + size] for start, size in zip(begins, sizes)]

        return (
            block_out,
            input_grad,
            gain_a_grad,
            shift_a_grad,
            query_grad,
            bias_q_grad,
            keyval_grad,
            bias_v_grad,
            output_grad,
            bias_o_grad,
            gain_m_grad,
            shift_m_grad,
            up_grad,
            bias_u_grad,
            down_grad,
            bias_d_grad,
        )

    return shards, depth, owner_axes


def solution(mesh):
    shards, depth, owner_axes = build(mesh)
    sizes = {"z": depth, "y": 2}
    fine = Mesh(
        mesh.devices.reshape(sizes[owner_axes[0]], sizes[owner_axes[1]], 2, 2),
        owner_axes + ("x", "c"),
    )
    rows = P(owner_axes + ("x", "c"), None, None)
    vec = P(owner_axes)
    mat = P(owner_axes, None)
    in_specs = (
        rows, rows, P(), P(),
        vec, vec, mat, vec, mat, vec, mat, vec, vec, vec, mat, vec, mat, vec,
    )
    out_specs = (
        rows, rows,
        vec, vec, mat, vec, mat, vec, mat, vec, vec, vec, mat, vec, mat, vec,
    )
    return jax.shard_map(shards, mesh=fine, in_specs=in_specs, out_specs=out_specs, check_vma=False)
```
